32 devices in a mesh: grp: 2 (over y), row: 16 (over z, x, core), col: 1.
Axes of the slice: x: 2, y: 2, z: 4, core: 2. Of those that a mesh axis runs over, the one named last changes fastest.
Arguments:
- pair_rep: bfloat16 [256, 128, 128], P(('grp', 'row'), 'col'), parts along dimension 0, may hold values from -6 to 6
- pair_mask: int32 [256, 128], P(('grp', 'row'), 'col'), parts along dimension 0, may hold values from 0 to 1, as said below
- cotangent: bfloat16 [256, 128, 128], P(('grp', 'row'), 'col'), parts along dimension 0, may hold values from -6 to 6
- in_gain: float32 [128], replicated, may hold values from 0.25 to 1.75
- in_bias: float32 [128], replicated, may hold values from -3 to 3
- proj_weight: bfloat16 [128, 512], replicated, may hold values from -0.5 to 0.5
- gate_weight: bfloat16 [128, 128], replicated, may hold values from -0.5 to 0.5
- mid_gain: float32 [128], replicated, may hold values from 0.25 to 1.75
- mid_bias: float32 [128], replicated, may hold values from -3 to 3
- out_weight: bfloat16 [128, 128], replicated, may hold values from -0.5 to 0.5
Outputs:
- output: bfloat16 [256, 128, 128], P(('grp', 'row'), 'col'), parts along dimension 0
- grad_pair: bfloat16 [256, 128, 128], P(('grp', 'row'), 'col'), parts along dimension 0
The draws below stay inside these ranges and needn't reach their ends.
There are 2 independent parts, one for each index of `grp`. The reference program is written for one: setup_inputs(seed, part) draws one part's arguments, and reference() takes and returns one part's arrays. A program takes and returns all parts, laid end to end along the dimension named above; an argument that names none is the same for every part. Nothing has to cross between parts.
Inputs may be any that keep to these rules, and one draw needn't show every extreme that they name: pair_mask[i, j] = v[i] v[j] for a residue validity v of 0 and 1: residues from some position on (at least 96 and below 128) are padding with v = 0, and single residues before it may also have v = 0.
All inputs are finite; a program needn't handle non-finite values.
Results may differ from the reference program's by a relative error of at most 0.0074.
Values may be sent and summed in bfloat16 or wider, within the bound.
No kernel may reach another device: no remote copies, remote signals or barrier semaphores. Data moves between devices by JAX's collectives and lax.ppermute only.
A program may use at most 64 MiB of HBM per device.

```python
import jax
import jax.numpy as jnp
from jax import lax

C = 128
H = 128
ROWS = 8
N = 128
N_ROW = 16


def draw_pair_mask(key, part):
    key = jax.random.fold_in(key, 11)
    key = jax.random.fold_in(key, part)
    length_key, missing_key = jax.random.split(key)
    length = jax.random.randint(length_key, (), 3 * N // 4, N, dtype=jnp.int32)
    missing = jax.random.randint(missing_key, (N,), 0, 4, dtype=jnp.int32)
    positions = jnp.arange(N, dtype=jnp.int32)
    valid = jnp.where((positions < length) & (missing != 0), 1, 0).astype(jnp.int32)
    return valid[:, None] * valid[None, :]


def block_levels(stream_key, shape, cuts, smallest, largest):
    level, own = 1.0, jax.random.fold_in(stream_key, 6)
    for position, shards_of in cuts:
        steps = jnp.exp(jax.random.uniform(jax.random.fold_in(own, position), (shards_of,), jnp.float32, smallest / len(cuts), largest / len(cuts)))
        level = level * jnp.repeat(steps, shape[position] // shards_of).reshape([-1 if axis == position else 1 for axis in range(len(shape))])
    return level


def centred(stream_key, extent, width, most, cuts=(), kind=jnp.bfloat16):
    factor_of = block_levels(stream_key, extent, cuts, -0.22, 0.18) if cuts else 1.0
    entries = jax.random.normal(stream_key, extent, jnp.float32) * width * factor_of
    return jnp.minimum(jnp.maximum(entries, -most), most).astype(kind)


def setup_inputs(seed: int = 0, part: int = 0) -> dict:
    streams_of = jax.random.split(jax.random.key(seed), 11)
    own_keys = jax.random.split(jax.random.fold_in(streams_of[10], part), 11)
    return {
        "pair_rep": centred(own_keys[0], (N, N, C), 1.0, 6.0, ((0, 16),)),
        "pair_mask": draw_pair_mask(jax.random.fold_in(jax.random.fold_in(streams_of[10], part), 71), part),
        "cotangent": centred(own_keys[2], (N, N, C), 1.0, 6.0, ((0, 16),)),
        "in_gain": jnp.clip(1.0 + 0.15 * jax.random.normal(streams_of[3], (C,), jnp.float32), 0.25, 1.75),
        "in_bias": centred(streams_of[4], (C,), 0.5, 3.0, (), jnp.float32),
        "proj_weight": centred(streams_of[5], (C, 4 * H), C ** -0.5, 0.5),
        "gate_weight": centred(streams_of[6], (C, C), C ** -0.5, 0.5),
        "mid_gain": jnp.clip(1.0 + 0.15 * jax.random.normal(streams_of[7], (H,), jnp.float32), 0.25, 1.75),
        "mid_bias": centred(streams_of[8], (H,), 0.5, 3.0, (), jnp.float32),
        "out_weight": centred(streams_of[9], (H, C), H ** -0.5, 0.5),
    }


EPSILON = 1e-05

def norm_stats(values, reduce_axis):
    center = values - lax.optimization_barrier(jnp.mean(values, axis=reduce_axis, keepdims=True))
    inverse = lax.rsqrt(lax.optimization_barrier(jnp.mean(center * center, axis=reduce_axis, keepdims=True)) + EPSILON)
    return (center * inverse, inverse)

def norm_back(grad_hat, normed, inverse, reduce_axis):
    first = lax.optimization_barrier(jnp.mean(grad_hat, axis=reduce_axis, keepdims=True))
    second = lax.optimization_barrier(jnp.mean(grad_hat * normed, axis=reduce_axis, keepdims=True))
    return inverse * (grad_hat - first - normed * second)

def rounded(values):
    return lax.optimization_barrier(values.astype(jnp.bfloat16)).astype(jnp.float32)

def reference(pair_rep, pair_mask, cotangent, in_gain, in_bias, proj_weight, gate_weight, mid_gain, mid_bias, out_weight):
    weights_four = proj_weight.astype(jnp.float32).reshape(C, 2, 2, H)
    gate_full = gate_weight.astype(jnp.float32)
    out_full = out_weight.astype(jnp.float32)
    block_ids = jnp.arange(N_ROW, dtype=jnp.int32)

    def input_side(block_index):
        row_start = block_index * ROWS
        pair_rows = lax.dynamic_slice_in_dim(pair_rep, row_start, ROWS, 0).astype(jnp.float32)
        mask_rows = lax.dynamic_slice_in_dim(pair_mask, row_start, ROWS, 0).astype(jnp.float32)
        normed_in, inverse_in = norm_stats(pair_rows, 2)
        scaled_in = rounded(normed_in * in_gain + in_bias)
        gate_pre = jnp.einsum('ijc,csh->shij', scaled_in, weights_four[:, :, 0])
        value_pre = jnp.einsum('ijc,csh->shij', scaled_in, weights_four[:, :, 1])
        gate_sig = jax.nn.sigmoid(jnp.einsum('ijc,cd->ijd', scaled_in, gate_full))
        return (normed_in, inverse_in, gate_pre, value_pre, gate_sig, mask_rows)

    def make_sides(block_index):
        normed_in, inverse_in, gate_pre, value_pre, gate_sig, mask_rows = input_side(block_index)
        return (jax.nn.sigmoid(gate_pre) * value_pre * mask_rows).astype(jnp.bfloat16)
    both_sides = lax.map(make_sides, block_ids)
    both_sides = jnp.transpose(both_sides, (1, 2, 0, 3, 4)).reshape(2, H, N, N)

    def contract(operands):
        left_side, right_side = operands
        product = jnp.dot(left_side.astype(jnp.float32), right_side.astype(jnp.float32).T, preferred_element_type=jnp.float32)
        return product.astype(jnp.bfloat16)
    mixed_pair = lax.map(contract, (both_sides[0], both_sides[1]))

    def middle(block_index):
        row_start = block_index * ROWS
        normed_in, inverse_in, gate_pre, value_pre, gate_sig, mask_rows = input_side(block_index)
        mixed_rows = lax.dynamic_slice_in_dim(mixed_pair, row_start, ROWS, 1).astype(jnp.float32)
        normed_mid, inverse_mid = norm_stats(mixed_rows, 0)
        scaled_mid = rounded(normed_mid * mid_gain[:, None, None] + mid_bias[:, None, None])
        update = jnp.einsum('hij,hc->ijc', scaled_mid, out_full)
        output_rows = (gate_sig * update).astype(jnp.bfloat16)
        grad_out = lax.dynamic_slice_in_dim(cotangent, row_start, ROWS, 0).astype(jnp.float32)
        grad_update = rounded(grad_out * gate_sig)
        grad_gate = (grad_out * update * gate_sig * (1.0 - gate_sig)).astype(jnp.bfloat16)
        grad_scaled = jnp.einsum('ijc,hc->hij', grad_update, out_full)
        grad_mixed = norm_back(grad_scaled * mid_gain[:, None, None], normed_mid, inverse_mid, 0).astype(jnp.bfloat16)
        return (output_rows, grad_mixed, grad_gate)
    output_blocks, grad_mixed, grad_gate = lax.map(middle, block_ids)
    output = output_blocks.reshape(N, N, C)
    grad_mixed = jnp.transpose(grad_mixed, (1, 0, 2, 3)).reshape(H, N, N)
    grad_gate = grad_gate.reshape(N, N, C)

    def grad_contract(operands):
        grad_rows, left_side, right_side = operands
        grad_rows = grad_rows.astype(jnp.float32)
        grad_left = jnp.dot(grad_rows, right_side.astype(jnp.float32), preferred_element_type=jnp.float32)
        grad_right = jnp.dot(grad_rows.T, left_side.astype(jnp.float32), preferred_element_type=jnp.float32)
        return jnp.stack([grad_left, grad_right]).astype(jnp.bfloat16)
    grad_sides = lax.map(grad_contract, (grad_mixed, both_sides[0], both_sides[1]))

    def input_grad(block_index):
        row_start = block_index * ROWS
        normed_in, inverse_in, gate_pre, value_pre, gate_sig, mask_rows = input_side(block_index)
        side_rows = lax.dynamic_slice_in_dim(grad_sides, row_start, ROWS, 2).astype(jnp.float32)
        side_rows = jnp.swapaxes(side_rows, 0, 1) * mask_rows
        sigmoid_gate = jax.nn.sigmoid(gate_pre)
        grad_value = rounded(side_rows * sigmoid_gate)
        grad_gate_pre = rounded(side_rows * value_pre * sigmoid_gate * (1.0 - sigmoid_gate))
        gate_rows = lax.dynamic_slice_in_dim(grad_gate, row_start, ROWS, 0).astype(jnp.float32)
        grad_scaled = jnp.einsum('shij,csh->ijc', grad_gate_pre, weights_four[:, :, 0])
        grad_scaled = grad_scaled + jnp.einsum('shij,csh->ijc', grad_value, weights_four[:, :, 1])
        grad_scaled = grad_scaled + jnp.einsum('ijd,cd->ijc', gate_rows, gate_full)
        return norm_back(grad_scaled * in_gain, normed_in, inverse_in, 2).astype(jnp.bfloat16)
    grad_pair = lax.map(input_grad, block_ids).reshape(N, N, C)
    return (output, grad_pair)
```

```python
import jax
import jax.numpy as jnp
from jax import lax
from jax.sharding import PartitionSpec as P

EPSILON = 1e-05
CORE, CHIP_X, Z_LOW, Z_HIGH = 1, 2, 4, 8
LEFT_OFFSETS = (0, CHIP_X, Z_LOW, Z_LOW | CHIP_X)
RIGHT_OFFSETS = (0, CORE, Z_HIGH, Z_HIGH | CORE)


def norm_stats(values, reduce_axis):
    center = values - jnp.mean(values, axis=reduce_axis, keepdims=True)
    inverse = lax.rsqrt(jnp.mean(center * center, axis=reduce_axis, keepdims=True) + EPSILON)
    return (center * inverse, inverse)


def norm_back(grad_hat, normed, inverse, reduce_axis):
    first = jnp.mean(grad_hat, axis=reduce_axis, keepdims=True)
    second = jnp.mean(grad_hat * normed, axis=reduce_axis, keepdims=True)
    return inverse * (grad_hat - first - normed * second)


def forward_products(left_chan, right_chan):
    return jnp.einsum("hik,hjk->hij", left_chan, right_chan, preferred_element_type=jnp.float32)


def backward_products(grad_full, left_chan, right_chan):
    grad_left = jnp.einsum(
        "hij,hjk->hik", grad_full, right_chan, preferred_element_type=jnp.float32
    )
    grad_right = jnp.einsum(
        "hij,hik->hjk", grad_full, left_chan, preferred_element_type=jnp.float32
    )
    return jnp.stack([grad_left, grad_right]).astype(jnp.bfloat16)


def swap(values, offset):
    return lax.ppermute(values, "row", [(s, s ^ offset) for s in range(16)])


def reduce_pair(parts, far, near):
    to_far = swap(parts[3], near).astype(jnp.float32) + parts[2].astype(jnp.float32)
    from_far = swap(to_far.astype(jnp.bfloat16), far).astype(jnp.float32)
    from_near = swap(parts[1], near).astype(jnp.float32)
    return parts[0].astype(jnp.float32) + from_near + from_far


def blocks_device(
    pair_rep,
    pair_mask,
    cotangent,
    in_gain,
    in_bias,
    proj_weight,
    gate_weight,
    mid_gain,
    mid_bias,
    out_weight,
):
    rows, cols, width = pair_rep.shape
    hidden = out_weight.shape[0]
    me = lax.axis_index("row")
    weights_four = proj_weight.reshape(width, 2, 2, hidden)
    mask_float = pair_mask.astype(jnp.float32)
    normed_in, inverse_in = norm_stats(pair_rep.astype(jnp.float32), 2)
    scaled_in = (normed_in * in_gain + in_bias).astype(jnp.bfloat16)
    gate_pre = jnp.einsum(
        "ijc,csh->shij", scaled_in, weights_four[:, :, 0], preferred_element_type=jnp.float32
    )
    value_pre = jnp.einsum(
        "ijc,csh->shij", scaled_in, weights_four[:, :, 1], preferred_element_type=jnp.float32
    )
    sigmoid_gate = jax.nn.sigmoid(gate_pre)
    both_sides = (sigmoid_gate * value_pre * mask_float).astype(jnp.bfloat16)
    left, right = both_sides[0], both_sides[1]
    left_far = swap(left, Z_LOW)
    right_far = swap(right, Z_HIGH)
    left_near = swap(left, CHIP_X)
    right_near = swap(right, CORE)
    left_both = swap(left_far, CHIP_X)
    right_both = swap(right_far, CORE)

    gate_sig = jax.nn.sigmoid(
        jnp.einsum("ijc,cd->ijd", scaled_in, gate_weight, preferred_element_type=jnp.float32)
    )
    grad_out = cotangent.astype(jnp.float32)
    grad_update = (grad_out * gate_sig).astype(jnp.bfloat16)

    def columns_for(offset):
        starts = [((me ^ offset) ^ other) * rows for other in RIGHT_OFFSETS]
        pieces = [lax.dynamic_slice_in_dim(grad_update, s, rows, 1) for s in starts]
        return jnp.concatenate(pieces, axis=1)

    grad_block = jnp.concatenate(
        [columns_for(0)] + [swap(columns_for(o), o) for o in LEFT_OFFSETS[1:]], axis=0
    )

    left_block = jnp.concatenate([left, left_near, left_far, left_both], axis=1)
    right_block = jnp.concatenate([right, right_near, right_far, right_both], axis=1)
    mixed = forward_products(left_block, right_block).astype(jnp.bfloat16)
    normed_mid, inverse_mid = norm_stats(mixed.astype(jnp.float32), 0)
    scaled_mid = (normed_mid * mid_gain[:, None, None] + mid_bias[:, None, None]).astype(
        jnp.bfloat16
    )
    update_block = jnp.einsum(
        "hij,hc->ijc", scaled_mid, out_weight, preferred_element_type=jnp.float32
    ).astype(jnp.bfloat16)
    grad_scaled_mid = jnp.einsum(
        "ijc,hc->hij", grad_block, out_weight, preferred_element_type=jnp.float32
    )
    grad_mixed = norm_back(
        grad_scaled_mid * mid_gain[:, None, None], normed_mid, inverse_mid, 0
    ).astype(jnp.bfloat16)
    grad_left, grad_right = backward_products(grad_mixed, left_block, right_block)
    left_parts = jnp.split(grad_left, 4, axis=1)
    right_parts = jnp.split(grad_right, 4, axis=1)
    grad_left = reduce_pair(left_parts, Z_LOW, CHIP_X)
    grad_right = reduce_pair(right_parts, Z_HIGH, CORE)

    update_parts = jnp.split(update_block, 4, axis=0)
    update_parts = [update_parts[0]] + [
        swap(p, o) for p, o in zip(update_parts[1:], LEFT_OFFSETS[1:])
    ]
    update = jnp.zeros((rows, cols, width), jnp.bfloat16)
    for part, offset in zip(update_parts, LEFT_OFFSETS):
        for place, other in enumerate(RIGHT_OFFSETS):
            piece = part[:, place * rows : (place + 1) * rows]
            update = lax.dynamic_update_slice_in_dim(
                update, piece, ((me ^ offset) ^ other) * rows, 1
            )
    update = update.astype(jnp.float32)
    output = (gate_sig * update).astype(jnp.bfloat16)
    grad_gate = (grad_out * update * gate_sig * (1.0 - gate_sig)).astype(jnp.bfloat16)

    side_float = jnp.stack([grad_left, grad_right]) * mask_float
    grad_value = (side_float * sigmoid_gate).astype(jnp.bfloat16)
    grad_gate_pre = (side_float * value_pre * sigmoid_gate * (1.0 - sigmoid_gate)).astype(
        jnp.bfloat16
    )
    grad_scaled = jnp.einsum(
        "shij,csh->ijc", grad_gate_pre, weights_four[:, :, 0], preferred_element_type=jnp.float32
    )
    grad_scaled = grad_scaled + jnp.einsum(
        "shij,csh->ijc", grad_value, weights_four[:, :, 1], preferred_element_type=jnp.float32
    )
    grad_scaled = grad_scaled + jnp.einsum(
        "ijd,cd->ijc", grad_gate, gate_weight, preferred_element_type=jnp.float32
    )
    grad_pair = norm_back(grad_scaled * in_gain, normed_in, inverse_in, 2).astype(jnp.bfloat16)
    return (output, grad_pair)


def channels_device(
    pair_rep,
    pair_mask,
    cotangent,
    in_gain,
    in_bias,
    proj_weight,
    gate_weight,
    mid_gain,
    mid_bias,
    out_weight,
):
    width = pair_rep.shape[2]
    hidden = out_weight.shape[0]
    weights_four = proj_weight.reshape(width, 2, 2, hidden)
    mask_float = pair_mask.astype(jnp.float32)
    normed_in, inverse_in = norm_stats(pair_rep.astype(jnp.float32), 2)
    scaled_in = (normed_in * in_gain + in_bias).astype(jnp.bfloat16)
    gate_pre = jnp.einsum(
        "ijc,csh->shij", scaled_in, weights_four[:, :, 0], preferred_element_type=jnp.float32
    )
    value_pre = jnp.einsum(
        "ijc,csh->shij", scaled_in, weights_four[:, :, 1], preferred_element_type=jnp.float32
    )
    sigmoid_gate = jax.nn.sigmoid(gate_pre)
    both_sides = (sigmoid_gate * value_pre * mask_float).astype(jnp.bfloat16)
    gate_sig = jax.nn.sigmoid(
        jnp.einsum("ijc,cd->ijd", scaled_in, gate_weight, preferred_element_type=jnp.float32)
    )
    sides_chan = lax.all_to_all(both_sides, "row", split_axis=1, concat_axis=2, tiled=True)
    partial_sum = forward_products(sides_chan[0], sides_chan[1])
    product = lax.psum_scatter(partial_sum, "col", scatter_dimension=2, tiled=True).astype(
        jnp.bfloat16
    )
    mixed_pair = lax.all_to_all(product, "row", split_axis=1, concat_axis=0, tiled=True)
    normed_mid, inverse_mid = norm_stats(mixed_pair.astype(jnp.float32), 0)
    scaled_mid = (normed_mid * mid_gain[:, None, None] + mid_bias[:, None, None]).astype(
        jnp.bfloat16
    )
    update = jnp.einsum("hij,hc->ijc", scaled_mid, out_weight, preferred_element_type=jnp.float32)
    output = (gate_sig * update).astype(jnp.bfloat16)
    grad_out = cotangent.astype(jnp.float32)
    grad_update = (grad_out * gate_sig).astype(jnp.bfloat16)
    grad_gate = (grad_out * update * gate_sig * (1.0 - gate_sig)).astype(jnp.bfloat16)
    grad_scaled_mid = jnp.einsum(
        "ijc,hc->hij", grad_update, out_weight, preferred_element_type=jnp.float32
    )
    grad_mixed = norm_back(
        grad_scaled_mid * mid_gain[:, None, None], normed_mid, inverse_mid, 0
    ).astype(jnp.bfloat16)
    grad_chan = lax.all_to_all(grad_mixed, "row", split_axis=0, concat_axis=1, tiled=True)
    grad_full = lax.all_gather(grad_chan, "col", axis=2, tiled=True)
    grad_local = backward_products(grad_full, sides_chan[0], sides_chan[1])
    grad_sides = lax.all_to_all(grad_local, "row", split_axis=2, concat_axis=1, tiled=True)
    side_float = grad_sides.astype(jnp.float32) * mask_float
    grad_value = (side_float * sigmoid_gate).astype(jnp.bfloat16)
    grad_gate_pre = (side_float * value_pre * sigmoid_gate * (1.0 - sigmoid_gate)).astype(
        jnp.bfloat16
    )
    grad_scaled = jnp.einsum(
        "shij,csh->ijc", grad_gate_pre, weights_four[:, :, 0], preferred_element_type=jnp.float32
    )
    grad_scaled = grad_scaled + jnp.einsum(
        "shij,csh->ijc", grad_value, weights_four[:, :, 1], preferred_element_type=jnp.float32
    )
    grad_scaled = grad_scaled + jnp.einsum(
        "ijd,cd->ijc", grad_gate, gate_weight, preferred_element_type=jnp.float32
    )
    grad_pair = norm_back(grad_scaled * in_gain, normed_in, inverse_in, 2).astype(jnp.bfloat16)
    return (output, grad_pair)


def solution(mesh):
    blocks = mesh.shape["row"] == 16 and mesh.shape["col"] == 1
    placed = (
        P(("grp", "row"), "col", None),
        P(("grp", "row"), "col"),
        P(("grp", "row"), "col", None),
        P(),
        P(),
        P(),
        P(),
        P(),
        P(),
        P(),
    )
    return jax.shard_map(
        blocks_device if blocks else channels_device,
        mesh=mesh,
        in_specs=placed,
        out_specs=(P(("grp", "row"), "col", None), P(("grp", "row"), "col", None)),
        check_vma=False,
    )
```

```python
import jax
import jax.numpy as jnp
from jax import lax
from jax.experimental import pallas as pl
from jax.experimental.pallas import tpu as pltpu
from jax.sharding import PartitionSpec as P

EPSILON = 1e-05
CORE, CHIP_X, Z_LOW, Z_HIGH = 1, 2, 4, 8
LEFT_OFFSETS = (0, CHIP_X, Z_LOW, Z_LOW | CHIP_X)
RIGHT_OFFSETS = (0, CORE, Z_HIGH, Z_HIGH | CORE)
ROWS = 8
PEERS = 4
VMEM_BYTES = 48 * 2**20

NT = (((1,), (1,)), ((), ()))
NN = (((1,), (0,)), ((), ()))
TN = (((0,), (0,)), ((), ()))


def dot(a, b, dims):
    return lax.dot_general(a, b, dims, preferred_element_type=jnp.float32)


def lane_norm(values):
    center = values - jnp.mean(values, axis=1, keepdims=True)
    inverse = lax.rsqrt(jnp.mean(center * center, axis=1, keepdims=True) + EPSILON)
    return center * inverse, inverse


def sigmoid(x):
    return 1.0 / (1.0 + jnp.exp(-x))


def call(kernel, out_shape, *args, scratch=(), flops=0, nbytes=2**20, exps=0, smem=0):
    specs = [pl.BlockSpec(memory_space=pltpu.SMEM)] * smem
    specs += [pl.BlockSpec(memory_space=pltpu.VMEM)] * (len(args) - smem)
    return pl.pallas_call(
        kernel,
        out_shape=out_shape,
        in_specs=specs,
        out_specs=jax.tree.map(lambda _: pl.BlockSpec(memory_space=pltpu.VMEM), out_shape),
        scratch_shapes=list(scratch),
        compiler_params=pltpu.CompilerParams(vmem_limit_bytes=VMEM_BYTES),
        cost_estimate=pl.CostEstimate(flops=flops, bytes_accessed=nbytes, transcendentals=exps),
    )(*args)


def side_rows(quarter, row, quarters):
    return pl.ds(quarter * ROWS + row, 32, stride=quarters * ROWS)


def sides_kernel(x_ref, mask_ref, gain_ref, bias_ref, weight_ref, left_ref, right_ref, rows_ref):
    hidden = weight_ref.shape[0] // 4
    for row in range(ROWS):
        normed, _ = lane_norm(x_ref[row].astype(jnp.float32))
        scaled = (normed * gain_ref[...] + bias_ref[...]).astype(jnp.bfloat16)
        projected = dot(weight_ref[...], scaled, NT)
        keep = mask_ref[row : row + 1].astype(jnp.float32)
        for side in range(2):
            base = 2 * side * hidden
            gate = projected[base : base + hidden]
            value = projected[base + hidden : base + 2 * hidden]
            result = sigmoid(gate) * value * keep
            for quarter in range(4):
                rows_ref[side, side_rows(quarter, row, 4), :] = result[
                    quarter * 32 : (quarter + 1) * 32
                ]
    left_ref[...] = rows_ref[0].astype(jnp.bfloat16)
    right_ref[...] = rows_ref[1].astype(jnp.bfloat16)


def gate_kernel(me_ref, x_ref, cot_ref, gain_ref, bias_ref, weight_ref, sig_ref, *rest):
    piece_refs, full_ref = rest[:PEERS], rest[PEERS]
    me = me_ref[0]
    for row in range(ROWS):
        normed, _ = lane_norm(x_ref[row].astype(jnp.float32))
        scaled = (normed * gain_ref[...] + bias_ref[...]).astype(jnp.bfloat16)
        gate_sig = sigmoid(dot(scaled, weight_ref[...], NN))
        sig_ref[row] = gate_sig
        full_ref[row] = cot_ref[row].astype(jnp.float32) * gate_sig
    for piece_ref, offset in zip(piece_refs, LEFT_OFFSETS):
        columns = []
        for other in RIGHT_OFFSETS:
            start = pl.multiple_of(((me ^ offset) ^ other) * ROWS, ROWS)
            columns.append(full_ref[:, pl.ds(start, ROWS), :])
        piece = jnp.concatenate(columns, axis=1)
        piece_ref[...] = piece.reshape(piece_ref.shape).astype(jnp.bfloat16)


def split_sum(values, ones):
    high = values.astype(jnp.bfloat16)
    low = (values - high.astype(jnp.float32)).astype(jnp.bfloat16)
    return dot(high, ones, NN) + dot(low, ones, NN)


def block_kernel(*refs):
    left_refs, right_refs, grad_refs = refs[0:4], refs[4:8], refs[8:12]
    weight_ref, gain_ref, bias_ref = refs[12:15]
    update_refs, grad_left_refs, grad_right_refs = refs[15:19], refs[19:23], refs[23:27]
    pairs_ref, = refs[27:]
    groups = pairs_ref.shape[0] // 32
    lane = lax.broadcasted_iota(jnp.int32, (ROWS, 128), 1)
    of_quarter = [((lane >> 3) & 3) == q for q in range(4)]

    def slab(side_refs, g):
        return jnp.concatenate([r[g * 32 : (g + 1) * 32, :] for r in side_refs], axis=0)

    for g in range(groups):
        full = dot(slab(left_refs, g), slab(right_refs, g), NT).reshape(4, 4, ROWS, 128)
        for m in range(4):
            kept = full[m, 3]
            for q in range(3):
                kept = jnp.where(of_quarter[q], full[m, q], kept)
            pairs_ref[g * 32 + m * ROWS : g * 32 + (m + 1) * ROWS, :] = kept

    turned = []
    for row in range(ROWS):
        turn = pairs_ref[pl.ds(row, 128, stride=ROWS), :].T.reshape(4, 4, ROWS, 128)
        turned.append(jnp.concatenate([turn[:, q].reshape(32, 128) for q in range(4)], axis=1))
    mixed = jnp.concatenate(turned, axis=0).astype(jnp.bfloat16).astype(jnp.float32)

    src = lax.broadcasted_iota(jnp.int32, (128, 128), 0)
    dst = lax.broadcasted_iota(jnp.int32, (128, 128), 1)
    ones = jnp.where((src & 3) == (dst & 3), 1.0, 0.0).astype(jnp.bfloat16)

    def channel_mean(values):
        total = values[:, :128] + values[:, 128:256] + values[:, 256:384] + values[:, 384:]
        mean = split_sum(total, ones) * (1.0 / 128.0)
        return jnp.concatenate([mean] * 4, axis=1)

    center = mixed - channel_mean(mixed)
    inverse = lax.rsqrt(channel_mean(center * center) + EPSILON)
    normed = center * inverse
    scaled = (normed * gain_ref[...] + bias_ref[...]).astype(jnp.bfloat16)
    update = dot(scaled, weight_ref[...], NN)
    for m in range(4):
        update_refs[m][...] = update[:, m * 128 : (m + 1) * 128].astype(jnp.bfloat16)
    grad_update = jnp.concatenate([r[...] for r in grad_refs], axis=1)
    grad_hat = dot(grad_update, weight_ref[...], NT) * gain_ref[...]
    first = channel_mean(grad_hat)
    second = channel_mean(grad_hat * normed)
    grad_mixed = inverse * (grad_hat - first - normed * second)

    for row in range(ROWS):
        part = grad_mixed[row * 32 : (row + 1) * 32]
        parts = [part[:, q * 128 : (q + 1) * 128].reshape(4, 1, ROWS, 128) for q in range(4)]
        turn = jnp.concatenate(parts, axis=1).reshape(128, 128)
        pairs_ref[pl.ds(row, 128, stride=ROWS), :] = turn.T

    for g in range(groups):
        rows = []
        for m in range(4):
            part = pairs_ref[g * 32 + m * ROWS : g * 32 + (m + 1) * ROWS, :]
            rows += [jnp.where(of_quarter[q], part, 0.0) for q in range(4)]
        spread = jnp.concatenate(rows, axis=0).astype(jnp.bfloat16)
        grad_right = dot(spread, slab(left_refs, g), TN).astype(jnp.bfloat16)
        grad_left = dot(spread, slab(right_refs, g), NN).astype(jnp.bfloat16)
        for m in range(4):
            grad_right_refs[m][g * 32 : (g + 1) * 32, :] = grad_right[m * 32 : (m + 1) * 32]
            grad_left_refs[m][g * 32 : (g + 1) * 32, :] = grad_left[m * 32 : (m + 1) * 32]


def out_kernel(me_ref, *refs):
    piece_refs = refs[:PEERS]
    sig_ref, cot_ref, weight_ref, out_ref, grad_ref, full_ref = refs[PEERS:]
    me = me_ref[0]
    for piece_ref, offset in zip(piece_refs, LEFT_OFFSETS):
        piece = piece_ref[...].astype(jnp.float32).reshape(ROWS, PEERS, ROWS, 128)
        for place, other in enumerate(RIGHT_OFFSETS):
            start = pl.multiple_of(((me ^ offset) ^ other) * ROWS, ROWS)
            full_ref[:, pl.ds(start, ROWS), :] = piece[:, place]
    for row in range(ROWS):
        update, gate_sig = full_ref[row], sig_ref[row]
        out = gate_sig * update
        out_ref[row] = out.astype(jnp.bfloat16)
        grad_gate = cot_ref[row].astype(jnp.float32) * out * (1.0 - gate_sig)
        grad_ref[row] = dot(grad_gate.astype(jnp.bfloat16), weight_ref[...], NT)


def add_kernel(mine_ref, got_ref, sum_ref):
    total = mine_ref[...].astype(jnp.float32) + got_ref[...].astype(jnp.float32)
    sum_ref[...] = total.astype(jnp.bfloat16)


def factor_kernel(x_ref, mask_ref, gain_ref, bias_ref, weight_ref, factor_ref):
    hidden = weight_ref.shape[0] // 4
    for row in range(ROWS):
        normed, _ = lane_norm(x_ref[row].astype(jnp.float32))
        scaled = (normed * gain_ref[...] + bias_ref[...]).astype(jnp.bfloat16)
        projected = dot(weight_ref[...], scaled, NT)
        keep = mask_ref[row : row + 1].astype(jnp.float32)
        for side in range(2):
            base = 2 * side * hidden
            gate = sigmoid(projected[base : base + hidden])
            value = projected[base + hidden : base + 2 * hidden]
            factor_ref[row, base : base + hidden, :] = keep * value * gate * (1.0 - gate)
            factor_ref[row, base + hidden : base + 2 * hidden, :] = keep * gate


def pair_kernel(*refs):
    left_refs, right_refs = refs[0:3], refs[3:6]
    factor_ref, x_ref, gate_ref, gain_ref, weight_ref, out_ref, rows_ref = refs[6:]
    hidden = weight_ref.shape[1] // 4
    for side, side_refs in enumerate((left_refs, right_refs)):
        total = side_refs[0][...].astype(jnp.float32)
        for r in side_refs[1:]:
            total = total + r[...].astype(jnp.float32)
        rows_ref[side] = total
    for row in range(ROWS):
        parts = []
        for side in range(2):
            grad = jnp.concatenate(
                [rows_ref[side, side_rows(q, row, 4), :] for q in range(4)], axis=0
            )
            base = 2 * side * hidden
            for place in (base, base + hidden):
                factor = factor_ref[row, place : place + hidden, :]
                parts.append((grad * factor).astype(jnp.bfloat16))
        grad_projected = jnp.concatenate(parts, axis=0)
        grad_scaled = dot(weight_ref[...], grad_projected, NN).T + gate_ref[row]
        normed, inverse = lane_norm(x_ref[row].astype(jnp.float32))
        grad_hat = grad_scaled * gain_ref[...]
        first = jnp.mean(grad_hat, axis=1, keepdims=True)
        second = jnp.mean(grad_hat * normed, axis=1, keepdims=True)
        out_ref[row] = (inverse * (grad_hat - first - normed * second)).astype(jnp.bfloat16)


def swap(values, offset):
    return lax.ppermute(values, "row", [(s, s ^ offset) for s in range(16)])


def blocks_device(
    pair_rep,
    pair_mask,
    cotangent,
    in_gain,
    in_bias,
    proj_weight,
    gate_weight,
    mid_gain,
    mid_bias,
    out_weight,
):
    rows, cols, width = pair_rep.shape
    hidden = out_weight.shape[0]
    f32, bf16 = jnp.float32, jnp.bfloat16
    shape = jax.ShapeDtypeStruct
    me = lax.axis_index("row").astype(jnp.int32).reshape(1)
    gain, bias = in_gain.reshape(1, width), in_bias.reshape(1, width)
    weight_t = proj_weight.T
    side = shape((hidden * rows, cols), bf16)
    piece = shape((rows * PEERS * rows, width), bf16)

    left, right = call(
        sides_kernel,
        (side, side),
        pair_rep,
        pair_mask,
        gain,
        bias,
        weight_t,
        scratch=[pltpu.VMEM((2, hidden * rows, cols), f32)],
        flops=2 * rows * cols * width * 4 * hidden,
    )
    left_far = swap(left, Z_LOW)
    right_far = swap(right, Z_HIGH)
    left_near = swap(left, CHIP_X)
    right_near = swap(right, CORE)

    gate_sig, *grad_pieces = call(
        gate_kernel,
        (shape(pair_rep.shape, f32),) + (piece,) * PEERS,
        me,
        pair_rep,
        cotangent,
        gain,
        bias,
        gate_weight,
        smem=1,
        scratch=[pltpu.VMEM(pair_rep.shape, f32)],
        flops=2 * rows * cols * width * width,
    )
    grads = [grad_pieces[0]] + [swap(p, o) for p, o in zip(grad_pieces[1:], LEFT_OFFSETS[1:])]
    left_both = swap(left_far, CHIP_X)
    right_both = swap(right_far, CORE)

    eye = jnp.eye(PEERS, dtype=out_weight.dtype)
    weight_block = (out_weight[:, None, None, :] * eye[None, :, :, None]).reshape(
        hidden * PEERS, PEERS * width
    )
    mid_gain_row = jnp.repeat(mid_gain, PEERS).reshape(1, -1)
    mid_bias_row = jnp.repeat(mid_bias, PEERS).reshape(1, -1)
    results = call(
        block_kernel,
        (piece,) * 4 + (side,) * 8,
        left,
        left_near,
        left_far,
        left_both,
        right,
        right_near,
        right_far,
        right_both,
        *grads,
        weight_block,
        mid_gain_row,
        mid_bias_row,
        scratch=[pltpu.VMEM((hidden * rows, 128), f32)],
        flops=2 * 3 * 32 * 128**3,
    )
    updates, left_parts, right_parts = results[0:4], results[4:8], results[8:12]

    def add(mine, got):
        return call(add_kernel, side, mine, got)

    right_sum = add(right_parts[2], swap(right_parts[3], CORE))
    left_sum = add(left_parts[2], swap(left_parts[3], CHIP_X))
    right_got = [right_parts[0], swap(right_parts[1], CORE), swap(right_sum, Z_HIGH)]
    left_got = [left_parts[0], swap(left_parts[1], CHIP_X), swap(left_sum, Z_LOW)]

    updates = [updates[0]] + [swap(p, o) for p, o in zip(updates[1:], LEFT_OFFSETS[1:])]
    factors = call(
        factor_kernel,
        shape((rows, 4 * hidden, cols), f32),
        pair_rep,
        pair_mask,
        gain,
        bias,
        weight_t,
        flops=2 * rows * cols * width * 4 * hidden,
    )
    output, gate_part = call(
        out_kernel,
        (shape(pair_rep.shape, bf16), shape(pair_rep.shape, f32)),
        me,
        *updates,
        gate_sig,
        cotangent,
        gate_weight,
        smem=1,
        scratch=[pltpu.VMEM(pair_rep.shape, f32)],
        flops=2 * rows * cols * width * width,
    )
    grad_pair = call(
        pair_kernel,
        shape(pair_rep.shape, bf16),
        *left_got,
        *right_got,
        factors,
        pair_rep,
        gate_part,
        gain,
        proj_weight,
        scratch=[pltpu.VMEM((2, hidden * rows, cols), f32)],
        flops=2 * rows * cols * width * 4 * hidden,
    )
    return (output, grad_pair)


def norm_stats(values, reduce_axis):
    center = values - jnp.mean(values, axis=reduce_axis, keepdims=True)
    inverse = lax.rsqrt(jnp.mean(center * center, axis=reduce_axis, keepdims=True) + EPSILON)
    return (center * inverse, inverse)


def norm_back(grad_hat, normed, inverse, reduce_axis):
    first = jnp.mean(grad_hat, axis=reduce_axis, keepdims=True)
    second = jnp.mean(grad_hat * normed, axis=reduce_axis, keepdims=True)
    return inverse * (grad_hat - first - normed * second)


def forward_products(left_chan, right_chan):
    return jnp.einsum("hik,hjk->hij", left_chan, right_chan, preferred_element_type=jnp.float32)


def backward_products(grad_full, left_chan, right_chan):
    grad_left = jnp.einsum(
        "hij,hjk->hik", grad_full, right_chan, preferred_element_type=jnp.float32
    )
    grad_right = jnp.einsum(
        "hij,hik->hjk", grad_full, left_chan, preferred_element_type=jnp.float32
    )
    return jnp.stack([grad_left, grad_right]).astype(jnp.bfloat16)


def channels_device(
    pair_rep,
    pair_mask,
    cotangent,
    in_gain,
    in_bias,
    proj_weight,
    gate_weight,
    mid_gain,
    mid_bias,
    out_weight,
):
    width = pair_rep.shape[2]
    hidden = out_weight.shape[0]
    weights_four = proj_weight.reshape(width, 2, 2, hidden)
    mask_float = pair_mask.astype(jnp.float32)
    normed_in, inverse_in = norm_stats(pair_rep.astype(jnp.float32), 2)
    scaled_in = (normed_in * in_gain + in_bias).astype(jnp.bfloat16)
    gate_pre = jnp.einsum(
        "ijc,csh->shij", scaled_in, weights_four[:, :, 0], preferred_element_type=jnp.float32
    )
    value_pre = jnp.einsum(
        "ijc,csh->shij", scaled_in, weights_four[:, :, 1], preferred_element_type=jnp.float32
    )
    sigmoid_gate = jax.nn.sigmoid(gate_pre)
    both_sides = (sigmoid_gate * value_pre * mask_float).astype(jnp.bfloat16)
    gate_sig = jax.nn.sigmoid(
        jnp.einsum("ijc,cd->ijd", scaled_in, gate_weight, preferred_element_type=jnp.float32)
    )
    sides_chan = lax.all_to_all(both_sides, "row", split_axis=1, concat_axis=2, tiled=True)
    partial_sum = forward_products(sides_chan[0], sides_chan[1])
    product = lax.psum_scatter(partial_sum, "col", scatter_dimension=2, tiled=True).astype(
        jnp.bfloat16
    )
    mixed_pair = lax.all_to_all(product, "row", split_axis=1, concat_axis=0, tiled=True)
    normed_mid, inverse_mid = norm_stats(mixed_pair.astype(jnp.float32), 0)
    scaled_mid = (normed_mid * mid_gain[:, None, None] + mid_bias[:, None, None]).astype(
        jnp.bfloat16
    )
    update = jnp.einsum("hij,hc->ijc", scaled_mid, out_weight, preferred_element_type=jnp.float32)
    output = (gate_sig * update).astype(jnp.bfloat16)
    grad_out = cotangent.astype(jnp.float32)
    grad_update = (grad_out * gate_sig).astype(jnp.bfloat16)
    grad_gate = (grad_out * update * gate_sig * (1.0 - gate_sig)).astype(jnp.bfloat16)
    grad_scaled_mid = jnp.einsum(
        "ijc,hc->hij", grad_update, out_weight, preferred_element_type=jnp.float32
    )
    grad_mixed = norm_back(
        grad_scaled_mid * mid_gain[:, None, None], normed_mid, inverse_mid, 0
    ).astype(jnp.bfloat16)
    grad_chan = lax.all_to_all(grad_mixed, "row", split_axis=0, concat_axis=1, tiled=True)
    grad_full = lax.all_gather(grad_chan, "col", axis=2, tiled=True)
    grad_local = backward_products(grad_full, sides_chan[0], sides_chan[1])
    grad_sides = lax.all_to_all(grad_local, "row", split_axis=2, concat_axis=1, tiled=True)
    side_float = grad_sides.astype(jnp.float32) * mask_float
    grad_value = (side_float * sigmoid_gate).astype(jnp.bfloat16)
    grad_gate_pre = (side_float * value_pre * sigmoid_gate * (1.0 - sigmoid_gate)).astype(
        jnp.bfloat16
    )
    grad_scaled = jnp.einsum(
        "shij,csh->ijc", grad_gate_pre, weights_four[:, :, 0], preferred_element_type=jnp.float32
    )
    grad_scaled = grad_scaled + jnp.einsum(
        "shij,csh->ijc", grad_value, weights_four[:, :, 1], preferred_element_type=jnp.float32
    )
    grad_scaled = grad_scaled + jnp.einsum(
        "ijd,cd->ijc", grad_gate, gate_weight, preferred_element_type=jnp.float32
    )
    grad_pair = norm_back(grad_scaled * in_gain, normed_in, inverse_in, 2).astype(jnp.bfloat16)
    return (output, grad_pair)


def solution(mesh):
    blocks = mesh.shape["row"] == 16 and mesh.shape["col"] == 1
    placed = (
        P(("grp", "row"), "col", None),
        P(("grp", "row"), "col"),
        P(("grp", "row"), "col", None),
        P(),
        P(),
        P(),
        P(),
        P(),
        P(),
        P(),
    )
    return jax.shard_map(
        blocks_device if blocks else channels_device,
        mesh=mesh,
        in_specs=placed,
        out_specs=(P(("grp", "row"), "col", None), P(("grp", "row"), "col", None)),
        check_vma=False,
    )
```

```python
import jax
import jax.numpy as jnp
from jax import lax
from jax.experimental import pallas as pl
from jax.experimental.pallas import tpu as pltpu
from jax.sharding import PartitionSpec as P

EPSILON = 1e-05
CORE, CHIP_X, Z_LOW, Z_HIGH = 1, 2, 4, 8
LEFT_OFFSETS = (0, CORE, Z_LOW, Z_LOW | CORE)
RIGHT_OFFSETS = (0, CHIP_X, Z_HIGH, Z_HIGH | CHIP_X)
ROWS = 8
SIDE = 1024
PIECE = 256
HEAD = PIECE + 16
VMEM_BYTES = 48 * 2**20

NT = (((1,), (1,)), ((), ()))
NN = (((1,), (0,)), ((), ()))
F32, BF16 = jnp.float32, jnp.bfloat16


def dot(a, b, dims):
    return lax.dot_general(a, b, dims, preferred_element_type=F32)


def norm(values, axis):
    center = values - jnp.mean(values, axis=axis, keepdims=True)
    inverse = lax.rsqrt(jnp.mean(center * center, axis=axis, keepdims=True) + EPSILON)
    return center * inverse, inverse


def sigmoid(x):
    return 1.0 / (1.0 + jnp.exp(-x))


def call(kernel, outs, smem=(), hbm=(), vmem=(), scratch=(), micros=1):
    here, there = len(smem), len(smem) + len(hbm)
    total = there + len(vmem)
    count = len(hbm)

    def body(*refs):
        ins, rest = refs[:total], refs[total:]
        results, extra = rest[: len(outs)], rest[len(outs) :]
        buffers, extra = extra[:count], extra[count:]
        if count:
            sems, extra = extra[0], extra[1:]
            copies = [
                pltpu.make_async_copy(src, dst, sems.at[n])
                for n, (src, dst) in enumerate(zip(ins[here:there], buffers))
            ]
            for c in copies:
                c.start()
            for c in copies:
                c.wait()
        kernel(*ins[:here], *buffers, *ins[there:], *results, *extra)

    vmem_spec = pl.BlockSpec(memory_space=pltpu.VMEM)
    specs = [pl.BlockSpec(memory_space=pltpu.SMEM)] * here
    specs += [pl.BlockSpec(memory_space=pl.ANY)] * count
    specs += [vmem_spec] * len(vmem)
    own = [pltpu.VMEM(a.shape, a.dtype) for a in hbm]
    if count:
        own.append(pltpu.SemaphoreType.DMA((count,)))
    return pl.pallas_call(
        body,
        out_shape=[jax.ShapeDtypeStruct(s, d) for s, d in outs],
        in_specs=specs,
        out_specs=[vmem_spec] * len(outs),
        scratch_shapes=own + list(scratch),
        compiler_params=pltpu.CompilerParams(vmem_limit_bytes=VMEM_BYTES),
        cost_estimate=pl.CostEstimate(
            flops=0, bytes_accessed=int(micros * 3.0e6), transcendentals=0
        ),
    )(*smem, *hbm, *vmem)


def side_rows(quarter, row):
    return pl.ds(quarter * ROWS + row, 32, stride=4 * ROWS)


def store_side(rows_ref, row, result):
    for q in range(4):
        rows_ref[side_rows(q, row), :] = result[q * 32 : (q + 1) * 32]


def load_side(rows_ref, row):
    return jnp.concatenate([rows_ref[side_rows(q, row), :] for q in range(4)], axis=0)


def columns_of(me, offsets):
    return [pl.multiple_of((me ^ o) * ROWS, ROWS) for o in offsets]


def pick_columns(full_ref, starts):
    columns = [full_ref[:, pl.ds(s, ROWS), :] for s in starts]
    return jnp.concatenate(columns, axis=1).reshape(PIECE, 128)


def pack_kernel(me_ref, x_ref, cot_ref, mask_ref, own_ref, near_ref, far_ref, full_ref):
    me = me_ref[0]
    full_ref[...] = cot_ref[...].astype(F32)
    mask = jnp.concatenate([mask_ref[...].astype(F32), jnp.zeros((ROWS, 128), F32)], axis=0)
    places = [(own_ref, 0), (near_ref, 0), (far_ref, 0), (far_ref, HEAD + SIDE)]
    for (ref, place), offset in zip(places, LEFT_OFFSETS):
        piece = pick_columns(full_ref, columns_of(me ^ offset, RIGHT_OFFSETS))
        ref[place : place + PIECE, :] = piece.astype(BF16)
        ref[place + PIECE : place + HEAD, :] = mask.astype(BF16)
    near_ref[HEAD:, :] = x_ref[...]
    far_ref[HEAD : HEAD + SIDE, :] = x_ref[...]


def own_kernel(
    me_ref,
    x_ref,
    mask_ref,
    weight_ref,
    gate_weight_ref,
    out_weight_ref,
    gain_ref,
    bias_ref,
    mid_gain_ref,
    mid_bias_ref,
    left_ref,
    right_ref,
    sig_ref,
    weight_t_ref,
    block_ref,
    mid_ref,
    rows_ref,
    scaled_ref,
):
    weight_t_ref[...] = weight_ref[...].astype(F32).T.astype(BF16)
    for row in range(ROWS):
        normed, _ = norm(x_ref[row * 128 : (row + 1) * 128, :].astype(F32), 1)
        scaled = normed * gain_ref[...] + bias_ref[...]
        scaled_ref[row] = scaled
        projected = dot(weight_t_ref[...], scaled.astype(BF16), NT)
        keep = mask_ref[row : row + 1].astype(F32)
        for side in range(2):
            base = 256 * side
            gate, value = projected[base : base + 128], projected[base + 128 : base + 256]
            result = sigmoid(gate) * value
            store_side(rows_ref.at[side], row, result if side else result * keep)
    left_ref[...] = rows_ref[0].astype(BF16)
    right_ref[...] = rows_ref[1].astype(BF16)
    picked = pick_columns(scaled_ref, columns_of(me_ref[0], RIGHT_OFFSETS))
    sig_ref[...] = sigmoid(dot(picked.astype(BF16), gate_weight_ref[...], NN))

    repeat = lax.broadcasted_iota(jnp.int32, (512, 128), 0)
    lane = lax.broadcasted_iota(jnp.int32, (512, 128), 1)
    spread = jnp.where((repeat >> 2) == lane, 1.0, 0.0).astype(BF16)
    tall = dot(spread, out_weight_ref[...], NN)
    for m in range(4):
        block_ref[:, m * 128 : (m + 1) * 128] = jnp.where((repeat & 3) == m, tall, 0.0).astype(BF16)
    rows = lax.broadcasted_iota(jnp.int32, (ROWS, 128), 0)
    both = jnp.where(rows == 0, mid_gain_ref[...], mid_bias_ref[...])
    wide = jnp.zeros((ROWS, 512), F32)
    for _ in range(3):
        term = both.astype(BF16)
        wide = wide + dot(term, spread, NT)
        both = both - term.astype(F32)
    mid_ref[...] = wide


def peer_kernel(side_at, piece_at):
    def kernel(
        me_ref,
        message_ref,
        *refs,
    ):
        right_in, rest = refs[:-9], refs[-9:]
        weight_t_ref, gate_weight_ref, gain_ref, bias_ref = rest[:4]
        left_ref, right_ref, sig_ref, rows_ref, scaled_ref = rest[4:]
        per = SIDE // len(right_in)
        for row in range(ROWS):
            start = side_at + row * 128
            normed, _ = norm(message_ref[start : start + 128, :].astype(F32), 1)
            scaled = normed * gain_ref[...] + bias_ref[...]
            scaled_ref[row] = scaled
            projected = dot(weight_t_ref[:256, :], scaled.astype(BF16), NT)
            at = piece_at + PIECE
            keep = message_ref[at : at + 16, :].astype(F32)[row : row + 1]
            store_side(rows_ref.at[0], row, sigmoid(projected[:128]) * projected[128:] * keep)
        for row in range(ROWS):
            ref, start = right_in[row * 128 // per], row * 128 % per
            normed, _ = norm(ref[start : start + 128, :].astype(F32), 1)
            scaled = normed * gain_ref[...] + bias_ref[...]
            projected = dot(weight_t_ref[256:, :], scaled.astype(BF16), NT)
            store_side(rows_ref.at[1], row, sigmoid(projected[:128]) * projected[128:])
        left_ref[...] = rows_ref[0].astype(BF16)
        right_ref[...] = rows_ref[1].astype(BF16)
        picked = pick_columns(scaled_ref, columns_of(me_ref[0], RIGHT_OFFSETS))
        sig_ref[...] = sigmoid(dot(picked.astype(BF16), gate_weight_ref[...], NN))

    return kernel


def split_sum(values, ones):
    high = values.astype(BF16)
    low = (values - high.astype(F32)).astype(BF16)
    return dot(high, ones, NN) + dot(low, ones, NN)


def block_kernel(*refs):
    me_ref, left_refs, right_refs, sig_refs, message_refs = (
        refs[0],
        refs[1:5],
        refs[5:9],
        refs[9:13],
        refs[13:17],
    )
    block_ref, mid_ref = refs[17:19]
    out_refs, out_at = refs[19:23], (0, SIDE, 0, SIDE)
    left_outs = (refs[23], refs[20], refs[24], refs[22])
    right_outs = refs[25:31]
    (pairs_ref,) = refs[31:]
    piece_at = (0, 0, 0, SIDE)
    me = me_ref[0]
    groups = SIDE // 32
    lane = lax.broadcasted_iota(jnp.int32, (ROWS, 128), 1)
    of_quarter = [((lane >> 3) & 3) == q for q in range(4)]

    seen = [r[a + PIECE : a + HEAD, :].astype(F32) for r, a in zip(message_refs, piece_at)]
    valid = jnp.max(jnp.concatenate(seen, axis=0), axis=0, keepdims=True)
    src = lax.broadcasted_iota(jnp.int32, (128, 128), 0)
    dst = lax.broadcasted_iota(jnp.int32, (128, 128), 1)
    pick = jnp.zeros((128, 128), F32)
    for n, offset in enumerate(RIGHT_OFFSETS):
        wanted = (me ^ offset) * ROWS + (dst & 7)
        pick = jnp.where((src == wanted) & ((dst >> 5) == n), 1.0, pick)
    spread = jnp.broadcast_to(valid, (ROWS, 128)).astype(BF16)
    column_valid = dot(spread, pick.astype(BF16), NN)

    def slab(side_refs, g):
        return jnp.concatenate([r[g * 32 : (g + 1) * 32, :] for r in side_refs], axis=0)

    for g in range(groups):
        full = dot(slab(left_refs, g), slab(right_refs, g), NT).reshape(4, 4, ROWS, 128)
        for m in range(4):
            kept = full[m, 3]
            for q in range(3):
                kept = jnp.where(of_quarter[q], full[m, q], kept)
            pairs_ref[g * 32 + m * ROWS : g * 32 + (m + 1) * ROWS, :] = kept * column_valid

    turned = []
    for row in range(ROWS):
        turn = pairs_ref[pl.ds(row, 128, stride=ROWS), :].T.reshape(4, 4, ROWS, 128)
        turned.append(jnp.concatenate([turn[:, q].reshape(32, 128) for q in range(4)], axis=1))
    mixed = jnp.concatenate(turned, axis=0).astype(BF16).astype(F32)

    ones = jnp.where((src & 3) == (dst & 3), 1.0, 0.0).astype(BF16)

    def channel_mean(values):
        total = values[:, :128] + values[:, 128:256] + values[:, 256:384] + values[:, 384:]
        mean = split_sum(total, ones) * (1.0 / 128.0)
        return jnp.concatenate([mean] * 4, axis=1)

    mid_gain, mid_bias = mid_ref[0:1, :], mid_ref[1:2, :]
    center = mixed - channel_mean(mixed)
    inverse = lax.rsqrt(channel_mean(center * center) + EPSILON)
    normed = center * inverse
    scaled = (normed * mid_gain + mid_bias).astype(BF16)
    update = dot(scaled, block_ref[...], NN)
    grad_update = []
    for m in range(4):
        sig = sig_refs[m][...]
        out = sig * update[:, m * 128 : (m + 1) * 128]
        out_refs[m][out_at[m] : out_at[m] + PIECE, :] = out.astype(BF16)
        cot = message_refs[m][piece_at[m] : piece_at[m] + PIECE, :].astype(F32)
        grad_update.append((cot * sig).astype(BF16))
    grad_hat = dot(jnp.concatenate(grad_update, axis=1), block_ref[...], NT) * mid_gain
    first = channel_mean(grad_hat)
    second = channel_mean(grad_hat * normed)
    grad_mixed = inverse * (grad_hat - first - normed * second)

    for row in range(ROWS):
        part = grad_mixed[row * 32 : (row + 1) * 32]
        parts = [part[:, q * 128 : (q + 1) * 128].reshape(4, 1, ROWS, 128) for q in range(4)]
        turn = jnp.concatenate(parts, axis=1).reshape(128, 128)
        pairs_ref[pl.ds(row, 128, stride=ROWS), :] = turn.T

    def right_out(n, g):
        if n < 2:
            return right_outs[n], g * 32
        half = groups // 2
        return right_outs[2 * n - 2 + g // half], (g % half) * 32

    for g in range(groups):
        rows = []
        for m in range(4):
            part = pairs_ref[g * 32 + m * ROWS : g * 32 + (m + 1) * ROWS, :] * column_valid
            rows += [jnp.where(of_quarter[q], part, 0.0) for q in range(4)]
        spread = jnp.concatenate(rows, axis=0)
        grad_right = dot(spread.T.astype(BF16), slab(left_refs, g), NN).astype(BF16)
        grad_left = dot(spread.astype(BF16), slab(right_refs, g), NN).astype(BF16)
        for m in range(4):
            left_outs[m][g * 32 : (g + 1) * 32, :] = grad_left[m * 32 : (m + 1) * 32]
            ref, at = right_out(m, g)
            ref[at : at + 32, :] = grad_right[m * 32 : (m + 1) * 32]


def add_kernel(mine_ref, got_ref, sum_ref):
    sum_ref[...] = (mine_ref[...].astype(F32) + got_ref[...].astype(F32)).astype(BF16)


def add_left_kernel(mine_ref, piece_ref, got_ref, sum_ref, out_ref):
    sum_ref[...] = (mine_ref[...].astype(F32) + got_ref[:SIDE, :].astype(F32)).astype(BF16)
    out_ref[:PIECE, :] = piece_ref[...]
    out_ref[PIECE:, :] = got_ref[SIDE:, :]


def factor_kernel(
    x_ref,
    cot_ref,
    mask_ref,
    gate_weight_ref,
    gain_ref,
    bias_ref,
    weight_t_ref,
    factor_ref,
    normed_ref,
    inverse_ref,
    open_ref,
    gain_t_ref,
):
    gain_t = jnp.broadcast_to(gain_ref[...], (128, 128)).T
    bias_t = jnp.broadcast_to(bias_ref[...], (128, 128)).T
    gain_t_ref[...] = gain_t
    for row in range(ROWS):
        x = x_ref[row * 128 : (row + 1) * 128, :].astype(F32)
        normed, inverse = norm(x.T, 0)
        normed_ref[row] = normed
        inverse_ref[row : row + 1, :] = inverse
        scaled = (normed * gain_t + bias_t).astype(BF16)
        projected = dot(weight_t_ref[...], scaled, NN)
        keep = mask_ref[row : row + 1].astype(F32)
        for side in range(2):
            base = 256 * side
            gate = sigmoid(projected[base : base + 128])
            value = projected[base + 128 : base + 256]
            factor_ref[row, base : base + 128, :] = keep * value * gate * (1.0 - gate)
            factor_ref[row, base + 128 : base + 256, :] = keep * gate
        normed, _ = norm(x, 1)
        scaled = (normed * gain_ref[...] + bias_ref[...]).astype(BF16)
        gate_sig = sigmoid(dot(scaled, gate_weight_ref[...], NN))
        open_ref[row] = cot_ref[row].astype(F32) * (1.0 - gate_sig)


def out_kernel(me_ref, own_ref, near_ref, far_ref, open_ref, weight_ref, out_ref, grad_ref, full_ref):
    places = [(own_ref, 0), (near_ref, SIDE), (far_ref, 0), (far_ref, PIECE)]
    for (ref, at), offset in zip(places, LEFT_OFFSETS):
        piece = ref[at : at + PIECE, :].astype(F32).reshape(ROWS, 4, ROWS, 128)
        for n, start in enumerate(columns_of(me_ref[0] ^ offset, RIGHT_OFFSETS)):
            full_ref[:, pl.ds(start, ROWS), :] = piece[:, n]
    for row in range(ROWS):
        out = full_ref[row]
        out_ref[row] = out.astype(BF16)
        grad_gate = (open_ref[row] * out).astype(BF16)
        grad_ref[row] = dot(weight_ref[...], grad_gate, NT)


def pair_kernel(*refs):
    left_refs, right_refs = refs[0:3], refs[3:7]
    factor_ref, normed_ref, inverse_ref, gain_t_ref, gate_ref, weight_ref = refs[7:13]
    out_ref, rows_ref = refs[13:]
    half = SIDE // 2
    left = [r[:SIDE, :].astype(F32) for r in left_refs]
    rows_ref[0] = left[0] + left[1] + left[2]
    for part in range(2):
        at = slice(part * half, (part + 1) * half)
        right = right_refs[0][at, :].astype(F32) + right_refs[1][at, :].astype(F32)
        rows_ref[1, at, :] = right + right_refs[2 + part][...].astype(F32)
    for row in range(ROWS):
        parts = []
        for side in range(2):
            grad = load_side(rows_ref.at[side], row)
            for place in (256 * side, 256 * side + 128):
                parts.append((grad * factor_ref[row, place : place + 128, :]).astype(BF16))
        grad_scaled = dot(weight_ref[...], jnp.concatenate(parts, axis=0), NN) + gate_ref[row]
        normed = normed_ref[row]
        grad_hat = grad_scaled * gain_t_ref[...]
        first = jnp.mean(grad_hat, axis=0, keepdims=True)
        second = jnp.mean(grad_hat * normed, axis=0, keepdims=True)
        grad = inverse_ref[row : row + 1, :] * (grad_hat - first - normed * second)
        out_ref[row] = grad.T.astype(BF16)


def swap(values, offset):
    return lax.ppermute(values, "row", [(s, s ^ offset) for s in range(16)])


def blocks_device(
    pair_rep,
    pair_mask,
    cotangent,
    in_gain,
    in_bias,
    proj_weight,
    gate_weight,
    mid_gain,
    mid_bias,
    out_weight,
):
    me = lax.axis_index("row").astype(jnp.int32).reshape(1)
    gain, bias = in_gain.reshape(1, 128), in_bias.reshape(1, 128)
    flat = pair_rep.reshape(SIDE, 128)
    half = SIDE // 2
    cube = (ROWS, 128, 128)
    side, piece = ((SIDE, 128), BF16), ((PIECE, 128), BF16)
    both, halves = ((SIDE + PIECE, 128), BF16), ((half, 128), BF16)
    sig = ((PIECE, 128), F32)
    rows_scratch = pltpu.VMEM((2, SIDE, 128), F32)
    cube_scratch = pltpu.VMEM(cube, F32)

    z_first = swap(flat[:half], Z_HIGH)
    x_near = swap(flat, CHIP_X)
    own_message, near_message, far_message = call(
        pack_kernel,
        [((HEAD, 128), BF16), ((HEAD + SIDE, 128), BF16), ((2 * HEAD + SIDE, 128), BF16)],
        smem=[me],
        hbm=[flat, cotangent, pair_mask],
        scratch=[cube_scratch],
    )
    far = swap(far_message, Z_LOW)
    near = swap(near_message, CORE)
    z_second = swap(flat[half:], Z_HIGH)
    left_0, right_0, sig_0, weight_t, block_weight, mid = call(
        own_kernel,
        [side, side, sig, ((512, 128), BF16), ((512, 512), BF16), ((ROWS, 512), F32)],
        smem=[me],
        hbm=[
            flat,
            pair_mask,
            proj_weight,
            gate_weight,
            out_weight,
            gain,
            bias,
            mid_gain.reshape(1, 128),
            mid_bias.reshape(1, 128),
        ],
        scratch=[rows_scratch, cube_scratch],
        micros=2,
    )
    x_first = swap(z_first, CHIP_X)
    both_message = swap(far[HEAD:], CORE)
    x_second = swap(z_second, CHIP_X)

    def peer(message, side_at, piece_at, *right_in):
        return call(
            peer_kernel(side_at, piece_at),
            [side, side, sig],
            smem=[me],
            hbm=[],
            vmem=[message, *right_in, weight_t, gate_weight, gain, bias],
            scratch=[rows_scratch, cube_scratch],
            micros=2,
        )

    left_1, right_1, sig_1 = peer(near, HEAD, 0, x_near)
    left_2, right_2, sig_2 = peer(far, HEAD, 0, z_first, z_second)
    left_3, right_3, sig_3 = peer(both_message, 0, SIDE, x_first, x_second)

    out_0, near_back, out_2, both_back, grad_left_0, grad_left_2, *grad_right = call(
        block_kernel,
        [piece, both, piece, both, side, side, side, side] + [halves] * 4,
        smem=[me],
        vmem=[left_0, left_1, left_2, left_3]
        + [right_0, right_1, right_2, right_3]
        + [sig_0, sig_1, sig_2, sig_3]
        + [own_message, near, far, both_message]
        + [block_weight, mid],
        scratch=[pltpu.VMEM((SIDE, 128), F32)],
        micros=3,
    )
    x_got = [swap(grad_right[4], CHIP_X), swap(grad_right[5], CHIP_X)]
    both_got = swap(both_back, CORE)
    z_got = []
    for mine, got in zip(grad_right[2:4], x_got):
        (total,) = call(add_kernel, [halves], vmem=[mine, got], micros=0.1)
        z_got.append(swap(total, Z_HIGH))
    left_sum, out_far = call(
        add_left_kernel,
        [side, ((2 * PIECE, 128), BF16)],
        vmem=[grad_left_2, out_2, both_got],
        micros=0.1,
    )
    out_far = swap(out_far, Z_LOW)
    left_got = swap(left_sum, Z_LOW)
    near_got = swap(near_back, CORE)
    right_near = swap(grad_right[1], CHIP_X)

    factors, normed, inverse, open_part, gain_t = call(
        factor_kernel,
        [((ROWS, 512, 128), F32), (cube, F32), ((ROWS, 128), F32), (cube, F32), ((128, 128), F32)],
        hbm=[flat, cotangent, pair_mask, gate_weight, gain, bias],
        vmem=[weight_t],
        micros=2,
    )
    output, gate_part = call(
        out_kernel,
        [(cube, BF16), (cube, F32)],
        smem=[me],
        vmem=[out_0, near_got, out_far, open_part, gate_weight],
        scratch=[cube_scratch],
    )
    (grad_pair,) = call(
        pair_kernel,
        [(cube, BF16)],
        vmem=[grad_left_0, near_got, left_got, grad_right[0], right_near, *z_got]
        + [factors, normed, inverse, gain_t, gate_part, proj_weight],
        scratch=[rows_scratch],
        micros=2,
    )
    return (output, grad_pair)


def norm_stats(values, reduce_axis):
    center = values - jnp.mean(values, axis=reduce_axis, keepdims=True)
    inverse = lax.rsqrt(jnp.mean(center * center, axis=reduce_axis, keepdims=True) + EPSILON)
    return (center * inverse, inverse)


def norm_back(grad_hat, normed, inverse, reduce_axis):
    first = jnp.mean(grad_hat, axis=reduce_axis, keepdims=True)
    second = jnp.mean(grad_hat * normed, axis=reduce_axis, keepdims=True)
    return inverse * (grad_hat - first - normed * second)


def forward_products(left_chan, right_chan):
    return jnp.einsum("hik,hjk->hij", left_chan, right_chan, preferred_element_type=jnp.float32)


def backward_products(grad_full, left_chan, right_chan):
    grad_left = jnp.einsum(
        "hij,hjk->hik", grad_full, right_chan, preferred_element_type=jnp.float32
    )
    grad_right = jnp.einsum(
        "hij,hik->hjk", grad_full, left_chan, preferred_element_type=jnp.float32
    )
    return jnp.stack([grad_left, grad_right]).astype(jnp.bfloat16)


def channels_device(
    pair_rep,
    pair_mask,
    cotangent,
    in_gain,
    in_bias,
    proj_weight,
    gate_weight,
    mid_gain,
    mid_bias,
    out_weight,
):
    width = pair_rep.shape[2]
    hidden = out_weight.shape[0]
    weights_four = proj_weight.reshape(width, 2, 2, hidden)
    mask_float = pair_mask.astype(jnp.float32)
    normed_in, inverse_in = norm_stats(pair_rep.astype(jnp.float32), 2)
    scaled_in = (normed_in * in_gain + in_bias).astype(jnp.bfloat16)
    gate_pre = jnp.einsum(
        "ijc,csh->shij", scaled_in, weights_four[:, :, 0], preferred_element_type=jnp.float32
    )
    value_pre = jnp.einsum(
        "ijc,csh->shij", scaled_in, weights_four[:, :, 1], preferred_element_type=jnp.float32
    )
    sigmoid_gate = jax.nn.sigmoid(gate_pre)
    both_sides = (sigmoid_gate * value_pre * mask_float).astype(jnp.bfloat16)
    gate_sig = jax.nn.sigmoid(
        jnp.einsum("ijc,cd->ijd", scaled_in, gate_weight, preferred_element_type=jnp.float32)
    )
    sides_chan = lax.all_to_all(both_sides, "row", split_axis=1, concat_axis=2, tiled=True)
    partial_sum = forward_products(sides_chan[0], sides_chan[1])
    product = lax.psum_scatter(partial_sum, "col", scatter_dimension=2, tiled=True).astype(
        jnp.bfloat16
    )
    mixed_pair = lax.all_to_all(product, "row", split_axis=1, concat_axis=0, tiled=True)
    normed_mid, inverse_mid = norm_stats(mixed_pair.astype(jnp.float32), 0)
    scaled_mid = (normed_mid * mid_gain[:, None, None] + mid_bias[:, None, None]).astype(
        jnp.bfloat16
    )
    update = jnp.einsum("hij,hc->ijc", scaled_mid, out_weight, preferred_element_type=jnp.float32)
    output = (gate_sig * update).astype(jnp.bfloat16)
    grad_out = cotangent.astype(jnp.float32)
    grad_update = (grad_out * gate_sig).astype(jnp.bfloat16)
    grad_gate = (grad_out * update * gate_sig * (1.0 - gate_sig)).astype(jnp.bfloat16)
    grad_scaled_mid = jnp.einsum(
        "ijc,hc->hij", grad_update, out_weight, preferred_element_type=jnp.float32
    )
    grad_mixed = norm_back(
        grad_scaled_mid * mid_gain[:, None, None], normed_mid, inverse_mid, 0
    ).astype(jnp.bfloat16)
    grad_chan = lax.all_to_all(grad_mixed, "row", split_axis=0, concat_axis=1, tiled=True)
    grad_full = lax.all_gather(grad_chan, "col", axis=2, tiled=True)
    grad_local = backward_products(grad_full, sides_chan[0], sides_chan[1])
    grad_sides = lax.all_to_all(grad_local, "row", split_axis=2, concat_axis=1, tiled=True)
    side_float = grad_sides.astype(jnp.float32) * mask_float
    grad_value = (side_float * sigmoid_gate).astype(jnp.bfloat16)
    grad_gate_pre = (side_float * value_pre * sigmoid_gate * (1.0 - sigmoid_gate)).astype(
        jnp.bfloat16
    )
    grad_scaled = jnp.einsum(
        "shij,csh->ijc", grad_gate_pre, weights_four[:, :, 0], preferred_element_type=jnp.float32
    )
    grad_scaled = grad_scaled + jnp.einsum(
        "shij,csh->ijc", grad_value, weights_four[:, :, 1], preferred_element_type=jnp.float32
    )
    grad_scaled = grad_scaled + jnp.einsum(
        "ijd,cd->ijc", grad_gate, gate_weight, preferred_element_type=jnp.float32
    )
    grad_pair = norm_back(grad_scaled * in_gain, normed_in, inverse_in, 2).astype(jnp.bfloat16)
    return (output, grad_pair)


def solution(mesh):
    blocks = mesh.shape["row"] == 16 and mesh.shape["col"] == 1
    placed = (
        P(("grp", "row"), "col", None),
        P(("grp", "row"), "col"),
        P(("grp", "row"), "col", None),
        P(),
        P(),
        P(),
        P(),
        P(),
        P(),
        P(),
    )
    return jax.shard_map(
        blocks_device if blocks else channels_device,
        mesh=mesh,
        in_specs=placed,
        out_specs=(P(("grp", "row"), "col", None), P(("grp", "row"), "col", None)),
        check_vma=False,
    )
```

```python
import jax
import jax.numpy as jnp
from jax import lax
from jax.experimental import pallas as pl
from jax.experimental.pallas import tpu as pltpu
from jax.sharding import PartitionSpec as P

EPSILON = 1e-05
CORE, CHIP_X, Z_LOW, Z_HIGH = 1, 2, 4, 8
LEFT_OFFSETS = (0, CORE, Z_LOW, Z_LOW | CORE)
RIGHT_OFFSETS = (0, CHIP_X, Z_HIGH, Z_HIGH | CHIP_X)
ROWS = 8
SIDE = 1024
PIECE = 256
HEAD = PIECE + 16
VMEM_BYTES = 48 * 2**20
WAIT = 5 * 10**9

NT = (((1,), (1,)), ((), ()))
NN = (((1,), (0,)), ((), ()))
TN = (((0,), (0,)), ((), ()))
F32, BF16 = jnp.float32, jnp.bfloat16


def dot(a, b, dims):
    return lax.dot_general(a, b, dims, preferred_element_type=F32)


def norm(values, axis):
    center = values - jnp.mean(values, axis=axis, keepdims=True)
    inverse = lax.rsqrt(jnp.mean(center * center, axis=axis, keepdims=True) + EPSILON)
    return center * inverse, inverse


def sigmoid(x):
    return 0.5 * jnp.tanh(0.5 * x) + 0.5


def call(kernel, outs, smem=(), hbm=(), vmem=(), scratch=(), weight=2**26, limit=VMEM_BYTES):
    vmem_spec = pl.BlockSpec(memory_space=pltpu.VMEM)
    specs = [pl.BlockSpec(memory_space=pltpu.SMEM)] * len(smem)
    specs += [pl.BlockSpec(memory_space=pltpu.HBM)] * len(hbm)
    specs += [vmem_spec] * len(vmem)
    return pl.pallas_call(
        kernel,
        out_shape=[jax.ShapeDtypeStruct(s, d) for s, d in outs],
        in_specs=specs,
        out_specs=[vmem_spec] * len(outs),
        scratch_shapes=list(scratch),
        compiler_params=pltpu.CompilerParams(vmem_limit_bytes=limit),
        cost_estimate=pl.CostEstimate(flops=weight, bytes_accessed=2**18, transcendentals=0),
    )(*smem, *hbm, *vmem)


def load_kernel(*refs):
    count = (len(refs) - 3) // 2
    ins, outs = refs[:count], refs[count:-1]
    half = SIDE // 2
    pairs = list(zip(ins, outs[:count]))
    pairs += [(ins[0].at[pl.ds(n * half, half)], outs[count + n]) for n in range(2)]
    copies = [pltpu.make_async_copy(a, b, refs[-1].at[n]) for n, (a, b) in enumerate(pairs)]
    for c in copies:
        c.start()
    for c in copies:
        c.wait()


def side_rows(quarter, row):
    return pl.ds(quarter * ROWS + row, 32, stride=4 * ROWS)


def store_side(rows_ref, row, result):
    for q in range(4):
        rows_ref[side_rows(q, row), :] = result[q * 32 : (q + 1) * 32]


def load_side(rows_ref, row):
    return jnp.concatenate([rows_ref[side_rows(q, row), :] for q in range(4)], axis=0)


def columns_of(me, offsets):
    return [pl.multiple_of((me ^ o) * ROWS, ROWS) for o in offsets]


def pick_columns(full_ref, starts):
    columns = [full_ref[:, pl.ds(s, ROWS), :] for s in starts]
    return jnp.concatenate(columns, axis=1).reshape(PIECE, 128)


def pack_kernel(me_ref, x_ref, cot_ref, mask_ref, own_ref, near_ref, far_ref, full_ref):
    me = me_ref[0]
    full_ref[...] = cot_ref[...].astype(F32)
    mask = jnp.concatenate([mask_ref[...].astype(F32), jnp.zeros((ROWS, 128), F32)], axis=0)
    places = [(own_ref, 0), (near_ref, 0), (far_ref, 0), (far_ref, HEAD + SIDE)]
    for (ref, place), offset in zip(places, LEFT_OFFSETS):
        piece = pick_columns(full_ref, columns_of(me ^ offset, RIGHT_OFFSETS))
        ref[place : place + PIECE, :] = piece.astype(BF16)
        ref[place + PIECE : place + HEAD, :] = mask.astype(BF16)
    near_ref[HEAD:, :] = x_ref[...]
    far_ref[HEAD : HEAD + SIDE, :] = x_ref[...]


def own_kernel(
    me_ref,
    x_ref,
    mask_ref,
    weight_ref,
    gate_weight_ref,
    out_weight_ref,
    gain_ref,
    bias_ref,
    mid_gain_ref,
    mid_bias_ref,
    left_ref,
    right_ref,
    sig_ref,
    weight_t_ref,
    block_ref,
    mid_ref,
    rows_ref,
    scaled_ref,
):
    weight_t_ref[...] = weight_ref[...].astype(F32).T.astype(BF16)
    for row in range(ROWS):
        normed, _ = norm(x_ref[row * 128 : (row + 1) * 128, :].astype(F32), 1)
        scaled = normed * gain_ref[...] + bias_ref[...]
        scaled_ref[row] = scaled
        projected = dot(weight_t_ref[...], scaled.astype(BF16), NT)
        keep = mask_ref[row : row + 1].astype(F32)
        for side in range(2):
            base = 256 * side
            gate, value = projected[base : base + 128], projected[base + 128 : base + 256]
            result = sigmoid(gate) * value
            store_side(rows_ref.at[side], row, result if side else result * keep)
    left_ref[...] = rows_ref[0].astype(BF16)
    right_ref[...] = rows_ref[1].astype(BF16)
    picked = pick_columns(scaled_ref, columns_of(me_ref[0], RIGHT_OFFSETS))
    sig_ref[...] = sigmoid(dot(picked.astype(BF16), gate_weight_ref[...], NN))

    repeat = lax.broadcasted_iota(jnp.int32, (512, 128), 0)
    lane = lax.broadcasted_iota(jnp.int32, (512, 128), 1)
    spread = jnp.where((repeat >> 2) == lane, 1.0, 0.0).astype(BF16)
    tall = dot(spread, out_weight_ref[...], NN)
    for m in range(4):
        block_ref[:, m * 128 : (m + 1) * 128] = jnp.where((repeat & 3) == m, tall, 0.0).astype(BF16)
    rows = lax.broadcasted_iota(jnp.int32, (ROWS, 128), 0)
    both = jnp.where(rows == 0, mid_gain_ref[...], mid_bias_ref[...])
    wide = jnp.zeros((ROWS, 512), F32)
    for _ in range(3):
        term = both.astype(BF16)
        wide = wide + dot(term, spread, NT)
        both = both - term.astype(F32)
    mid_ref[...] = wide


def peer_kernel(side_at, piece_at):
    def kernel(
        me_ref,
        message_ref,
        *refs,
    ):
        right_in, rest = refs[:-9], refs[-9:]
        weight_t_ref, gate_weight_ref, gain_ref, bias_ref = rest[:4]
        left_ref, right_ref, sig_ref, rows_ref, scaled_ref = rest[4:]
        per = SIDE // len(right_in)
        for row in range(ROWS):
            start = side_at + row * 128
            normed, _ = norm(message_ref[start : start + 128, :].astype(F32), 1)
            scaled = normed * gain_ref[...] + bias_ref[...]
            scaled_ref[row] = scaled
            projected = dot(weight_t_ref[:256, :], scaled.astype(BF16), NT)
            at = piece_at + PIECE
            keep = message_ref[at : at + 16, :].astype(F32)[row : row + 1]
            store_side(rows_ref.at[0], row, sigmoid(projected[:128]) * projected[128:] * keep)
        for row in range(ROWS):
            ref, start = right_in[row * 128 // per], row * 128 % per
            normed, _ = norm(ref[start : start + 128, :].astype(F32), 1)
            scaled = normed * gain_ref[...] + bias_ref[...]
            projected = dot(weight_t_ref[256:, :], scaled.astype(BF16), NT)
            store_side(rows_ref.at[1], row, sigmoid(projected[:128]) * projected[128:])
        left_ref[...] = rows_ref[0].astype(BF16)
        right_ref[...] = rows_ref[1].astype(BF16)
        picked = pick_columns(scaled_ref, columns_of(me_ref[0], RIGHT_OFFSETS))
        sig_ref[...] = sigmoid(dot(picked.astype(BF16), gate_weight_ref[...], NN))

    return kernel


def split_sum(values, ones):
    high = values.astype(BF16)
    low = (values - high.astype(F32)).astype(BF16)
    return dot(high, ones, NN) + dot(low, ones, NN)


def block_kernel(*refs):
    me_ref, left_refs, right_refs, sig_refs, message_refs = (
        refs[0],
        refs[1:5],
        refs[5:9],
        refs[9:13],
        refs[13:17],
    )
    block_ref, mid_ref = refs[17:19]
    core_ref = refs[21]
    out_refs, out_at = (refs[19], core_ref, refs[20], core_ref), (0, SIDE, 0, 2 * SIDE + PIECE)
    left_outs, left_at = (refs[22], core_ref, refs[23], core_ref), (0, 0, 0, SIDE + PIECE)
    right_outs = refs[24:30]
    (pairs_ref,) = refs[30:]
    piece_at = (0, 0, 0, SIDE)
    me = me_ref[0]
    groups = SIDE // 32
    lane = lax.broadcasted_iota(jnp.int32, (ROWS, 128), 1)
    of_quarter = [((lane >> 3) & 3) == q for q in range(4)]

    seen = [r[a + PIECE : a + HEAD, :].astype(F32) for r, a in zip(message_refs, piece_at)]
    valid = jnp.max(jnp.concatenate(seen, axis=0), axis=0, keepdims=True)
    src = lax.broadcasted_iota(jnp.int32, (128, 128), 0)
    dst = lax.broadcasted_iota(jnp.int32, (128, 128), 1)
    pick = jnp.zeros((128, 128), F32)
    for n, offset in enumerate(RIGHT_OFFSETS):
        wanted = (me ^ offset) * ROWS + (dst & 7)
        pick = jnp.where((src == wanted) & ((dst >> 5) == n), 1.0, pick)
    spread = jnp.broadcast_to(valid, (ROWS, 128)).astype(BF16)
    column_valid = dot(spread, pick.astype(BF16), NN)

    def slab(side_refs, g):
        return jnp.concatenate([r[g * 32 : (g + 1) * 32, :] for r in side_refs], axis=0)

    for g in range(groups):
        full = dot(slab(left_refs, g), slab(right_refs, g), NT).reshape(4, 4, ROWS, 128)
        for m in range(4):
            kept = full[m, 3]
            for q in range(3):
                kept = jnp.where(of_quarter[q], full[m, q], kept)
            pairs_ref[g * 32 + m * ROWS : g * 32 + (m + 1) * ROWS, :] = kept * column_valid

    turned = []
    for row in range(ROWS):
        turn = pairs_ref[pl.ds(row, 128, stride=ROWS), :].T.reshape(4, 4, ROWS, 128)
        turned.append(jnp.concatenate([turn[:, q].reshape(32, 128) for q in range(4)], axis=1))
    mixed = jnp.concatenate(turned, axis=0).astype(BF16).astype(F32)

    ones = jnp.where((src & 3) == (dst & 3), 1.0, 0.0).astype(BF16)

    def channel_mean(values):
        total = values[:, :128] + values[:, 128:256] + values[:, 256:384] + values[:, 384:]
        mean = split_sum(total, ones) * (1.0 / 128.0)
        return jnp.concatenate([mean] * 4, axis=1)

    mid_gain, mid_bias = mid_ref[0:1, :], mid_ref[1:2, :]
    center = mixed - channel_mean(mixed)
    inverse = lax.rsqrt(channel_mean(center * center) + EPSILON)
    normed = center * inverse
    scaled = (normed * mid_gain + mid_bias).astype(BF16)
    update = dot(scaled, block_ref[...], NN)
    grad_update = []
    for m in range(4):
        sig = sig_refs[m][...]
        out = sig * update[:, m * 128 : (m + 1) * 128]
        out_refs[m][out_at[m] : out_at[m] + PIECE, :] = out.astype(BF16)
        cot = message_refs[m][piece_at[m] : piece_at[m] + PIECE, :].astype(F32)
        grad_update.append((cot * sig).astype(BF16))
    grad_hat = dot(jnp.concatenate(grad_update, axis=1), block_ref[...], NT) * mid_gain
    first = channel_mean(grad_hat)
    second = channel_mean(grad_hat * normed)
    grad_mixed = inverse * (grad_hat - first - normed * second)

    for row in range(ROWS):
        part = grad_mixed[row * 32 : (row + 1) * 32]
        parts = [part[:, q * 128 : (q + 1) * 128].reshape(4, 1, ROWS, 128) for q in range(4)]
        turn = jnp.concatenate(parts, axis=1).reshape(128, 128)
        pairs_ref[pl.ds(row, 128, stride=ROWS), :] = turn.T

    def right_out(n, g):
        if n < 2:
            return right_outs[n], g * 32
        half = groups // 2
        return right_outs[2 * n - 2 + g // half], (g % half) * 32

    for g in range(groups):
        rows = []
        for m in range(4):
            part = pairs_ref[g * 32 + m * ROWS : g * 32 + (m + 1) * ROWS, :] * column_valid
            rows += [jnp.where(of_quarter[q], part, 0.0) for q in range(4)]
        spread = jnp.concatenate(rows, axis=0).astype(BF16)
        grad_right = dot(spread, slab(left_refs, g), TN).astype(BF16)
        grad_left = dot(spread, slab(right_refs, g), NN).astype(BF16)
        for m in range(4):
            at = left_at[m] + g * 32
            left_outs[m][at : at + 32, :] = grad_left[m * 32 : (m + 1) * 32]
            ref, at = right_out(m, g)
            ref[at : at + 32, :] = grad_right[m * 32 : (m + 1) * 32]


def pass_kernel(start):
    def kernel(message_ref, *refs):
        refs[-1][...] = message_ref[start:, :]

    return kernel


def add_kernel(mine_ref, got_ref, sum_ref):
    sum_ref[...] = (mine_ref[...].astype(F32) + got_ref[...].astype(F32)).astype(BF16)


def add_left_kernel(mine_ref, piece_ref, got_ref, sum_ref, out_ref):
    at = SIDE + PIECE
    sum_ref[...] = (mine_ref[...].astype(F32) + got_ref[at : at + SIDE, :].astype(F32)).astype(BF16)
    out_ref[:PIECE, :] = piece_ref[...]
    out_ref[PIECE:, :] = got_ref[at + SIDE :, :]


def factor_kernel(
    x_ref,
    cot_ref,
    mask_ref,
    gate_weight_ref,
    gain_ref,
    bias_ref,
    weight_t_ref,
    factor_ref,
    normed_ref,
    inverse_ref,
    open_ref,
    gain_t_ref,
):
    gain_t = jnp.broadcast_to(gain_ref[...], (128, 128)).T
    bias_t = jnp.broadcast_to(bias_ref[...], (128, 128)).T
    gain_t_ref[...] = gain_t
    for row in range(ROWS):
        x = x_ref[row * 128 : (row + 1) * 128, :].astype(F32)
        normed, inverse = norm(x.T, 0)
        normed_ref[row] = normed
        inverse_ref[row : row + 1, :] = inverse
        scaled = (normed * gain_t + bias_t).astype(BF16)
        projected = dot(weight_t_ref[...], scaled, NN)
        keep = mask_ref[row : row + 1].astype(F32)
        for side in range(2):
            base = 256 * side
            gate = sigmoid(projected[base : base + 128])
            value = projected[base + 128 : base + 256]
            factor_ref[row, base : base + 128, :] = keep * value * gate * (1.0 - gate)
            factor_ref[row, base + 128 : base + 256, :] = keep * gate
        normed, _ = norm(x, 1)
        scaled = (normed * gain_ref[...] + bias_ref[...]).astype(BF16)
        gate_sig = sigmoid(dot(scaled, gate_weight_ref[...], NN))
        open_ref[row] = cot_ref[row].astype(F32) * (1.0 - gate_sig)


def out_kernel(me_ref, own_ref, near_ref, far_ref, open_ref, weight_ref, out_ref, grad_ref, full_ref):
    places = [(own_ref, 0), (near_ref, SIDE), (far_ref, 0), (far_ref, PIECE)]
    for (ref, at), offset in zip(places, LEFT_OFFSETS):
        piece = ref[at : at + PIECE, :].astype(F32).reshape(ROWS, 4, ROWS, 128)
        for n, start in enumerate(columns_of(me_ref[0] ^ offset, RIGHT_OFFSETS)):
            full_ref[:, pl.ds(start, ROWS), :] = piece[:, n]
    for row in range(ROWS):
        out = full_ref[row]
        out_ref[row] = out.astype(BF16)
        grad_gate = (open_ref[row] * out).astype(BF16)
        grad_ref[row] = dot(weight_ref[...], grad_gate, NT)


def pair_kernel(*refs):
    left_refs, right_refs = refs[0:3], refs[3:7]
    factor_ref, normed_ref, inverse_ref, gain_t_ref, gate_ref, weight_ref = refs[7:13]
    out_ref, rows_ref = refs[13:]
    half = SIDE // 2
    left = [r[:SIDE, :].astype(F32) for r in left_refs]
    rows_ref[0] = left[0] + left[1] + left[2]
    for part in range(2):
        at = slice(part * half, (part + 1) * half)
        right = right_refs[0][at, :].astype(F32) + right_refs[1][at, :].astype(F32)
        rows_ref[1, at, :] = right + right_refs[2 + part][...].astype(F32)
    for row in range(ROWS):
        parts = []
        for side in range(2):
            grad = load_side(rows_ref.at[side], row)
            for place in (256 * side, 256 * side + 128):
                parts.append((grad * factor_ref[row, place : place + 128, :]).astype(BF16))
        grad_scaled = dot(weight_ref[...], jnp.concatenate(parts, axis=0), NN) + gate_ref[row]
        normed = normed_ref[row]
        grad_hat = grad_scaled * gain_t_ref[...]
        first = jnp.mean(grad_hat, axis=0, keepdims=True)
        second = jnp.mean(grad_hat * normed, axis=0, keepdims=True)
        grad = inverse_ref[row : row + 1, :] * (grad_hat - first - normed * second)
        out_ref[row] = grad.T.astype(BF16)


def swap(values, offset):
    return lax.ppermute(values, "row", [(s, s ^ offset) for s in range(16)])


def blocks_device(
    pair_rep,
    pair_mask,
    cotangent,
    in_gain,
    in_bias,
    proj_weight,
    gate_weight,
    mid_gain,
    mid_bias,
    out_weight,
):
    me = lax.axis_index("row").astype(jnp.int32).reshape(1)
    half = SIDE // 2
    cube = (ROWS, 128, 128)
    side, piece = ((SIDE, 128), BF16), ((PIECE, 128), BF16)
    halves, core = ((half, 128), BF16), ((2 * (SIDE + PIECE), 128), BF16)
    sig = ((PIECE, 128), F32)
    rows_scratch = pltpu.VMEM((2, SIDE, 128), F32)
    cube_scratch = pltpu.VMEM(cube, F32)

    inputs = [pair_rep.reshape(SIDE, 128), cotangent, pair_mask]
    loaded = call(
        load_kernel,
        [(a.shape, a.dtype) for a in inputs] + [halves] * 2,
        hbm=inputs,
        scratch=[pltpu.SemaphoreType.DMA((len(inputs) + 2,))],
        limit=None,
    )
    flat, cot, mask, first, second = loaded
    proj, gate, out_w = proj_weight, gate_weight, out_weight
    gain, bias = in_gain.reshape(1, 128), in_bias.reshape(1, 128)
    mid_gain, mid_bias = mid_gain.reshape(1, 128), mid_bias.reshape(1, 128)

    z_first = swap(first, Z_HIGH)
    own_message, near_message, far_message = call(
        pack_kernel,
        [((HEAD, 128), BF16), ((HEAD + SIDE, 128), BF16), ((2 * HEAD + SIDE, 128), BF16)],
        smem=[me],
        vmem=[flat, cot, mask],
        scratch=[cube_scratch],
    )
    far = swap(far_message, Z_LOW)
    x_near = swap(flat, CHIP_X)
    near = swap(near_message, CORE)
    z_second = swap(second, Z_HIGH)
    left_0, right_0, sig_0, weight_t, block_weight, mid = call(
        own_kernel,
        [side, side, sig, ((512, 128), BF16), ((512, 512), BF16), ((ROWS, 512), F32)],
        smem=[me],
        vmem=[flat, mask, proj, gate, out_w, gain, bias, mid_gain, mid_bias],
        scratch=[rows_scratch, cube_scratch],
        weight=WAIT,
    )

    def peer(message, side_at, piece_at, *right_in):
        return call(
            peer_kernel(side_at, piece_at),
            [side, side, sig],
            smem=[me],
            vmem=[message, *right_in, weight_t, gate, gain, bias],
            scratch=[rows_scratch, cube_scratch],
            weight=WAIT,
        )

    left_1, right_1, sig_1 = peer(near, HEAD, 0, x_near)
    (passed,) = call(pass_kernel(HEAD), [((HEAD + SIDE, 128), BF16)], vmem=[far, sig_1])
    both_message = swap(passed, CORE)
    (passed,) = call(pass_kernel(0), [halves], vmem=[z_first, sig_1])
    x_first = swap(passed, CHIP_X)
    (passed,) = call(pass_kernel(0), [halves], vmem=[z_second, sig_1])
    x_second = swap(passed, CHIP_X)
    left_2, right_2, sig_2 = peer(far, HEAD, 0, z_first, z_second)
    left_3, right_3, sig_3 = peer(both_message, 0, SIDE, x_first, x_second)

    out_0, out_2, core_back, grad_left_0, grad_left_2, *grad_right = call(
        block_kernel,
        [piece, piece, core, side, side, side, side] + [halves] * 4,
        smem=[me],
        vmem=[left_0, left_1, left_2, left_3]
        + [right_0, right_1, right_2, right_3]
        + [sig_0, sig_1, sig_2, sig_3]
        + [own_message, near, far, both_message]
        + [block_weight, mid],
        scratch=[pltpu.VMEM((SIDE, 128), F32)],
    )
    core_got = swap(core_back, CORE)
    x_got = [swap(grad_right[4], CHIP_X), swap(grad_right[5], CHIP_X)]
    left_sum, out_far = call(
        add_left_kernel,
        [side, ((2 * PIECE, 128), BF16)],
        vmem=[grad_left_2, out_2, core_got],
    )
    left_got = swap(left_sum, Z_LOW)
    out_far = swap(out_far, Z_LOW)
    totals = []
    for mine, got in zip(grad_right[2:4], x_got):
        totals += call(add_kernel, [halves], vmem=[mine, got])
    z_got = [swap(total, Z_HIGH) for total in totals]
    (passed,) = call(pass_kernel(0), [side], vmem=[grad_right[1], *totals])
    right_near = swap(passed, CHIP_X)

    factors, normed, inverse, open_part, gain_t = call(
        factor_kernel,
        [((ROWS, 512, 128), F32), (cube, F32), ((ROWS, 128), F32), (cube, F32), ((128, 128), F32)],
        vmem=[flat, cot, mask, gate, gain, bias, weight_t],
        weight=WAIT,
    )
    output, gate_part = call(
        out_kernel,
        [(cube, BF16), (cube, F32)],
        smem=[me],
        vmem=[out_0, core_got, out_far, open_part, gate],
        scratch=[cube_scratch],
    )
    (grad_pair,) = call(
        pair_kernel,
        [(cube, BF16)],
        vmem=[grad_left_0, core_got, left_got, grad_right[0], right_near, *z_got]
        + [factors, normed, inverse, gain_t, gate_part, proj],
        scratch=[rows_scratch],
    )
    return (output, grad_pair)


def norm_stats(values, reduce_axis):
    center = values - jnp.mean(values, axis=reduce_axis, keepdims=True)
    inverse = lax.rsqrt(jnp.mean(center * center, axis=reduce_axis, keepdims=True) + EPSILON)
    return (center * inverse, inverse)


def norm_back(grad_hat, normed, inverse, reduce_axis):
    first = jnp.mean(grad_hat, axis=reduce_axis, keepdims=True)
    second = jnp.mean(grad_hat * normed, axis=reduce_axis, keepdims=True)
    return inverse * (grad_hat - first - normed * second)


def forward_products(left_chan, right_chan):
    return jnp.einsum("hik,hjk->hij", left_chan, right_chan, preferred_element_type=jnp.float32)


def backward_products(grad_full, left_chan, right_chan):
    grad_left = jnp.einsum(
        "hij,hjk->hik", grad_full, right_chan, preferred_element_type=jnp.float32
    )
    grad_right = jnp.einsum(
        "hij,hik->hjk", grad_full, left_chan, preferred_element_type=jnp.float32
    )
    return jnp.stack([grad_left, grad_right]).astype(jnp.bfloat16)


def channels_device(
    pair_rep,
    pair_mask,
    cotangent,
    in_gain,
    in_bias,
    proj_weight,
    gate_weight,
    mid_gain,
    mid_bias,
    out_weight,
):
    width = pair_rep.shape[2]
    hidden = out_weight.shape[0]
    weights_four = proj_weight.reshape(width, 2, 2, hidden)
    mask_float = pair_mask.astype(jnp.float32)
    normed_in, inverse_in = norm_stats(pair_rep.astype(jnp.float32), 2)
    scaled_in = (normed_in * in_gain + in_bias).astype(jnp.bfloat16)
    gate_pre = jnp.einsum(
        "ijc,csh->shij", scaled_in, weights_four[:, :, 0], preferred_element_type=jnp.float32
    )
    value_pre = jnp.einsum(
        "ijc,csh->shij", scaled_in, weights_four[:, :, 1], preferred_element_type=jnp.float32
    )
    sigmoid_gate = jax.nn.sigmoid(gate_pre)
    both_sides = (sigmoid_gate * value_pre * mask_float).astype(jnp.bfloat16)
    gate_sig = jax.nn.sigmoid(
        jnp.einsum("ijc,cd->ijd", scaled_in, gate_weight, preferred_element_type=jnp.float32)
    )
    sides_chan = lax.all_to_all(both_sides, "row", split_axis=1, concat_axis=2, tiled=True)
    partial_sum = forward_products(sides_chan[0], sides_chan[1])
    product = lax.psum_scatter(partial_sum, "col", scatter_dimension=2, tiled=True).astype(
        jnp.bfloat16
    )
    mixed_pair = lax.all_to_all(product, "row", split_axis=1, concat_axis=0, tiled=True)
    normed_mid, inverse_mid = norm_stats(mixed_pair.astype(jnp.float32), 0)
    scaled_mid = (normed_mid * mid_gain[:, None, None] + mid_bias[:, None, None]).astype(
        jnp.bfloat16
    )
    update = jnp.einsum("hij,hc->ijc", scaled_mid, out_weight, preferred_element_type=jnp.float32)
    output = (gate_sig * update).astype(jnp.bfloat16)
    grad_out = cotangent.astype(jnp.float32)
    grad_update = (grad_out * gate_sig).astype(jnp.bfloat16)
    grad_gate = (grad_out * update * gate_sig * (1.0 - gate_sig)).astype(jnp.bfloat16)
    grad_scaled_mid = jnp.einsum(
        "ijc,hc->hij", grad_update, out_weight, preferred_element_type=jnp.float32
    )
    grad_mixed = norm_back(
        grad_scaled_mid * mid_gain[:, None, None], normed_mid, inverse_mid, 0
    ).astype(jnp.bfloat16)
    grad_chan = lax.all_to_all(grad_mixed, "row", split_axis=0, concat_axis=1, tiled=True)
    grad_full = lax.all_gather(grad_chan, "col", axis=2, tiled=True)
    grad_local = backward_products(grad_full, sides_chan[0], sides_chan[1])
    grad_sides = lax.all_to_all(grad_local, "row", split_axis=2, concat_axis=1, tiled=True)
    side_float = grad_sides.astype(jnp.float32) * mask_float
    grad_value = (side_float * sigmoid_gate).astype(jnp.bfloat16)
    grad_gate_pre = (side_float * value_pre * sigmoid_gate * (1.0 - sigmoid_gate)).astype(
        jnp.bfloat16
    )
    grad_scaled = jnp.einsum(
        "shij,csh->ijc", grad_gate_pre, weights_four[:, :, 0], preferred_element_type=jnp.float32
    )
    grad_scaled = grad_scaled + jnp.einsum(
        "shij,csh->ijc", grad_value, weights_four[:, :, 1], preferred_element_type=jnp.float32
    )
    grad_scaled = grad_scaled + jnp.einsum(
        "ijd,cd->ijc", grad_gate, gate_weight, preferred_element_type=jnp.float32
    )
    grad_pair = norm_back(grad_scaled * in_gain, normed_in, inverse_in, 2).astype(jnp.bfloat16)
    return (output, grad_pair)


def solution(mesh):
    blocks = mesh.shape["row"] == 16 and mesh.shape["col"] == 1
    placed = (
        P(("grp", "row"), "col", None),
        P(("grp", "row"), "col"),
        P(("grp", "row"), "col", None),
        P(),
        P(),
        P(),
        P(),
        P(),
        P(),
        P(),
    )
    return jax.shard_map(
        blocks_device if blocks else channels_device,
        mesh=mesh,
        in_specs=placed,
        out_specs=(P(("grp", "row"), "col", None), P(("grp", "row"), "col", None)),
        check_vma=False,
    )
```

```python
import jax
import jax.numpy as jnp
from jax import lax
from jax.experimental import pallas as pl
from jax.experimental.pallas import tpu as pltpu
from jax.sharding import PartitionSpec as P

EPSILON = 1e-05
CORE, CHIP_X, Z_LOW, Z_HIGH = 1, 2, 4, 8
LEFT_OFFSETS = (0, CORE, Z_LOW, Z_LOW | CORE)
RIGHT_OFFSETS = (0, CHIP_X, Z_HIGH, Z_HIGH | CHIP_X)
ROWS = 8
SIDE = 1024
PIECE = 256
HEAD = PIECE + 16
VMEM_BYTES = 48 * 2**20
WAIT = 5 * 10**9

NT = (((1,), (1,)), ((), ()))
NN = (((1,), (0,)), ((), ()))
TN = (((0,), (0,)), ((), ()))
F32, BF16 = jnp.float32, jnp.bfloat16


def dot(a, b, dims):
    return lax.dot_general(a, b, dims, preferred_element_type=F32)


def norm(values, axis):
    center = values - jnp.mean(values, axis=axis, keepdims=True)
    inverse = lax.rsqrt(jnp.mean(center * center, axis=axis, keepdims=True) + EPSILON)
    return center * inverse, inverse


def sigmoid(x):
    return 0.5 * jnp.tanh(0.5 * x) + 0.5


def call(kernel, outs, smem=(), vmem=(), scratch=(), weight=2**26):
    vmem_spec = pl.BlockSpec(memory_space=pltpu.VMEM)
    specs = [pl.BlockSpec(memory_space=pltpu.SMEM)] * len(smem)
    specs += [vmem_spec] * len(vmem)
    return pl.pallas_call(
        kernel,
        out_shape=[jax.ShapeDtypeStruct(s, d) for s, d in outs],
        in_specs=specs,
        out_specs=[vmem_spec] * len(outs),
        scratch_shapes=list(scratch),
        compiler_params=pltpu.CompilerParams(vmem_limit_bytes=VMEM_BYTES),
        cost_estimate=pl.CostEstimate(flops=weight, bytes_accessed=2**18, transcendentals=0),
    )(*smem, *vmem)


def side_rows(quarter, row):
    return pl.ds(quarter * ROWS + row, 32, stride=4 * ROWS)


def store_side(rows_ref, row, result):
    for q in range(4):
        rows_ref[side_rows(q, row), :] = result[q * 32 : (q + 1) * 32]


def load_side(rows_ref, row):
    return jnp.concatenate([rows_ref[side_rows(q, row), :] for q in range(4)], axis=0)


def columns_of(me, offsets):
    return [pl.multiple_of((me ^ o) * ROWS, ROWS) for o in offsets]


def pick_columns(full_ref, starts):
    columns = [full_ref[:, pl.ds(s, ROWS), :] for s in starts]
    return jnp.concatenate(columns, axis=1).reshape(PIECE, 128)


def pack_kernel(me_ref, cot_ref, mask_ref, after_ref, own_ref, core_ref, far_ref, full_ref):
    me = me_ref[0]
    full_ref[...] = cot_ref[...].astype(F32)
    mask = jnp.concatenate([mask_ref[...].astype(F32), jnp.zeros((ROWS, 128), F32)], axis=0)
    places = [(own_ref, 0), (core_ref, 0), (far_ref, 0), (far_ref, HEAD)]
    for (ref, place), offset in zip(places, LEFT_OFFSETS):
        piece = pick_columns(full_ref, columns_of(me ^ offset, RIGHT_OFFSETS))
        ref[place : place + PIECE, :] = piece.astype(BF16)
        ref[place + PIECE : place + HEAD, :] = mask.astype(BF16)


def rows_of(refs, row):
    part, start = divmod(row * 128, SIDE // len(refs))
    return refs[part][start : start + 128, :].astype(F32)


def scale_in(values, params_ref):
    return norm(values, 1)[0] * params_ref[0:1, :] + params_ref[1:2, :]


def make_side(projected):
    return sigmoid(projected[:128]) * projected[128:]


def block_gate(me_ref, scaled_ref, weight_ref):
    picked = pick_columns(scaled_ref, columns_of(me_ref[0], RIGHT_OFFSETS))
    return sigmoid(dot(picked.astype(BF16), weight_ref[:, 512:640], NN))


def own_kernel(
    me_ref,
    x_ref,
    weight_ref,
    params_ref,
    left_ref,
    right_ref,
    sig_ref,
    weight_t_ref,
    block_ref,
    mid_ref,
    rows_ref,
    scaled_ref,
):
    weight_t_ref[...] = weight_ref[:, :512].astype(F32).T.astype(BF16)
    for row in range(ROWS):
        scaled = scale_in(rows_of([x_ref], row), params_ref)
        scaled_ref[row] = scaled
        projected = dot(weight_t_ref[...], scaled.astype(BF16), NT)
        store_side(rows_ref.at[0], row, make_side(projected[:256]))
        store_side(rows_ref.at[1], row, make_side(projected[256:]))
    left_ref[...] = rows_ref[0].astype(BF16)
    right_ref[...] = rows_ref[1].astype(BF16)
    sig_ref[...] = block_gate(me_ref, scaled_ref, weight_ref)

    repeat = lax.broadcasted_iota(jnp.int32, (512, 128), 0)
    lane = lax.broadcasted_iota(jnp.int32, (512, 128), 1)
    spread = jnp.where((repeat >> 2) == lane, 1.0, 0.0).astype(BF16)
    tall = dot(spread, weight_ref[:, 640:], NN)
    for m in range(4):
        block_ref[:, m * 128 : (m + 1) * 128] = jnp.where((repeat & 3) == m, tall, 0.0).astype(BF16)
    rows = lax.broadcasted_iota(jnp.int32, (ROWS, 128), 0)
    both = jnp.where(rows == 0, params_ref[2:3, :], params_ref[3:4, :])
    wide = jnp.zeros((ROWS, 512), F32)
    for _ in range(3):
        term = both.astype(BF16)
        wide = wide + dot(term, spread, NT)
        both = both - term.astype(F32)
    mid_ref[...] = wide


def peer_kernel(me_ref, left_in, *refs):
    right_in, rest = refs[:-8], refs[-8:]
    weight_t_ref, weight_ref, params_ref, left_ref, right_ref, sig_ref, rows_ref, scaled_ref = rest
    for row in range(ROWS):
        scaled = scale_in(rows_of([left_in], row), params_ref)
        scaled_ref[row] = scaled
        projected = dot(weight_t_ref[:256, :], scaled.astype(BF16), NT)
        store_side(rows_ref.at[0], row, make_side(projected))
        scaled = scale_in(rows_of(right_in, row), params_ref)
        projected = dot(weight_t_ref[256:, :], scaled.astype(BF16), NT)
        store_side(rows_ref.at[1], row, make_side(projected))
    left_ref[...] = rows_ref[0].astype(BF16)
    right_ref[...] = rows_ref[1].astype(BF16)
    sig_ref[...] = block_gate(me_ref, scaled_ref, weight_ref)


def split_sum(values, ones):
    high = values.astype(BF16)
    low = (values - high.astype(F32)).astype(BF16)
    return dot(high, ones, NN) + dot(low, ones, NN)


def block_kernel(*refs):
    me_ref, left_refs, right_refs, sig_refs = refs[0], refs[1:5], refs[5:9], refs[9:13]
    own_ref, core_in, far_in, block_ref, mid_ref = refs[13:18]
    pieces = [(own_ref, 0), (core_in, 0), (far_in, 0), (core_in, HEAD)]
    out_0, out_2, core_ref, left_0, left_2 = refs[18:23]
    outs = [(out_0, 0), (core_ref, SIDE), (out_2, 0), (core_ref, 2 * SIDE + PIECE)]
    lefts = [(left_0, 0), (core_ref, 0), (left_2, 0), (core_ref, SIDE + PIECE)]
    right_outs, pairs_ref = refs[23:29], refs[29]
    me = me_ref[0]
    groups = SIDE // 32
    lane = lax.broadcasted_iota(jnp.int32, (ROWS, 128), 1)
    of_quarter = [((lane >> 3) & 3) == q for q in range(4)]

    masks = [ref[at + PIECE : at + HEAD, :].astype(F32) for ref, at in pieces]
    valid = jnp.max(jnp.concatenate(masks, axis=0), axis=0, keepdims=True)
    src = lax.broadcasted_iota(jnp.int32, (128, 128), 0)
    dst = lax.broadcasted_iota(jnp.int32, (128, 128), 1)
    pick = jnp.zeros((128, 128), F32)
    for n, offset in enumerate(RIGHT_OFFSETS):
        wanted = (me ^ offset) * ROWS + (dst & 7)
        pick = jnp.where((src == wanted) & ((dst >> 5) == n), 1.0, pick)
    spread = jnp.broadcast_to(valid, (ROWS, 128)).astype(BF16)
    column_valid = dot(spread, pick.astype(BF16), NN)
    pair_valid = [jnp.max(k[:ROWS], axis=1, keepdims=True) * column_valid for k in masks]
    valid = jnp.broadcast_to(valid, (128, 128)).astype(BF16)

    def slab(side_refs, g):
        return jnp.concatenate([r[g * 32 : (g + 1) * 32, :] for r in side_refs], axis=0)

    for g in range(groups):
        full = dot(slab(left_refs, g) * valid, slab(right_refs, g), NT).reshape(4, 4, ROWS, 128)
        for m in range(4):
            kept = full[m, 3]
            for q in range(3):
                kept = jnp.where(of_quarter[q], full[m, q], kept)
            pairs_ref[g * 32 + m * ROWS : g * 32 + (m + 1) * ROWS, :] = kept * pair_valid[m]

    turned = []
    for row in range(ROWS):
        turn = pairs_ref[pl.ds(row, 128, stride=ROWS), :].T.reshape(4, 4, ROWS, 128)
        turned.append(jnp.concatenate([turn[:, q].reshape(32, 128) for q in range(4)], axis=1))
    mixed = jnp.concatenate(turned, axis=0).astype(BF16).astype(F32)

    ones = jnp.where((src & 3) == (dst & 3), 1.0, 0.0).astype(BF16)

    def channel_mean(values):
        total = values[:, :128] + values[:, 128:256] + values[:, 256:384] + values[:, 384:]
        mean = split_sum(total, ones) * (1.0 / 128.0)
        return jnp.concatenate([mean] * 4, axis=1)

    mid_gain, mid_bias = mid_ref[0:1, :], mid_ref[1:2, :]
    center = mixed - channel_mean(mixed)
    inverse = lax.rsqrt(channel_mean(center * center) + EPSILON)
    normed = center * inverse
    scaled = (normed * mid_gain + mid_bias).astype(BF16)
    update = dot(scaled, block_ref[...], NN)
    grad_update = []
    for m in range(4):
        sig = sig_refs[m][...]
        out = sig * update[:, m * 128 : (m + 1) * 128]
        ref, at = outs[m]
        ref[at : at + PIECE, :] = out.astype(BF16)
        ref, at = pieces[m]
        cot = ref[at : at + PIECE, :].astype(F32)
        grad_update.append((cot * sig).astype(BF16))
    grad_hat = dot(jnp.concatenate(grad_update, axis=1), block_ref[...], NT) * mid_gain
    first = channel_mean(grad_hat)
    second = channel_mean(grad_hat * normed)
    grad_mixed = inverse * (grad_hat - first - normed * second)

    for row in range(ROWS):
        part = grad_mixed[row * 32 : (row + 1) * 32]
        parts = [part[:, q * 128 : (q + 1) * 128].reshape(4, 1, ROWS, 128) for q in range(4)]
        turn = jnp.concatenate(parts, axis=1).reshape(128, 128)
        pairs_ref[pl.ds(row, 128, stride=ROWS), :] = turn.T

    def right_out(n, g):
        if n < 2:
            return right_outs[n], g * 32
        half = groups // 2
        return right_outs[2 * n - 2 + g // half], (g % half) * 32

    for g in range(groups):
        rows = []
        for m in range(4):
            part = pairs_ref[g * 32 + m * ROWS : g * 32 + (m + 1) * ROWS, :] * pair_valid[m]
            rows += [jnp.where(of_quarter[q], part, 0.0) for q in range(4)]
        spread = jnp.concatenate(rows, axis=0).astype(BF16)
        grad_right = dot(spread, slab(left_refs, g), TN).astype(BF16)
        grad_left = dot(spread, slab(right_refs, g), NN).astype(BF16)
        for m in range(4):
            ref, at = lefts[m]
            at += g * 32
            ref[at : at + 32, :] = grad_left[m * 32 : (m + 1) * 32]
            ref, at = right_out(m, g)
            ref[at : at + 32, :] = grad_right[m * 32 : (m + 1) * 32]


def pass_kernel(message_ref, *refs):
    refs[-1][...] = message_ref[...]


def join_kernel(mine_ref, got_ref, both_ref):
    both_ref[:HEAD, :] = mine_ref[...]
    both_ref[HEAD:, :] = got_ref[HEAD:, :]


def add_kernel(mine_ref, got_ref, *refs):
    sum_ref = refs[-1]
    sum_ref[...] = (mine_ref[...].astype(F32) + got_ref[...].astype(F32)).astype(BF16)


def add_left_kernel(mine_ref, piece_ref, got_ref, sum_ref, out_ref):
    at = SIDE + PIECE
    sum_ref[...] = (mine_ref[...].astype(F32) + got_ref[at : at + SIDE, :].astype(F32)).astype(BF16)
    out_ref[:PIECE, :] = piece_ref[...]
    out_ref[PIECE:, :] = got_ref[at + SIDE :, :]


def factor_kernel(
    x_ref,
    cot_ref,
    mask_ref,
    weight_ref,
    params_ref,
    weight_t_ref,
    factor_ref,
    normed_ref,
    inverse_ref,
    open_ref,
    gain_t_ref,
):
    gain_t = jnp.broadcast_to(params_ref[0:1, :], (128, 128)).T
    bias_t = jnp.broadcast_to(params_ref[1:2, :], (128, 128)).T
    gain_t_ref[...] = gain_t
    for row in range(ROWS):
        x = rows_of([x_ref], row)
        normed, inverse = norm(x.T, 0)
        normed_ref[row] = normed
        inverse_ref[row : row + 1, :] = inverse
        scaled = (normed * gain_t + bias_t).astype(BF16)
        projected = dot(weight_t_ref[...], scaled, NN)
        keep = mask_ref[row : row + 1].astype(F32)
        for side in range(2):
            base = 256 * side
            gate = sigmoid(projected[base : base + 128])
            value = projected[base + 128 : base + 256]
            factor_ref[row, base : base + 128, :] = keep * value * gate * (1.0 - gate)
            factor_ref[row, base + 128 : base + 256, :] = keep * gate
        scaled = scale_in(x, params_ref).astype(BF16)
        gate_sig = sigmoid(dot(scaled, weight_ref[:, 512:640], NN))
        open_ref[row] = cot_ref[row].astype(F32) * (1.0 - gate_sig)


def out_kernel(me_ref, own_ref, near_ref, far_ref, open_ref, weight_ref, out_ref, grad_ref, full_ref):
    places = [(own_ref, 0), (near_ref, SIDE), (far_ref, 0), (far_ref, PIECE)]
    for (ref, at), offset in zip(places, LEFT_OFFSETS):
        piece = ref[at : at + PIECE, :].astype(F32).reshape(ROWS, 4, ROWS, 128)
        for n, start in enumerate(columns_of(me_ref[0] ^ offset, RIGHT_OFFSETS)):
            full_ref[:, pl.ds(start, ROWS), :] = piece[:, n]
    for row in range(ROWS):
        out = full_ref[row]
        out_ref[row] = out.astype(BF16)
        grad_gate = (open_ref[row] * out).astype(BF16)
        grad_ref[row] = dot(weight_ref[:, 512:640], grad_gate, NT)


def pair_kernel(*refs):
    left_refs, right_refs = refs[0:3], refs[3:7]
    factor_ref, normed_ref, inverse_ref, gain_t_ref, gate_ref, weight_ref = refs[7:13]
    out_ref, rows_ref = refs[13:]
    half = SIDE // 2
    left = [r[:SIDE, :].astype(F32) for r in left_refs]
    rows_ref[0] = left[0] + left[1] + left[2]
    for part in range(2):
        at = slice(part * half, (part + 1) * half)
        right = right_refs[0][at, :].astype(F32) + right_refs[1][at, :].astype(F32)
        rows_ref[1, at, :] = right + right_refs[2 + part][...].astype(F32)
    for row in range(ROWS):
        parts = []
        for side in range(2):
            grad = load_side(rows_ref.at[side], row)
            for place in (256 * side, 256 * side + 128):
                parts.append((grad * factor_ref[row, place : place + 128, :]).astype(BF16))
        grad_scaled = dot(weight_ref[:, :512], jnp.concatenate(parts, axis=0), NN) + gate_ref[row]
        normed = normed_ref[row]
        grad_hat = grad_scaled * gain_t_ref[...]
        first = jnp.mean(grad_hat, axis=0, keepdims=True)
        second = jnp.mean(grad_hat * normed, axis=0, keepdims=True)
        grad = inverse_ref[row : row + 1, :] * (grad_hat - first - normed * second)
        out_ref[row] = grad.T.astype(BF16)


def swap(values, offset):
    return lax.ppermute(values, "row", [(s, s ^ offset) for s in range(16)])


def blocks_device(
    pair_rep,
    pair_mask,
    cotangent,
    in_gain,
    in_bias,
    proj_weight,
    gate_weight,
    mid_gain,
    mid_bias,
    out_weight,
):
    me = lax.axis_index("row").astype(jnp.int32).reshape(1)
    half = SIDE // 2
    cube = (ROWS, 128, 128)
    side, piece = ((SIDE, 128), BF16), ((PIECE, 128), BF16)
    halves, core = ((half, 128), BF16), ((2 * (SIDE + PIECE), 128), BF16)
    sig = ((PIECE, 128), F32)
    rows_scratch = pltpu.VMEM((2, SIDE, 128), F32)
    cube_scratch = pltpu.VMEM(cube, F32)

    flat = pair_rep.reshape(SIDE, 128)
    weights = jnp.concatenate([proj_weight, gate_weight, out_weight], axis=1)
    params = jnp.stack([in_gain, in_bias, mid_gain, mid_bias])

    far = swap(flat, Z_LOW)
    x_near = swap(flat, CHIP_X)
    near = swap(flat, CORE)
    z_first, z_second = swap(flat[:half], Z_HIGH), swap(flat[half:], Z_HIGH)
    left_0, right_0, sig_0, weight_t, block_weight, mid = call(
        own_kernel,
        [side, side, sig, ((512, 128), BF16), ((512, 512), BF16), ((ROWS, 512), F32)],
        smem=[me],
        vmem=[flat, weights, params],
        scratch=[rows_scratch, cube_scratch],
        weight=WAIT,
    )

    def peer(*messages):
        return call(
            peer_kernel,
            [side, side, sig],
            smem=[me],
            vmem=[*messages, weight_t, weights, params],
            scratch=[rows_scratch, cube_scratch],
            weight=WAIT,
        )

    def after(message, *others):
        return call(pass_kernel, [(message.shape, BF16)], vmem=[message, *others])[0]

    left_1, right_1, sig_1 = peer(near, x_near)
    own_piece, core_piece, far_piece = call(
        pack_kernel,
        [((HEAD, 128), BF16), ((HEAD, 128), BF16), ((2 * HEAD, 128), BF16)],
        smem=[me],
        vmem=[cotangent, pair_mask, sig_1],
        scratch=[cube_scratch],
    )
    far_got = swap(far_piece, Z_LOW)
    both = swap(far, CORE)
    x_first = swap(after(z_first, sig_1, core_piece), CHIP_X)
    x_second = swap(after(z_second, sig_1, core_piece), CHIP_X)
    (joined,) = call(join_kernel, [((2 * HEAD, 128), BF16)], vmem=[core_piece, far_got])
    core_pieces = swap(joined, CORE)
    left_2, right_2, sig_2 = peer(far, z_first, z_second)
    left_3, right_3, sig_3 = peer(both, x_first, x_second)

    out_0, out_2, core_back, grad_left_0, grad_left_2, *grad_right = call(
        block_kernel,
        [piece, piece, core, side, side, side, side] + [halves] * 4,
        smem=[me],
        vmem=[left_0, left_1, left_2, left_3]
        + [right_0, right_1, right_2, right_3]
        + [sig_0, sig_1, sig_2, sig_3]
        + [own_piece, core_pieces, far_got, block_weight, mid],
        scratch=[pltpu.VMEM((SIDE, 128), F32)],
    )
    core_got = swap(core_back, CORE)
    x_got = [swap(grad_right[4], CHIP_X), swap(grad_right[5], CHIP_X)]
    left_sum, out_far = call(
        add_left_kernel,
        [side, ((2 * PIECE, 128), BF16)],
        vmem=[grad_left_2, out_2, core_got],
    )
    left_got = swap(left_sum, Z_LOW)
    out_far = swap(out_far, Z_LOW)
    totals = []
    for mine, got in zip(grad_right[2:4], x_got):
        totals += call(add_kernel, [halves], vmem=[mine, got, left_sum])
    z_got = [swap(total, Z_HIGH) for total in totals]
    right_near = swap(after(grad_right[1], *totals), CHIP_X)

    factors, normed, inverse, open_part, gain_t = call(
        factor_kernel,
        [((ROWS, 512, 128), F32), (cube, F32), ((ROWS, 128), F32), (cube, F32), ((128, 128), F32)],
        vmem=[flat, cotangent, pair_mask, weights, params, weight_t],
        weight=WAIT,
    )
    output, gate_part = call(
        out_kernel,
        [(cube, BF16), (cube, F32)],
        smem=[me],
        vmem=[out_0, core_got, out_far, open_part, weights],
        scratch=[cube_scratch],
    )
    (grad_pair,) = call(
        pair_kernel,
        [(cube, BF16)],
        vmem=[grad_left_0, core_got, left_got, grad_right[0], right_near, *z_got]
        + [factors, normed, inverse, gain_t, gate_part, weights],
        scratch=[rows_scratch],
    )
    return (output, grad_pair)


def norm_stats(values, reduce_axis):
    center = values - jnp.mean(values, axis=reduce_axis, keepdims=True)
    inverse = lax.rsqrt(jnp.mean(center * center, axis=reduce_axis, keepdims=True) + EPSILON)
    return (center * inverse, inverse)


def norm_back(grad_hat, normed, inverse, reduce_axis):
    first = jnp.mean(grad_hat, axis=reduce_axis, keepdims=True)
    second = jnp.mean(grad_hat * normed, axis=reduce_axis, keepdims=True)
    return inverse * (grad_hat - first - normed * second)


def forward_products(left_chan, right_chan):
    return jnp.einsum("hik,hjk->hij", left_chan, right_chan, preferred_element_type=jnp.float32)


def backward_products(grad_full, left_chan, right_chan):
    grad_left = jnp.einsum(
        "hij,hjk->hik", grad_full, right_chan, preferred_element_type=jnp.float32
    )
    grad_right = jnp.einsum(
        "hij,hik->hjk", grad_full, left_chan, preferred_element_type=jnp.float32
    )
    return jnp.stack([grad_left, grad_right]).astype(jnp.bfloat16)


def channels_device(
    pair_rep,
    pair_mask,
    cotangent,
    in_gain,
    in_bias,
    proj_weight,
    gate_weight,
    mid_gain,
    mid_bias,
    out_weight,
):
    width = pair_rep.shape[2]
    hidden = out_weight.shape[0]
    weights_four = proj_weight.reshape(width, 2, 2, hidden)
    mask_float = pair_mask.astype(jnp.float32)
    normed_in, inverse_in = norm_stats(pair_rep.astype(jnp.float32), 2)
    scaled_in = (normed_in * in_gain + in_bias).astype(jnp.bfloat16)
    gate_pre = jnp.einsum(
        "ijc,csh->shij", scaled_in, weights_four[:, :, 0], preferred_element_type=jnp.float32
    )
    value_pre = jnp.einsum(
        "ijc,csh->shij", scaled_in, weights_four[:, :, 1], preferred_element_type=jnp.float32
    )
    sigmoid_gate = jax.nn.sigmoid(gate_pre)
    both_sides = (sigmoid_gate * value_pre * mask_float).astype(jnp.bfloat16)
    gate_sig = jax.nn.sigmoid(
        jnp.einsum("ijc,cd->ijd", scaled_in, gate_weight, preferred_element_type=jnp.float32)
    )
    sides_chan = lax.all_to_all(both_sides, "row", split_axis=1, concat_axis=2, tiled=True)
    partial_sum = forward_products(sides_chan[0], sides_chan[1])
    product = lax.psum_scatter(partial_sum, "col", scatter_dimension=2, tiled=True).astype(
        jnp.bfloat16
    )
    mixed_pair = lax.all_to_all(product, "row", split_axis=1, concat_axis=0, tiled=True)
    normed_mid, inverse_mid = norm_stats(mixed_pair.astype(jnp.float32), 0)
    scaled_mid = (normed_mid * mid_gain[:, None, None] + mid_bias[:, None, None]).astype(
        jnp.bfloat16
    )
    update = jnp.einsum("hij,hc->ijc", scaled_mid, out_weight, preferred_element_type=jnp.float32)
    output = (gate_sig * update).astype(jnp.bfloat16)
    grad_out = cotangent.astype(jnp.float32)
    grad_update = (grad_out * gate_sig).astype(jnp.bfloat16)
    grad_gate = (grad_out * update * gate_sig * (1.0 - gate_sig)).astype(jnp.bfloat16)
    grad_scaled_mid = jnp.einsum(
        "ijc,hc->hij", grad_update, out_weight, preferred_element_type=jnp.float32
    )
    grad_mixed = norm_back(
        grad_scaled_mid * mid_gain[:, None, None], normed_mid, inverse_mid, 0
    ).astype(jnp.bfloat16)
    grad_chan = lax.all_to_all(grad_mixed, "row", split_axis=0, concat_axis=1, tiled=True)
    grad_full = lax.all_gather(grad_chan, "col", axis=2, tiled=True)
    grad_local = backward_products(grad_full, sides_chan[0], sides_chan[1])
    grad_sides = lax.all_to_all(grad_local, "row", split_axis=2, concat_axis=1, tiled=True)
    side_float = grad_sides.astype(jnp.float32) * mask_float
    grad_value = (side_float * sigmoid_gate).astype(jnp.bfloat16)
    grad_gate_pre = (side_float * value_pre * sigmoid_gate * (1.0 - sigmoid_gate)).astype(
        jnp.bfloat16
    )
    grad_scaled = jnp.einsum(
        "shij,csh->ijc", grad_gate_pre, weights_four[:, :, 0], preferred_element_type=jnp.float32
    )
    grad_scaled = grad_scaled + jnp.einsum(
        "shij,csh->ijc", grad_value, weights_four[:, :, 1], preferred_element_type=jnp.float32
    )
    grad_scaled = grad_scaled + jnp.einsum(
        "ijd,cd->ijc", grad_gate, gate_weight, preferred_element_type=jnp.float32
    )
    grad_pair = norm_back(grad_scaled * in_gain, normed_in, inverse_in, 2).astype(jnp.bfloat16)
    return (output, grad_pair)


def solution(mesh):
    blocks = mesh.shape["row"] == 16 and mesh.shape["col"] == 1
    placed = (
        P(("grp", "row"), "col", None),
        P(("grp", "row"), "col"),
        P(("grp", "row"), "col", None),
        P(),
        P(),
        P(),
        P(),
        P(),
        P(),
        P(),
    )
    return jax.shard_map(
        blocks_device if blocks else channels_device,
        mesh=mesh,
        in_specs=placed,
        out_specs=(P(("grp", "row"), "col", None), P(("grp", "row"), "col", None)),
        check_vma=False,
    )
```

```python
import jax
import jax.numpy as jnp
from jax import lax
from jax.experimental import pallas as pl
from jax.experimental.pallas import tpu as pltpu
from jax.sharding import PartitionSpec as P

EPSILON = 1e-05
CORE, CHIP_X, Z_LOW, Z_HIGH = 1, 2, 4, 8
LEFT_OFFSETS = (0, CORE, Z_LOW, Z_LOW | CORE)
RIGHT_OFFSETS = (0, CHIP_X, Z_HIGH, Z_HIGH | CHIP_X)
ROWS = 8
SIDE = 1024
PIECE = 256
HEAD = PIECE + 16
VMEM_BYTES = 48 * 2**20
WAIT = 5 * 10**9

NT = (((1,), (1,)), ((), ()))
NN = (((1,), (0,)), ((), ()))
TN = (((0,), (0,)), ((), ()))
F32, BF16 = jnp.float32, jnp.bfloat16


def dot(a, b, dims):
    return lax.dot_general(a, b, dims, preferred_element_type=F32)


def norm(values, axis):
    center = values - jnp.mean(values, axis=axis, keepdims=True)
    inverse = lax.rsqrt(jnp.mean(center * center, axis=axis, keepdims=True) + EPSILON)
    return center * inverse, inverse


def sigmoid(x):
    return 0.5 * jnp.tanh(0.5 * x) + 0.5


def call(kernel, outs, smem=(), vmem=(), scratch=(), weight=2**26):
    vmem_spec = pl.BlockSpec(memory_space=pltpu.VMEM)
    specs = [pl.BlockSpec(memory_space=pltpu.SMEM)] * len(smem)
    specs += [vmem_spec] * len(vmem)
    return pl.pallas_call(
        kernel,
        out_shape=[jax.ShapeDtypeStruct(s, d) for s, d in outs],
        in_specs=specs,
        out_specs=[vmem_spec] * len(outs),
        scratch_shapes=list(scratch),
        compiler_params=pltpu.CompilerParams(vmem_limit_bytes=VMEM_BYTES),
        cost_estimate=pl.CostEstimate(flops=weight, bytes_accessed=2**18, transcendentals=0),
    )(*smem, *vmem)


def side_rows(quarter, row):
    return pl.ds(quarter * ROWS + row, 32, stride=4 * ROWS)


def store_side(rows_ref, row, result):
    for q in range(4):
        rows_ref[side_rows(q, row), :] = result[q * 32 : (q + 1) * 32]


def load_side(rows_ref, row):
    return jnp.concatenate([rows_ref[side_rows(q, row), :] for q in range(4)], axis=0)


def columns_of(me, offsets):
    return [pl.multiple_of((me ^ o) * ROWS, ROWS) for o in offsets]


def pick_columns(full_ref, starts):
    columns = [full_ref[:, pl.ds(s, ROWS), :] for s in starts]
    return jnp.concatenate(columns, axis=1).reshape(PIECE, 128)


def pack_kernel(me_ref, cot_ref, mask_ref, after_ref, own_ref, core_ref, far_ref, full_ref):
    me = me_ref[0]
    full_ref[...] = cot_ref[...].astype(F32)
    mask = jnp.concatenate([mask_ref[...].astype(F32), jnp.zeros((ROWS, 128), F32)], axis=0)
    places = [(own_ref, 0), (core_ref, 0), (far_ref, 0), (far_ref, HEAD)]
    for (ref, place), offset in zip(places, LEFT_OFFSETS):
        piece = pick_columns(full_ref, columns_of(me ^ offset, RIGHT_OFFSETS))
        ref[place : place + PIECE, :] = piece.astype(BF16)
        ref[place + PIECE : place + HEAD, :] = mask.astype(BF16)


def rows_of(refs, row):
    part, start = divmod(row * 128, SIDE // len(refs))
    return refs[part][start : start + 128, :].astype(F32)


def scale_in(values, params_ref):
    return norm(values, 1)[0] * params_ref[0:1, :] + params_ref[1:2, :]


def make_side(projected):
    return sigmoid(projected[:128]) * projected[128:]


def block_gate(me_ref, scaled_ref, weight_ref):
    picked = pick_columns(scaled_ref, columns_of(me_ref[0], RIGHT_OFFSETS))
    return sigmoid(dot(picked.astype(BF16), weight_ref[:, 512:640], NN))


def own_kernel(
    me_ref,
    x_ref,
    weight_ref,
    params_ref,
    left_ref,
    right_ref,
    sig_ref,
    weight_t_ref,
    block_ref,
    mid_ref,
    rows_ref,
    scaled_ref,
):
    weight_t_ref[...] = weight_ref[:, :512].astype(F32).T.astype(BF16)
    for row in range(ROWS):
        scaled = scale_in(rows_of([x_ref], row), params_ref)
        scaled_ref[row] = scaled
        projected = dot(weight_t_ref[...], scaled.astype(BF16), NT)
        store_side(rows_ref.at[0], row, make_side(projected[:256]))
        store_side(rows_ref.at[1], row, make_side(projected[256:]))
    left_ref[...] = rows_ref[0].astype(BF16)
    right_ref[...] = rows_ref[1].astype(BF16)
    sig_ref[...] = block_gate(me_ref, scaled_ref, weight_ref)

    repeat = lax.broadcasted_iota(jnp.int32, (512, 128), 0)
    lane = lax.broadcasted_iota(jnp.int32, (512, 128), 1)
    spread = jnp.where((repeat >> 2) == lane, 1.0, 0.0).astype(BF16)
    tall = dot(spread, weight_ref[:, 640:], NN)
    for m in range(4):
        block_ref[:, m * 128 : (m + 1) * 128] = jnp.where((repeat & 3) == m, tall, 0.0).astype(BF16)
    rows = lax.broadcasted_iota(jnp.int32, (ROWS, 128), 0)
    both = jnp.where(rows == 0, params_ref[2:3, :], params_ref[3:4, :])
    wide = jnp.zeros((ROWS, 512), F32)
    for _ in range(3):
        term = both.astype(BF16)
        wide = wide + dot(term, spread, NT)
        both = both - term.astype(F32)
    mid_ref[...] = wide


def peer_kernel(me_ref, left_in, *refs):
    right_in, rest = refs[:-8], refs[-8:]
    weight_t_ref, weight_ref, params_ref, left_ref, right_ref, sig_ref, rows_ref, scaled_ref = rest
    for row in range(ROWS):
        scaled = scale_in(rows_of([left_in], row), params_ref)
        scaled_ref[row] = scaled
        projected = dot(weight_t_ref[:256, :], scaled.astype(BF16), NT)
        store_side(rows_ref.at[0], row, make_side(projected))
        scaled = scale_in(rows_of(right_in, row), params_ref)
        projected = dot(weight_t_ref[256:, :], scaled.astype(BF16), NT)
        store_side(rows_ref.at[1], row, make_side(projected))
    left_ref[...] = rows_ref[0].astype(BF16)
    right_ref[...] = rows_ref[1].astype(BF16)
    sig_ref[...] = block_gate(me_ref, scaled_ref, weight_ref)


def left_kernel(
    me_ref, x_ref, weight_t_ref, weight_ref, params_ref, left_ref, sig_ref, rows_ref, scaled_ref
):
    for row in range(ROWS):
        scaled = scale_in(rows_of([x_ref], row), params_ref)
        scaled_ref[row] = scaled
        store_side(rows_ref, row, make_side(dot(weight_t_ref[:256, :], scaled.astype(BF16), NT)))
    left_ref[...] = rows_ref[...].astype(BF16)
    sig_ref[...] = block_gate(me_ref, scaled_ref, weight_ref)


def right_kernel(first, last):
    def kernel(x_ref, weight_t_ref, params_ref, rest_ref, right_ref, rows_ref):
        if last:
            rows_ref[...] = rest_ref[...]
        else:
            rows_ref[...] = jnp.zeros_like(rows_ref)
        for row in range(ROWS // 2):
            scaled = scale_in(x_ref[row * 128 : (row + 1) * 128, :].astype(F32), params_ref)
            projected = dot(weight_t_ref[256:, :], scaled.astype(BF16), NT)
            store_side(rows_ref, first + row, make_side(projected))
        right_ref[...] = rows_ref[...].astype(right_ref.dtype)

    return kernel


def split_sum(values, ones):
    high = values.astype(BF16)
    low = (values - high.astype(F32)).astype(BF16)
    return dot(high, ones, NN) + dot(low, ones, NN)


GROUPS = SIDE // 32


def quarters():
    lane = lax.broadcasted_iota(jnp.int32, (ROWS, 128), 1)
    return [((lane >> 3) & 3) == q for q in range(4)]


def slab(side_refs, g):
    return jnp.concatenate([r[g * 32 : (g + 1) * 32, :] for r in side_refs], axis=0)


def block_kernel(*refs):
    me_ref, left_refs, right_refs, sig_refs = refs[0], refs[1:5], refs[5:9], refs[9:13]
    own_ref, core_in, far_in, block_ref, mid_ref = refs[13:18]
    pieces = [(own_ref, 0), (core_in, 0), (far_in, 0), (core_in, HEAD)]
    out_refs, pairs_ref = refs[18:22], refs[22]
    me = me_ref[0]
    of_quarter = quarters()

    masks = [ref[at + PIECE : at + HEAD, :].astype(F32) for ref, at in pieces]
    valid = jnp.max(jnp.concatenate(masks, axis=0), axis=0, keepdims=True)
    src = lax.broadcasted_iota(jnp.int32, (128, 128), 0)
    dst = lax.broadcasted_iota(jnp.int32, (128, 128), 1)
    pick = jnp.zeros((128, 128), F32)
    for n, offset in enumerate(RIGHT_OFFSETS):
        wanted = (me ^ offset) * ROWS + (dst & 7)
        pick = jnp.where((src == wanted) & ((dst >> 5) == n), 1.0, pick)
    spread = jnp.broadcast_to(valid, (ROWS, 128)).astype(BF16)
    column_valid = dot(spread, pick.astype(BF16), NN)
    pair_valid = [jnp.max(k[:ROWS], axis=1, keepdims=True) * column_valid for k in masks]
    valid = jnp.broadcast_to(valid, (128, 128)).astype(BF16)

    for g in range(GROUPS):
        full = dot(slab(left_refs, g) * valid, slab(right_refs, g), NT).reshape(4, 4, ROWS, 128)
        for m in range(4):
            kept = full[m, 3]
            for q in range(3):
                kept = jnp.where(of_quarter[q], full[m, q], kept)
            pairs_ref[g * 32 + m * ROWS : g * 32 + (m + 1) * ROWS, :] = kept * pair_valid[m]

    turned = []
    for row in range(ROWS):
        turn = pairs_ref[pl.ds(row, 128, stride=ROWS), :].T.reshape(4, 4, ROWS, 128)
        turned.append(jnp.concatenate([turn[:, q].reshape(32, 128) for q in range(4)], axis=1))
    mixed = jnp.concatenate(turned, axis=0).astype(BF16).astype(F32)

    ones = jnp.where((src & 3) == (dst & 3), 1.0, 0.0).astype(BF16)

    def channel_mean(values):
        total = values[:, :128] + values[:, 128:256] + values[:, 256:384] + values[:, 384:]
        mean = split_sum(total, ones) * (1.0 / 128.0)
        return jnp.concatenate([mean] * 4, axis=1)

    mid_gain, mid_bias = mid_ref[0:1, :], mid_ref[1:2, :]
    center = mixed - channel_mean(mixed)
    inverse = lax.rsqrt(channel_mean(center * center) + EPSILON)
    normed = center * inverse
    scaled = (normed * mid_gain + mid_bias).astype(BF16)
    update = dot(scaled, block_ref[...], NN)
    grad_update = []
    for m in range(4):
        sig = sig_refs[m][...]
        out = sig * update[:, m * 128 : (m + 1) * 128]
        out_refs[m][...] = out.astype(BF16)
        ref, at = pieces[m]
        cot = ref[at : at + PIECE, :].astype(F32)
        grad_update.append((cot * sig).astype(BF16))
    grad_hat = dot(jnp.concatenate(grad_update, axis=1), block_ref[...], NT) * mid_gain
    first = channel_mean(grad_hat)
    second = channel_mean(grad_hat * normed)
    grad_mixed = inverse * (grad_hat - first - normed * second)

    mask = jnp.concatenate(pair_valid, axis=0)
    for row in range(ROWS):
        part = grad_mixed[row * 32 : (row + 1) * 32]
        parts = [part[:, q * 128 : (q + 1) * 128].reshape(4, 1, ROWS, 128) for q in range(4)]
        turn = jnp.concatenate(parts, axis=1).reshape(128, 128)
        pairs_ref[pl.ds(row, 128, stride=ROWS), :] = turn.T
    for g in range(GROUPS):
        pairs_ref[g * 32 : (g + 1) * 32, :] = pairs_ref[g * 32 : (g + 1) * 32, :] * mask


def spread_group(pairs_ref, g, of_quarter):
    rows = []
    for m in range(4):
        part = pairs_ref[g * 32 + m * ROWS : g * 32 + (m + 1) * ROWS, :]
        rows += [jnp.where(of_quarter[q], part, 0.0) for q in range(4)]
    return jnp.concatenate(rows, axis=0).astype(BF16)


def grad_right_kernel(half):
    def kernel(pairs_ref, *refs):
        left_refs, out_refs = refs[:4], refs[4:]
        of_quarter = quarters()
        for g in range(GROUPS // 2):
            spread = spread_group(pairs_ref, half * GROUPS // 2 + g, of_quarter)
            grad = dot(spread, slab(left_refs, half * GROUPS // 2 + g), TN).astype(BF16)
            for n in range(4):
                out_refs[n][g * 32 : (g + 1) * 32, :] = grad[n * 32 : (n + 1) * 32]

    return kernel


def grad_left_kernel(pairs_ref, *refs):
    right_refs, (out_near, out_both), (left_0, core_ref, left_2) = refs[:4], refs[4:6], refs[7:]
    lefts = [(left_0, 0), (core_ref, 0), (left_2, 0), (core_ref, SIDE + PIECE)]
    of_quarter = quarters()
    for g in range(GROUPS):
        spread = spread_group(pairs_ref, g, of_quarter)
        grad = dot(spread, slab(right_refs, g), NN).astype(BF16)
        for m, (ref, at) in enumerate(lefts):
            ref[at + g * 32 : at + (g + 1) * 32, :] = grad[m * 32 : (m + 1) * 32]
    core_ref[SIDE : SIDE + PIECE, :] = out_near[...]
    core_ref[2 * SIDE + PIECE :, :] = out_both[...]


def halves_kernel(x_ref, first_ref, second_ref):
    first_ref[...] = x_ref[: SIDE // 2, :]
    second_ref[...] = x_ref[SIDE // 2 :, :]


def pass_kernel(message_ref, *refs):
    refs[-1][...] = message_ref[...]


def join_kernel(mine_ref, got_ref, both_ref):
    both_ref[:HEAD, :] = mine_ref[...]
    both_ref[HEAD:, :] = got_ref[HEAD:, :]


def add_kernel(mine_ref, got_ref, *refs):
    sum_ref = refs[-1]
    sum_ref[...] = (mine_ref[...].astype(F32) + got_ref[...].astype(F32)).astype(BF16)


def near_kernel(first_ref, second_ref, after_ref, both_ref):
    both_ref[: SIDE // 2, :] = first_ref[...]
    both_ref[SIDE // 2 :, :] = second_ref[...]


def add_left_kernel(mine_ref, piece_ref, got_ref, sum_ref, out_ref):
    at = SIDE + PIECE
    sum_ref[...] = (mine_ref[...].astype(F32) + got_ref[at : at + SIDE, :].astype(F32)).astype(BF16)
    out_ref[:PIECE, :] = piece_ref[...]
    out_ref[PIECE:, :] = got_ref[at + SIDE :, :]


def factor_kernel(
    x_ref,
    cot_ref,
    mask_ref,
    weight_ref,
    params_ref,
    weight_t_ref,
    factor_ref,
    normed_ref,
    inverse_ref,
    open_ref,
    gain_t_ref,
):
    gain_t = jnp.broadcast_to(params_ref[0:1, :], (128, 128)).T
    bias_t = jnp.broadcast_to(params_ref[1:2, :], (128, 128)).T
    gain_t_ref[...] = gain_t
    for row in range(ROWS):
        x = rows_of([x_ref], row)
        normed, inverse = norm(x.T, 0)
        normed_ref[row] = normed
        inverse_ref[row : row + 1, :] = inverse
        scaled = (normed * gain_t + bias_t).astype(BF16)
        projected = dot(weight_t_ref[...], scaled, NN)
        keep = mask_ref[row : row + 1].astype(F32)
        for side in range(2):
            base = 256 * side
            gate = sigmoid(projected[base : base + 128])
            value = projected[base + 128 : base + 256]
            factor_ref[row, base : base + 128, :] = keep * value * gate * (1.0 - gate)
            factor_ref[row, base + 128 : base + 256, :] = keep * gate
        scaled = scale_in(x, params_ref).astype(BF16)
        gate_sig = sigmoid(dot(scaled, weight_ref[:, 512:640], NN))
        open_ref[row] = cot_ref[row].astype(F32) * (1.0 - gate_sig)


def out_kernel(me_ref, own_ref, near_ref, far_ref, open_ref, weight_ref, out_ref, grad_ref, full_ref):
    places = [(own_ref, 0), (near_ref, SIDE), (far_ref, 0), (far_ref, PIECE)]
    for (ref, at), offset in zip(places, LEFT_OFFSETS):
        piece = ref[at : at + PIECE, :].astype(F32).reshape(ROWS, 4, ROWS, 128)
        for n, start in enumerate(columns_of(me_ref[0] ^ offset, RIGHT_OFFSETS)):
            full_ref[:, pl.ds(start, ROWS), :] = piece[:, n]
    for row in range(ROWS):
        out = full_ref[row]
        out_ref[row] = out.astype(BF16)
        grad_gate = (open_ref[row] * out).astype(BF16)
        grad_ref[row] = dot(weight_ref[:, 512:640], grad_gate, NT)


def right_terms(rows_ref, factor_ref, row, half):
    parts = []
    nothing = jnp.zeros((16, 128), BF16)
    for place in (256, 384):
        for q in range(4):
            grad = rows_ref[pl.ds(q * ROWS + row, 16, stride=4 * ROWS), :]
            at = place + q * 32 + half * 16
            term = (grad * factor_ref[row, at : at + 16, :]).astype(BF16)
            parts += [nothing, term] if half else [term, nothing]
    return jnp.concatenate(parts, axis=0)


def partial_kernel(*refs):
    left_refs, (own_ref, near_ref, got_ref) = refs[0:3], refs[3:6]
    factor_ref, gate_ref, weight_ref, sum_ref, left_rows, right_rows = refs[6:]
    left = [r[:SIDE, :].astype(F32) for r in left_refs]
    left_rows[...] = left[0] + left[1] + left[2]
    right = own_ref[...].astype(F32) + near_ref[: SIDE // 2, :].astype(F32)
    right_rows[...] = right + got_ref[...].astype(F32)
    for row in range(ROWS):
        grad = load_side(left_rows, row)
        parts = [(grad * factor_ref[row, a : a + 128, :]).astype(BF16) for a in (0, 128)]
        parts.append(right_terms(right_rows, factor_ref, row, 0))
        grad_projected = jnp.concatenate(parts, axis=0)
        sum_ref[row] = dot(weight_ref[:, :512], grad_projected, NN) + gate_ref[row]


def pair_kernel(
    own_ref,
    near_ref,
    got_ref,
    factor_ref,
    sum_ref,
    normed_ref,
    inverse_ref,
    gain_t_ref,
    weight_ref,
    out_ref,
    right_rows,
):
    right = own_ref[...].astype(F32) + near_ref[SIDE // 2 :, :].astype(F32)
    right_rows[...] = right + got_ref[...].astype(F32)
    for row in range(ROWS):
        terms = right_terms(right_rows, factor_ref, row, 1)
        grad_scaled = dot(weight_ref[:, 256:512], terms, NN) + sum_ref[row]
        normed = normed_ref[row]
        grad_hat = grad_scaled * gain_t_ref[...]
        first = jnp.mean(grad_hat, axis=0, keepdims=True)
        second = jnp.mean(grad_hat * normed, axis=0, keepdims=True)
        grad = inverse_ref[row : row + 1, :] * (grad_hat - first - normed * second)
        out_ref[row] = grad.T.astype(BF16)


def swap(values, offset):
    return lax.ppermute(values, "row", [(s, s ^ offset) for s in range(16)])


def blocks_device(
    pair_rep,
    pair_mask,
    cotangent,
    in_gain,
    in_bias,
    proj_weight,
    gate_weight,
    mid_gain,
    mid_bias,
    out_weight,
):
    me = lax.axis_index("row").astype(jnp.int32).reshape(1)
    half = SIDE // 2
    cube = (ROWS, 128, 128)
    side, piece = ((SIDE, 128), BF16), ((PIECE, 128), BF16)
    halves, core = ((half, 128), BF16), ((2 * (SIDE + PIECE), 128), BF16)
    sig = ((PIECE, 128), F32)
    rows_scratch = pltpu.VMEM((2, SIDE, 128), F32)
    cube_scratch = pltpu.VMEM(cube, F32)

    def after(message, *others):
        return call(pass_kernel, [(message.shape, BF16)], vmem=[message, *others])[0]

    flat = pair_rep.reshape(SIDE, 128)
    weights = jnp.concatenate([proj_weight, gate_weight, out_weight], axis=1)
    params = jnp.stack([in_gain, in_bias, mid_gain, mid_bias])

    first, second = call(halves_kernel, [halves] * 2, vmem=[flat])
    z_first, z_second = swap(first, Z_HIGH), swap(second, Z_HIGH)
    whole = after(flat, second)
    far = swap(whole, Z_LOW)
    x_near = swap(whole, CHIP_X)
    near = swap(whole, CORE)
    left_0, right_0, sig_0, weight_t, block_weight, mid = call(
        own_kernel,
        [side, side, sig, ((512, 128), BF16), ((512, 512), BF16), ((ROWS, 512), F32)],
        smem=[me],
        vmem=[flat, weights, params],
        scratch=[rows_scratch, cube_scratch],
        weight=WAIT,
    )

    def peer(*messages):
        return call(
            peer_kernel,
            [side, side, sig],
            smem=[me],
            vmem=[*messages, weight_t, weights, params],
            scratch=[rows_scratch, cube_scratch],
            weight=WAIT,
        )

    left_1, right_1, sig_1 = peer(near, x_near)
    own_piece, core_piece, far_piece = call(
        pack_kernel,
        [((HEAD, 128), BF16), ((HEAD, 128), BF16), ((2 * HEAD, 128), BF16)],
        smem=[me],
        vmem=[cotangent, pair_mask, x_near],
        scratch=[cube_scratch],
    )
    far_got = swap(far_piece, Z_LOW)
    both = swap(far, CORE)
    x_second = swap(z_second, CHIP_X)
    x_first = swap(after(z_first, x_second, left_0), CHIP_X)
    (joined,) = call(join_kernel, [((2 * HEAD, 128), BF16)], vmem=[core_piece, far_got])
    core_pieces = swap(joined, CORE)
    left_2, right_2, sig_2 = peer(far, z_first, z_second)
    left_3, sig_3 = call(
        left_kernel,
        [side, sig],
        smem=[me],
        vmem=[both, weight_t, weights, params],
        scratch=[pltpu.VMEM((SIDE, 128), F32), cube_scratch],
        weight=WAIT,
    )

    def right_half(first, last, *operands):
        return call(
            right_kernel(first, last),
            [((SIDE, 128), BF16 if last else F32)],
            vmem=operands,
            scratch=[pltpu.VMEM((SIDE, 128), F32)],
            weight=WAIT // 4,
        )[0]

    right_part = right_half(ROWS // 2, False, x_second, weight_t, params, left_3)
    right_3 = right_half(0, True, x_first, weight_t, params, right_part)

    lefts, rights = [left_0, left_1, left_2, left_3], [right_0, right_1, right_2, right_3]
    out_0, out_1, out_2, out_3, pairs = call(
        block_kernel,
        [piece] * 4 + [((SIDE, 128), F32)],
        smem=[me],
        vmem=lefts
        + rights
        + [sig_0, sig_1, sig_2, sig_3]
        + [own_piece, core_pieces, far_got, block_weight, mid],
    )
    right_a = call(grad_right_kernel(0), [halves] * 4, vmem=[pairs, *lefts])
    x_got = [swap(right_a[3], CHIP_X)]
    grad_left_0, core_back, grad_left_2 = call(
        grad_left_kernel,
        [side, core, side],
        vmem=[pairs, *rights, out_1, out_3, right_a[3]],
    )
    core_got = swap(core_back, CORE)
    right_b = call(grad_right_kernel(1), [halves] * 4, vmem=[pairs, *lefts])
    x_got.append(swap(after(right_b[3], x_got[0]), CHIP_X))
    left_sum, out_far = call(
        add_left_kernel,
        [side, ((2 * PIECE, 128), BF16)],
        vmem=[grad_left_2, out_2, core_got],
    )
    left_got = swap(left_sum, Z_LOW)
    out_far = swap(out_far, Z_LOW)
    (total,) = call(add_kernel, [halves], vmem=[right_a[2], x_got[0]])
    z_got = [swap(total, Z_HIGH)]
    (total,) = call(add_kernel, [halves], vmem=[right_b[2], x_got[1], left_sum])
    z_got.append(swap(total, Z_HIGH))
    (near_back,) = call(near_kernel, [side], vmem=[right_a[1], right_b[1], total])
    right_near = swap(near_back, CHIP_X)

    factors, normed, inverse, open_part, gain_t = call(
        factor_kernel,
        [((ROWS, 512, 128), F32), (cube, F32), ((ROWS, 128), F32), (cube, F32), ((128, 128), F32)],
        vmem=[flat, cotangent, pair_mask, weights, params, weight_t],
        weight=WAIT,
    )
    output, gate_part = call(
        out_kernel,
        [(cube, BF16), (cube, F32)],
        smem=[me],
        vmem=[out_0, core_got, out_far, open_part, weights],
        scratch=[cube_scratch],
    )
    half_scratch = pltpu.VMEM((half, 128), F32)
    (partial,) = call(
        partial_kernel,
        [(cube, F32)],
        vmem=[grad_left_0, core_got, left_got, right_a[0], right_near, z_got[0]]
        + [factors, gate_part, weights],
        scratch=[pltpu.VMEM((SIDE, 128), F32), half_scratch],
        weight=WAIT // 4,
    )
    (grad_pair,) = call(
        pair_kernel,
        [(cube, BF16)],
        vmem=[right_b[0], right_near, z_got[1]]
        + [factors, partial, normed, inverse, gain_t, weights],
        scratch=[half_scratch],
    )
    return (output, grad_pair)


def norm_stats(values, reduce_axis):
    center = values - jnp.mean(values, axis=reduce_axis, keepdims=True)
    inverse = lax.rsqrt(jnp.mean(center * center, axis=reduce_axis, keepdims=True) + EPSILON)
    return (center * inverse, inverse)


def norm_back(grad_hat, normed, inverse, reduce_axis):
    first = jnp.mean(grad_hat, axis=reduce_axis, keepdims=True)
    second = jnp.mean(grad_hat * normed, axis=reduce_axis, keepdims=True)
    return inverse * (grad_hat - first - normed * second)


def forward_products(left_chan, right_chan):
    return jnp.einsum("hik,hjk->hij", left_chan, right_chan, preferred_element_type=jnp.float32)


def backward_products(grad_full, left_chan, right_chan):
    grad_left = jnp.einsum(
        "hij,hjk->hik", grad_full, right_chan, preferred_element_type=jnp.float32
    )
    grad_right = jnp.einsum(
        "hij,hik->hjk", grad_full, left_chan, preferred_element_type=jnp.float32
    )
    return jnp.stack([grad_left, grad_right]).astype(jnp.bfloat16)


def channels_device(
    pair_rep,
    pair_mask,
    cotangent,
    in_gain,
    in_bias,
    proj_weight,
    gate_weight,
    mid_gain,
    mid_bias,
    out_weight,
):
    width = pair_rep.shape[2]
    hidden = out_weight.shape[0]
    weights_four = proj_weight.reshape(width, 2, 2, hidden)
    mask_float = pair_mask.astype(jnp.float32)
    normed_in, inverse_in = norm_stats(pair_rep.astype(jnp.float32), 2)
    scaled_in = (normed_in * in_gain + in_bias).astype(jnp.bfloat16)
    gate_pre = jnp.einsum(
        "ijc,csh->shij", scaled_in, weights_four[:, :, 0], preferred_element_type=jnp.float32
    )
    value_pre = jnp.einsum(
        "ijc,csh->shij", scaled_in, weights_four[:, :, 1], preferred_element_type=jnp.float32
    )
    sigmoid_gate = jax.nn.sigmoid(gate_pre)
    both_sides = (sigmoid_gate * value_pre * mask_float).astype(jnp.bfloat16)
    gate_sig = jax.nn.sigmoid(
        jnp.einsum("ijc,cd->ijd", scaled_in, gate_weight, preferred_element_type=jnp.float32)
    )
    sides_chan = lax.all_to_all(both_sides, "row", split_axis=1, concat_axis=2, tiled=True)
    partial_sum = forward_products(sides_chan[0], sides_chan[1])
    product = lax.psum_scatter(partial_sum, "col", scatter_dimension=2, tiled=True).astype(
        jnp.bfloat16
    )
    mixed_pair = lax.all_to_all(product, "row", split_axis=1, concat_axis=0, tiled=True)
    normed_mid, inverse_mid = norm_stats(mixed_pair.astype(jnp.float32), 0)
    scaled_mid = (normed_mid * mid_gain[:, None, None] + mid_bias[:, None, None]).astype(
        jnp.bfloat16
    )
    update = jnp.einsum("hij,hc->ijc", scaled_mid, out_weight, preferred_element_type=jnp.float32)
    output = (gate_sig * update).astype(jnp.bfloat16)
    grad_out = cotangent.astype(jnp.float32)
    grad_update = (grad_out * gate_sig).astype(jnp.bfloat16)
    grad_gate = (grad_out * update * gate_sig * (1.0 - gate_sig)).astype(jnp.bfloat16)
    grad_scaled_mid = jnp.einsum(
        "ijc,hc->hij", grad_update, out_weight, preferred_element_type=jnp.float32
    )
    grad_mixed = norm_back(
        grad_scaled_mid * mid_gain[:, None, None], normed_mid, inverse_mid, 0
    ).astype(jnp.bfloat16)
    grad_chan = lax.all_to_all(grad_mixed, "row", split_axis=0, concat_axis=1, tiled=True)
    grad_full = lax.all_gather(grad_chan, "col", axis=2, tiled=True)
    grad_local = backward_products(grad_full, sides_chan[0], sides_chan[1])
    grad_sides = lax.all_to_all(grad_local, "row", split_axis=2, concat_axis=1, tiled=True)
    side_float = grad_sides.astype(jnp.float32) * mask_float
    grad_value = (side_float * sigmoid_gate).astype(jnp.bfloat16)
    grad_gate_pre = (side_float * value_pre * sigmoid_gate * (1.0 - sigmoid_gate)).astype(
        jnp.bfloat16
    )
    grad_scaled = jnp.einsum(
        "shij,csh->ijc", grad_gate_pre, weights_four[:, :, 0], preferred_element_type=jnp.float32
    )
    grad_scaled = grad_scaled + jnp.einsum(
        "shij,csh->ijc", grad_value, weights_four[:, :, 1], preferred_element_type=jnp.float32
    )
    grad_scaled = grad_scaled + jnp.einsum(
        "ijd,cd->ijc", grad_gate, gate_weight, preferred_element_type=jnp.float32
    )
    grad_pair = norm_back(grad_scaled * in_gain, normed_in, inverse_in, 2).astype(jnp.bfloat16)
    return (output, grad_pair)


def solution(mesh):
    blocks = mesh.shape["row"] == 16 and mesh.shape["col"] == 1
    placed = (
        P(("grp", "row"), "col", None),
        P(("grp", "row"), "col"),
        P(("grp", "row"), "col", None),
        P(),
        P(),
        P(),
        P(),
        P(),
        P(),
        P(),
    )
    return jax.shard_map(
        blocks_device if blocks else channels_device,
        mesh=mesh,
        in_specs=placed,
        out_specs=(P(("grp", "row"), "col", None), P(("grp", "row"), "col", None)),
        check_vma=False,
    )
```

```python
import jax
import jax.numpy as jnp
from jax import lax
from jax.experimental import pallas as pl
from jax.experimental.pallas import tpu as pltpu
from jax.sharding import PartitionSpec as P

EPSILON = 1e-05
CORE, CHIP_X, Z_LOW, Z_HIGH = 1, 2, 4, 8
LEFT_OFFSETS = (0, CORE, Z_LOW, Z_LOW | CORE)
RIGHT_OFFSETS = (0, CHIP_X, Z_HIGH, Z_HIGH | CHIP_X)
ROWS = 8
SIDE = 1024
PIECE = 256
HEAD = PIECE + 16
VMEM_BYTES = 48 * 2**20
WAIT = 5 * 10**9

NT = (((1,), (1,)), ((), ()))
NN = (((1,), (0,)), ((), ()))
TN = (((0,), (0,)), ((), ()))
F32, BF16 = jnp.float32, jnp.bfloat16


def dot(a, b, dims):
    return lax.dot_general(a, b, dims, preferred_element_type=F32)


def norm(values, axis):
    center = values - jnp.mean(values, axis=axis, keepdims=True)
    inverse = lax.rsqrt(jnp.mean(center * center, axis=axis, keepdims=True) + EPSILON)
    return center * inverse, inverse


def sigmoid(x):
    return 0.5 * jnp.tanh(0.5 * x) + 0.5


def call(kernel, outs, smem=(), vmem=(), scratch=(), weight=2**26):
    vmem_spec = pl.BlockSpec(memory_space=pltpu.VMEM)
    specs = [pl.BlockSpec(memory_space=pltpu.SMEM)] * len(smem)
    specs += [vmem_spec] * len(vmem)
    return pl.pallas_call(
        kernel,
        out_shape=[jax.ShapeDtypeStruct(s, d) for s, d in outs],
        in_specs=specs,
        out_specs=[vmem_spec] * len(outs),
        scratch_shapes=list(scratch),
        compiler_params=pltpu.CompilerParams(vmem_limit_bytes=VMEM_BYTES),
        cost_estimate=pl.CostEstimate(flops=weight, bytes_accessed=2**18, transcendentals=0),
    )(*smem, *vmem)


def side_rows(quarter, row):
    return pl.ds(quarter * ROWS + row, 32, stride=4 * ROWS)


def store_side(rows_ref, row, result):
    for q in range(4):
        rows_ref[side_rows(q, row), :] = result[q * 32 : (q + 1) * 32]


def load_side(rows_ref, row):
    return jnp.concatenate([rows_ref[side_rows(q, row), :] for q in range(4)], axis=0)


def columns_of(me, offsets):
    return [pl.multiple_of((me ^ o) * ROWS, ROWS) for o in offsets]


def pick_columns(full_ref, starts):
    columns = [full_ref[:, pl.ds(s, ROWS), :] for s in starts]
    return jnp.concatenate(columns, axis=1).reshape(PIECE, 128)


def pack_kernel(me_ref, cot_ref, mask_ref, after_ref, own_ref, core_ref, far_ref, full_ref):
    me = me_ref[0]
    full_ref[...] = cot_ref[...].astype(F32)
    mask = jnp.concatenate([mask_ref[...].astype(F32), jnp.zeros((ROWS, 128), F32)], axis=0)
    places = [(own_ref, 0), (core_ref, 0), (far_ref, 0), (far_ref, HEAD)]
    for (ref, place), offset in zip(places, LEFT_OFFSETS):
        piece = pick_columns(full_ref, columns_of(me ^ offset, RIGHT_OFFSETS))
        ref[place : place + PIECE, :] = piece.astype(BF16)
        ref[place + PIECE : place + HEAD, :] = mask.astype(BF16)


def split_sum(values, ones):
    high = values.astype(BF16)
    low = (values - high.astype(F32)).astype(BF16)
    return dot(high, ones, NN) + dot(low, ones, NN)


def scale_in(x, params_ref):
    ones = jnp.ones((128, 128), BF16)
    center = x.astype(F32) - dot(x, ones, NN) * (1.0 / 128.0)
    inverse = lax.rsqrt(split_sum(center * center, ones) * (1.0 / 128.0) + EPSILON)
    return center * inverse * params_ref[0:1, :] + params_ref[1:2, :]


def block_of(values, row):
    return values[row * 128 : (row + 1) * 128]


def make_side(projected):
    return sigmoid(projected[:128]) * projected[128:]


def block_gate(me_ref, scaled_ref, weight_ref):
    picked = pick_columns(scaled_ref, columns_of(me_ref[0], RIGHT_OFFSETS))
    return sigmoid(dot(picked.astype(BF16), weight_ref[:, 512:640], NN))


def own_kernel(
    me_ref,
    x_ref,
    weight_ref,
    params_ref,
    left_ref,
    right_ref,
    sig_ref,
    weight_t_ref,
    block_ref,
    mid_ref,
    rows_ref,
    scaled_ref,
):
    weight_t_ref[...] = weight_ref[:, :512].astype(F32).T.astype(BF16)
    scaled = scale_in(x_ref[...], params_ref)
    scaled_ref[...] = scaled.reshape(scaled_ref.shape)
    scaled = scaled.astype(BF16)
    for row in range(ROWS):
        projected = dot(weight_t_ref[...], block_of(scaled, row), NT)
        store_side(rows_ref.at[0], row, make_side(projected[:256]))
        store_side(rows_ref.at[1], row, make_side(projected[256:]))
    left_ref[...] = rows_ref[0].astype(BF16)
    right_ref[...] = rows_ref[1].astype(BF16)
    sig_ref[...] = block_gate(me_ref, scaled_ref, weight_ref)

    repeat = lax.broadcasted_iota(jnp.int32, (512, 128), 0)
    lane = lax.broadcasted_iota(jnp.int32, (512, 128), 1)
    spread = jnp.where((repeat >> 2) == lane, 1.0, 0.0).astype(BF16)
    tall = dot(spread, weight_ref[:, 640:], NN)
    for m in range(4):
        block_ref[:, m * 128 : (m + 1) * 128] = jnp.where((repeat & 3) == m, tall, 0.0).astype(BF16)
    rows = lax.broadcasted_iota(jnp.int32, (ROWS, 128), 0)
    both = jnp.where(rows == 0, params_ref[2:3, :], params_ref[3:4, :])
    wide = jnp.zeros((ROWS, 512), F32)
    for _ in range(3):
        term = both.astype(BF16)
        wide = wide + dot(term, spread, NT)
        both = both - term.astype(F32)
    mid_ref[...] = wide


def peer_kernel(me_ref, left_in, *refs):
    right_in, rest = refs[:-8], refs[-8:]
    weight_t_ref, weight_ref, params_ref, left_ref, right_ref, sig_ref, rows_ref, scaled_ref = rest
    scaled = scale_in(left_in[...], params_ref)
    scaled_ref[...] = scaled.reshape(scaled_ref.shape)
    scaled = scaled.astype(BF16)
    for row in range(ROWS):
        projected = dot(weight_t_ref[:256, :], block_of(scaled, row), NT)
        store_side(rows_ref.at[0], row, make_side(projected))
    scaled = [scale_in(r[...], params_ref).astype(BF16) for r in right_in]
    for row in range(ROWS):
        part, place = divmod(row, ROWS // len(right_in))
        projected = dot(weight_t_ref[256:, :], block_of(scaled[part], place), NT)
        store_side(rows_ref.at[1], row, make_side(projected))
    left_ref[...] = rows_ref[0].astype(BF16)
    right_ref[...] = rows_ref[1].astype(BF16)
    sig_ref[...] = block_gate(me_ref, scaled_ref, weight_ref)


def left_kernel(
    me_ref, x_ref, weight_t_ref, weight_ref, params_ref, left_ref, sig_ref, rows_ref, scaled_ref
):
    scaled = scale_in(x_ref[...], params_ref)
    scaled_ref[...] = scaled.reshape(scaled_ref.shape)
    scaled = scaled.astype(BF16)
    for row in range(ROWS):
        projected = dot(weight_t_ref[:256, :], block_of(scaled, row), NT)
        store_side(rows_ref, row, make_side(projected))
    left_ref[...] = rows_ref[...].astype(BF16)
    sig_ref[...] = block_gate(me_ref, scaled_ref, weight_ref)


def right_kernel(first, last):
    def kernel(x_ref, weight_t_ref, params_ref, rest_ref, right_ref, rows_ref):
        if last:
            rows_ref[...] = rest_ref[...]
        else:
            rows_ref[...] = jnp.zeros_like(rows_ref)
        scaled = scale_in(x_ref[...], params_ref).astype(BF16)
        for row in range(ROWS // 2):
            projected = dot(weight_t_ref[256:, :], block_of(scaled, row), NT)
            store_side(rows_ref, first + row, make_side(projected))
        right_ref[...] = rows_ref[...].astype(right_ref.dtype)

    return kernel


GROUPS = SIDE // 32


def quarters():
    lane = lax.broadcasted_iota(jnp.int32, (ROWS, 128), 1)
    return [((lane >> 3) & 3) == q for q in range(4)]


def slab(side_refs, g):
    return jnp.concatenate([r[g * 32 : (g + 1) * 32, :] for r in side_refs], axis=0)


def block_kernel(*refs):
    me_ref, left_refs, right_refs, sig_refs = refs[0], refs[1:5], refs[5:9], refs[9:13]
    own_ref, core_in, far_in, block_ref, mid_ref = refs[13:18]
    pieces = [(own_ref, 0), (core_in, 0), (far_in, 0), (core_in, HEAD)]
    out_refs, pairs_ref = refs[18:22], refs[22]
    me = me_ref[0]
    of_quarter = quarters()

    masks = [ref[at + PIECE : at + HEAD, :].astype(F32) for ref, at in pieces]
    valid = jnp.max(jnp.concatenate(masks, axis=0), axis=0, keepdims=True)
    src = lax.broadcasted_iota(jnp.int32, (128, 128), 0)
    dst = lax.broadcasted_iota(jnp.int32, (128, 128), 1)
    pick = jnp.zeros((128, 128), F32)
    for n, offset in enumerate(RIGHT_OFFSETS):
        wanted = (me ^ offset) * ROWS + (dst & 7)
        pick = jnp.where((src == wanted) & ((dst >> 5) == n), 1.0, pick)
    spread = jnp.broadcast_to(valid, (ROWS, 128)).astype(BF16)
    column_valid = dot(spread, pick.astype(BF16), NN)
    pair_valid = [jnp.max(k[:ROWS], axis=1, keepdims=True) * column_valid for k in masks]
    valid = jnp.broadcast_to(valid, (128, 128)).astype(BF16)

    for g in range(GROUPS):
        full = dot(slab(left_refs, g) * valid, slab(right_refs, g), NT).reshape(4, 4, ROWS, 128)
        for m in range(4):
            kept = full[m, 3]
            for q in range(3):
                kept = jnp.where(of_quarter[q], full[m, q], kept)
            pairs_ref[g * 32 + m * ROWS : g * 32 + (m + 1) * ROWS, :] = kept * pair_valid[m]

    turned = []
    for row in range(ROWS):
        turn = pairs_ref[pl.ds(row, 128, stride=ROWS), :].T.reshape(4, 4, ROWS, 128)
        turned.append(jnp.concatenate([turn[:, q].reshape(32, 128) for q in range(4)], axis=1))
    mixed = jnp.concatenate(turned, axis=0).astype(BF16).astype(F32)

    ones = jnp.where((src & 3) == (dst & 3), 1.0, 0.0).astype(BF16)

    def channel_mean(values):
        total = values[:, :128] + values[:, 128:256] + values[:, 256:384] + values[:, 384:]
        mean = split_sum(total, ones) * (1.0 / 128.0)
        return jnp.concatenate([mean] * 4, axis=1)

    mid_gain, mid_bias = mid_ref[0:1, :], mid_ref[1:2, :]
    center = mixed - channel_mean(mixed)
    inverse = lax.rsqrt(channel_mean(center * center) + EPSILON)
    normed = center * inverse
    scaled = (normed * mid_gain + mid_bias).astype(BF16)
    update = dot(scaled, block_ref[...], NN)
    grad_update = []
    for m in range(4):
        sig = sig_refs[m][...]
        out = sig * update[:, m * 128 : (m + 1) * 128]
        out_refs[m][...] = out.astype(BF16)
        ref, at = pieces[m]
        cot = ref[at : at + PIECE, :].astype(F32)
        grad_update.append((cot * sig).astype(BF16))
    grad_hat = dot(jnp.concatenate(grad_update, axis=1), block_ref[...], NT) * mid_gain
    first = channel_mean(grad_hat)
    second = channel_mean(grad_hat * normed)
    grad_mixed = inverse * (grad_hat - first - normed * second)

    mask = jnp.concatenate(pair_valid, axis=0)
    for row in range(ROWS):
        part = grad_mixed[row * 32 : (row + 1) * 32]
        parts = [part[:, q * 128 : (q + 1) * 128].reshape(4, 1, ROWS, 128) for q in range(4)]
        turn = jnp.concatenate(parts, axis=1).reshape(128, 128)
        pairs_ref[pl.ds(row, 128, stride=ROWS), :] = turn.T
    for g in range(GROUPS):
        pairs_ref[g * 32 : (g + 1) * 32, :] = pairs_ref[g * 32 : (g + 1) * 32, :] * mask


def spread_group(pairs_ref, g, of_quarter):
    rows = []
    for m in range(4):
        part = pairs_ref[g * 32 + m * ROWS : g * 32 + (m + 1) * ROWS, :]
        rows += [jnp.where(of_quarter[q], part, 0.0) for q in range(4)]
    return jnp.concatenate(rows, axis=0).astype(BF16)


def grad_right_kernel(half):
    def kernel(pairs_ref, *refs):
        left_refs, out_refs = refs[:4], refs[4:]
        of_quarter = quarters()
        for g in range(GROUPS // 2):
            spread = spread_group(pairs_ref, half * GROUPS // 2 + g, of_quarter)
            grad = dot(spread, slab(left_refs, half * GROUPS // 2 + g), TN).astype(BF16)
            for n in range(4):
                out_refs[n][g * 32 : (g + 1) * 32, :] = grad[n * 32 : (n + 1) * 32]

    return kernel


def grad_left_kernel(pairs_ref, *refs):
    right_refs, (out_near, out_both), lefts = refs[:4], refs[4:6], refs[7:]
    of_quarter = quarters()
    for g in range(GROUPS):
        spread = spread_group(pairs_ref, g, of_quarter)
        grad = dot(spread, slab(right_refs, g), NN).astype(BF16)
        for m, ref in enumerate(lefts):
            ref[g * 32 : (g + 1) * 32, :] = grad[m * 32 : (m + 1) * 32]
    lefts[1][SIDE:, :] = out_near[...]
    lefts[3][SIDE:, :] = out_both[...]


def halves_kernel(x_ref, first_ref, second_ref):
    first_ref[...] = x_ref[: SIDE // 2, :]
    second_ref[...] = x_ref[SIDE // 2 :, :]


def pass_kernel(message_ref, *refs):
    refs[-1][...] = message_ref[...]


def join_kernel(mine_ref, got_ref, both_ref):
    both_ref[:HEAD, :] = mine_ref[...]
    both_ref[HEAD:, :] = got_ref[HEAD:, :]


def add_kernel(mine_ref, got_ref, *refs):
    sum_ref = refs[-1]
    sum_ref[...] = (mine_ref[...].astype(F32) + got_ref[...].astype(F32)).astype(BF16)


def near_kernel(first_ref, second_ref, after_ref, both_ref):
    both_ref[: SIDE // 2, :] = first_ref[...]
    both_ref[SIDE // 2 :, :] = second_ref[...]


def add_left_kernel(mine_ref, piece_ref, got_ref, sum_ref, out_ref):
    sum_ref[...] = (mine_ref[...].astype(F32) + got_ref[:SIDE, :].astype(F32)).astype(BF16)
    out_ref[:PIECE, :] = piece_ref[...]
    out_ref[PIECE:, :] = got_ref[SIDE:, :]


def factor_kernel(
    x_ref,
    cot_ref,
    mask_ref,
    weight_ref,
    params_ref,
    weight_t_ref,
    factor_ref,
    normed_ref,
    inverse_ref,
    open_ref,
    gain_t_ref,
):
    gain_t = jnp.broadcast_to(params_ref[0:1, :], (128, 128)).T
    bias_t = jnp.broadcast_to(params_ref[1:2, :], (128, 128)).T
    gain_t_ref[...] = gain_t
    for row in range(ROWS):
        x = x_ref[row * 128 : (row + 1) * 128, :]
        normed, inverse = norm(x.astype(F32).T, 0)
        normed_ref[row] = normed
        inverse_ref[row : row + 1, :] = inverse
        scaled = (normed * gain_t + bias_t).astype(BF16)
        projected = dot(weight_t_ref[...], scaled, NN)
        keep = mask_ref[row : row + 1].astype(F32)
        for side in range(2):
            base = 256 * side
            gate = sigmoid(projected[base : base + 128])
            value = projected[base + 128 : base + 256]
            factor_ref[row, base : base + 128, :] = keep * value * gate * (1.0 - gate)
            factor_ref[row, base + 128 : base + 256, :] = keep * gate
        scaled = scale_in(x, params_ref).astype(BF16)
        gate_sig = sigmoid(dot(scaled, weight_ref[:, 512:640], NN))
        open_ref[row] = cot_ref[row].astype(F32) * (1.0 - gate_sig)


def out_kernel(me_ref, own_ref, near_ref, far_ref, open_ref, weight_ref, out_ref, grad_ref, full_ref):
    places = [(own_ref, 0), (near_ref, SIDE), (far_ref, 0), (far_ref, PIECE)]
    for (ref, at), offset in zip(places, LEFT_OFFSETS):
        piece = ref[at : at + PIECE, :].astype(F32).reshape(ROWS, 4, ROWS, 128)
        for n, start in enumerate(columns_of(me_ref[0] ^ offset, RIGHT_OFFSETS)):
            full_ref[:, pl.ds(start, ROWS), :] = piece[:, n]
    for row in range(ROWS):
        out = full_ref[row]
        out_ref[row] = out.astype(BF16)
        grad_gate = (open_ref[row] * out).astype(BF16)
        grad_ref[row] = dot(weight_ref[:, 512:640], grad_gate, NT)


def right_terms(rows_ref, factor_ref, row, half):
    parts = []
    nothing = jnp.zeros((16, 128), BF16)
    for place in (256, 384):
        for q in range(4):
            grad = rows_ref[pl.ds(q * ROWS + row, 16, stride=4 * ROWS), :]
            at = place + q * 32 + half * 16
            term = (grad * factor_ref[row, at : at + 16, :]).astype(BF16)
            parts += [nothing, term] if half else [term, nothing]
    return jnp.concatenate(parts, axis=0)


def partial_kernel(*refs):
    left_refs, (own_ref, near_ref, got_ref) = refs[0:3], refs[3:6]
    factor_ref, gate_ref, weight_ref, sum_ref, left_rows, right_rows = refs[6:]
    left = [r[:SIDE, :].astype(F32) for r in left_refs]
    left_rows[...] = left[0] + left[1] + left[2]
    right = own_ref[...].astype(F32) + near_ref[: SIDE // 2, :].astype(F32)
    right_rows[...] = right + got_ref[...].astype(F32)
    for row in range(ROWS):
        grad = load_side(left_rows, row)
        parts = [(grad * factor_ref[row, a : a + 128, :]).astype(BF16) for a in (0, 128)]
        parts.append(right_terms(right_rows, factor_ref, row, 0))
        grad_projected = jnp.concatenate(parts, axis=0)
        sum_ref[row] = dot(weight_ref[:, :512], grad_projected, NN) + gate_ref[row]


def pair_kernel(
    own_ref,
    near_ref,
    got_ref,
    factor_ref,
    sum_ref,
    normed_ref,
    inverse_ref,
    gain_t_ref,
    weight_ref,
    out_ref,
    right_rows,
):
    right = own_ref[...].astype(F32) + near_ref[SIDE // 2 :, :].astype(F32)
    right_rows[...] = right + got_ref[...].astype(F32)
    for row in range(ROWS):
        terms = right_terms(right_rows, factor_ref, row, 1)
        grad_scaled = dot(weight_ref[:, 256:512], terms, NN) + sum_ref[row]
        normed = normed_ref[row]
        grad_hat = grad_scaled * gain_t_ref[...]
        first = jnp.mean(grad_hat, axis=0, keepdims=True)
        second = jnp.mean(grad_hat * normed, axis=0, keepdims=True)
        grad = inverse_ref[row : row + 1, :] * (grad_hat - first - normed * second)
        out_ref[row] = grad.T.astype(BF16)


def swap(values, offset):
    return lax.ppermute(values, "row", [(s, s ^ offset) for s in range(16)])


def blocks_device(
    pair_rep,
    pair_mask,
    cotangent,
    in_gain,
    in_bias,
    proj_weight,
    gate_weight,
    mid_gain,
    mid_bias,
    out_weight,
):
    me = lax.axis_index("row").astype(jnp.int32).reshape(1)
    half = SIDE // 2
    cube = (ROWS, 128, 128)
    side, piece = ((SIDE, 128), BF16), ((PIECE, 128), BF16)
    halves, core = ((half, 128), BF16), ((SIDE + PIECE, 128), BF16)
    sig = ((PIECE, 128), F32)
    rows_scratch = pltpu.VMEM((2, SIDE, 128), F32)
    cube_scratch = pltpu.VMEM(cube, F32)

    def after(message, *others):
        return call(pass_kernel, [(message.shape, BF16)], vmem=[message, *others])[0]

    flat = pair_rep.reshape(SIDE, 128)
    weights = jnp.concatenate([proj_weight, gate_weight, out_weight], axis=1)
    params = jnp.stack([in_gain, in_bias, mid_gain, mid_bias])

    first, second = call(halves_kernel, [halves] * 2, vmem=[flat])
    z_first, z_second = swap(first, Z_HIGH), swap(second, Z_HIGH)
    whole = after(flat, second)
    far = swap(whole, Z_LOW)
    x_near = swap(whole, CHIP_X)
    near = swap(whole, CORE)
    left_0, right_0, sig_0, weight_t, block_weight, mid = call(
        own_kernel,
        [side, side, sig, ((512, 128), BF16), ((512, 512), BF16), ((ROWS, 512), F32)],
        smem=[me],
        vmem=[flat, weights, params],
        scratch=[rows_scratch, cube_scratch],
        weight=WAIT,
    )

    def peer(*messages):
        return call(
            peer_kernel,
            [side, side, sig],
            smem=[me],
            vmem=[*messages, weight_t, weights, params],
            scratch=[rows_scratch, cube_scratch],
            weight=WAIT,
        )

    left_1, right_1, sig_1 = peer(near, x_near)
    own_piece, core_piece, far_piece = call(
        pack_kernel,
        [((HEAD, 128), BF16), ((HEAD, 128), BF16), ((2 * HEAD, 128), BF16)],
        smem=[me],
        vmem=[cotangent, pair_mask, x_near],
        scratch=[cube_scratch],
    )
    far_got = swap(far_piece, Z_LOW)
    both = swap(far, CORE)
    x_second = swap(z_second, CHIP_X)
    x_first = swap(after(z_first, x_second, left_0), CHIP_X)
    (joined,) = call(join_kernel, [((2 * HEAD, 128), BF16)], vmem=[core_piece, far_got])
    core_pieces = swap(joined, CORE)
    left_2, right_2, sig_2 = peer(far, z_first, z_second)
    left_3, sig_3 = call(
        left_kernel,
        [side, sig],
        smem=[me],
        vmem=[both, weight_t, weights, params],
        scratch=[pltpu.VMEM((SIDE, 128), F32), cube_scratch],
        weight=WAIT,
    )

    def right_half(first, last, *operands):
        return call(
            right_kernel(first, last),
            [((SIDE, 128), BF16 if last else F32)],
            vmem=operands,
            scratch=[pltpu.VMEM((SIDE, 128), F32)],
            weight=WAIT // 4,
        )[0]

    right_part = right_half(ROWS // 2, False, x_second, weight_t, params, left_3)
    right_3 = right_half(0, True, x_first, weight_t, params, right_part)

    lefts, rights = [left_0, left_1, left_2, left_3], [right_0, right_1, right_2, right_3]
    out_0, out_1, out_2, out_3, pairs = call(
        block_kernel,
        [piece] * 4 + [((SIDE, 128), F32)],
        smem=[me],
        vmem=lefts
        + rights
        + [sig_0, sig_1, sig_2, sig_3]
        + [own_piece, core_pieces, far_got, block_weight, mid],
    )
    right_a = call(grad_right_kernel(0), [halves] * 4, vmem=[pairs, *lefts])
    x_got = [swap(right_a[3], CHIP_X)]
    grad_left_0, near_back, grad_left_2, both_back = call(
        grad_left_kernel,
        [side, core, side, core],
        vmem=[pairs, *rights, out_1, out_3, right_a[3]],
    )
    both_got = swap(both_back, CORE)
    right_b = call(grad_right_kernel(1), [halves] * 4, vmem=[pairs, *lefts])
    left_sum, out_far = call(
        add_left_kernel,
        [side, ((2 * PIECE, 128), BF16)],
        vmem=[grad_left_2, out_2, both_got],
    )
    x_got.append(swap(after(right_b[3], left_sum), CHIP_X))
    left_got = swap(left_sum, Z_LOW)
    out_far = swap(out_far, Z_LOW)
    (total,) = call(add_kernel, [halves], vmem=[right_a[2], x_got[0], left_sum])
    z_got = [swap(total, Z_HIGH)]
    (total,) = call(add_kernel, [halves], vmem=[right_b[2], x_got[1], left_sum])
    z_got.append(swap(total, Z_HIGH))
    (right_back,) = call(near_kernel, [side], vmem=[right_a[1], right_b[1], total])
    right_near = swap(right_back, CHIP_X)
    near_got = swap(after(near_back, total), CORE)

    factors, normed, inverse, open_part, gain_t = call(
        factor_kernel,
        [((ROWS, 512, 128), F32), (cube, F32), ((ROWS, 128), F32), (cube, F32), ((128, 128), F32)],
        vmem=[flat, cotangent, pair_mask, weights, params, weight_t],
        weight=WAIT,
    )
    output, gate_part = call(
        out_kernel,
        [(cube, BF16), (cube, F32)],
        smem=[me],
        vmem=[out_0, near_got, out_far, open_part, weights],
        scratch=[cube_scratch],
    )
    half_scratch = pltpu.VMEM((half, 128), F32)
    (partial,) = call(
        partial_kernel,
        [(cube, F32)],
        vmem=[grad_left_0, near_got, left_got, right_a[0], right_near, z_got[0]]
        + [factors, gate_part, weights],
        scratch=[pltpu.VMEM((SIDE, 128), F32), half_scratch],
        weight=WAIT // 4,
    )
    (grad_pair,) = call(
        pair_kernel,
        [(cube, BF16)],
        vmem=[right_b[0], right_near, z_got[1]]
        + [factors, partial, normed, inverse, gain_t, weights],
        scratch=[half_scratch],
    )
    return (output, grad_pair)


def norm_stats(values, reduce_axis):
    center = values - jnp.mean(values, axis=reduce_axis, keepdims=True)
    inverse = lax.rsqrt(jnp.mean(center * center, axis=reduce_axis, keepdims=True) + EPSILON)
    return (center * inverse, inverse)


def norm_back(grad_hat, normed, inverse, reduce_axis):
    first = jnp.mean(grad_hat, axis=reduce_axis, keepdims=True)
    second = jnp.mean(grad_hat * normed, axis=reduce_axis, keepdims=True)
    return inverse * (grad_hat - first - normed * second)


def forward_products(left_chan, right_chan):
    return jnp.einsum("hik,hjk->hij", left_chan, right_chan, preferred_element_type=jnp.float32)


def backward_products(grad_full, left_chan, right_chan):
    grad_left = jnp.einsum(
        "hij,hjk->hik", grad_full, right_chan, preferred_element_type=jnp.float32
    )
    grad_right = jnp.einsum(
        "hij,hik->hjk", grad_full, left_chan, preferred_element_type=jnp.float32
    )
    return jnp.stack([grad_left, grad_right]).astype(jnp.bfloat16)


def channels_device(
    pair_rep,
    pair_mask,
    cotangent,
    in_gain,
    in_bias,
    proj_weight,
    gate_weight,
    mid_gain,
    mid_bias,
    out_weight,
):
    width = pair_rep.shape[2]
    hidden = out_weight.shape[0]
    weights_four = proj_weight.reshape(width, 2, 2, hidden)
    mask_float = pair_mask.astype(jnp.float32)
    normed_in, inverse_in = norm_stats(pair_rep.astype(jnp.float32), 2)
    scaled_in = (normed_in * in_gain + in_bias).astype(jnp.bfloat16)
    gate_pre = jnp.einsum(
        "ijc,csh->shij", scaled_in, weights_four[:, :, 0], preferred_element_type=jnp.float32
    )
    value_pre = jnp.einsum(
        "ijc,csh->shij", scaled_in, weights_four[:, :, 1], preferred_element_type=jnp.float32
    )
    sigmoid_gate = jax.nn.sigmoid(gate_pre)
    both_sides = (sigmoid_gate * value_pre * mask_float).astype(jnp.bfloat16)
    gate_sig = jax.nn.sigmoid(
        jnp.einsum("ijc,cd->ijd", scaled_in, gate_weight, preferred_element_type=jnp.float32)
    )
    sides_chan = lax.all_to_all(both_sides, "row", split_axis=1, concat_axis=2, tiled=True)
    partial_sum = forward_products(sides_chan[0], sides_chan[1])
    product = lax.psum_scatter(partial_sum, "col", scatter_dimension=2, tiled=True).astype(
        jnp.bfloat16
    )
    mixed_pair = lax.all_to_all(product, "row", split_axis=1, concat_axis=0, tiled=True)
    normed_mid, inverse_mid = norm_stats(mixed_pair.astype(jnp.float32), 0)
    scaled_mid = (normed_mid * mid_gain[:, None, None] + mid_bias[:, None, None]).astype(
        jnp.bfloat16
    )
    update = jnp.einsum("hij,hc->ijc", scaled_mid, out_weight, preferred_element_type=jnp.float32)
    output = (gate_sig * update).astype(jnp.bfloat16)
    grad_out = cotangent.astype(jnp.float32)
    grad_update = (grad_out * gate_sig).astype(jnp.bfloat16)
    grad_gate = (grad_out * update * gate_sig * (1.0 - gate_sig)).astype(jnp.bfloat16)
    grad_scaled_mid = jnp.einsum(
        "ijc,hc->hij", grad_update, out_weight, preferred_element_type=jnp.float32
    )
    grad_mixed = norm_back(
        grad_scaled_mid * mid_gain[:, None, None], normed_mid, inverse_mid, 0
    ).astype(jnp.bfloat16)
    grad_chan = lax.all_to_all(grad_mixed, "row", split_axis=0, concat_axis=1, tiled=True)
    grad_full = lax.all_gather(grad_chan, "col", axis=2, tiled=True)
    grad_local = backward_products(grad_full, sides_chan[0], sides_chan[1])
    grad_sides = lax.all_to_all(grad_local, "row", split_axis=2, concat_axis=1, tiled=True)
    side_float = grad_sides.astype(jnp.float32) * mask_float
    grad_value = (side_float * sigmoid_gate).astype(jnp.bfloat16)
    grad_gate_pre = (side_float * value_pre * sigmoid_gate * (1.0 - sigmoid_gate)).astype(
        jnp.bfloat16
    )
    grad_scaled = jnp.einsum(
        "shij,csh->ijc", grad_gate_pre, weights_four[:, :, 0], preferred_element_type=jnp.float32
    )
    grad_scaled = grad_scaled + jnp.einsum(
        "shij,csh->ijc", grad_value, weights_four[:, :, 1], preferred_element_type=jnp.float32
    )
    grad_scaled = grad_scaled + jnp.einsum(
        "ijd,cd->ijc", grad_gate, gate_weight, preferred_element_type=jnp.float32
    )
    grad_pair = norm_back(grad_scaled * in_gain, normed_in, inverse_in, 2).astype(jnp.bfloat16)
    return (output, grad_pair)


def solution(mesh):
    blocks = mesh.shape["row"] == 16 and mesh.shape["col"] == 1
    placed = (
        P(("grp", "row"), "col", None),
        P(("grp", "row"), "col"),
        P(("grp", "row"), "col", None),
        P(),
        P(),
        P(),
        P(),
        P(),
        P(),
        P(),
    )
    return jax.shard_map(
        blocks_device if blocks else channels_device,
        mesh=mesh,
        in_specs=placed,
        out_specs=(P(("grp", "row"), "col", None), P(("grp", "row"), "col", None)),
        check_vma=False,
    )
```

```python
import jax
import jax.numpy as jnp
from jax import lax
from jax.experimental import pallas as pl
from jax.experimental.pallas import tpu as pltpu
from jax.sharding import PartitionSpec as P

EPSILON = 1e-05
CORE, CHIP_X, Z_LOW, Z_HIGH = 1, 2, 4, 8
LEFT_OFFSETS = (0, CORE, Z_LOW, Z_LOW | CORE)
RIGHT_OFFSETS = (0, CHIP_X, Z_HIGH, Z_HIGH | CHIP_X)
ROWS = 8
SIDE = 1024
PIECE = 256
HEAD = PIECE + 16
VMEM_BYTES = 48 * 2**20
WAIT = 5 * 10**9

NT = (((1,), (1,)), ((), ()))
NN = (((1,), (0,)), ((), ()))
TN = (((0,), (0,)), ((), ()))
F32, BF16 = jnp.float32, jnp.bfloat16


def dot(a, b, dims):
    return lax.dot_general(a, b, dims, preferred_element_type=F32)


def norm(values, axis):
    center = values - jnp.mean(values, axis=axis, keepdims=True)
    inverse = lax.rsqrt(jnp.mean(center * center, axis=axis, keepdims=True) + EPSILON)
    return center * inverse, inverse


def sigmoid(x):
    return 0.5 * jnp.tanh(0.5 * x) + 0.5


def call(kernel, outs, smem=(), vmem=(), scratch=(), weight=2**26):
    vmem_spec = pl.BlockSpec(memory_space=pltpu.VMEM)
    specs = [pl.BlockSpec(memory_space=pltpu.SMEM)] * len(smem)
    specs += [vmem_spec] * len(vmem)
    return pl.pallas_call(
        kernel,
        out_shape=[jax.ShapeDtypeStruct(s, d) for s, d in outs],
        in_specs=specs,
        out_specs=[vmem_spec] * len(outs),
        scratch_shapes=list(scratch),
        compiler_params=pltpu.CompilerParams(vmem_limit_bytes=VMEM_BYTES),
        cost_estimate=pl.CostEstimate(flops=weight, bytes_accessed=2**18, transcendentals=0),
    )(*smem, *vmem)


def side_rows(quarter, row):
    return pl.ds(quarter * ROWS + row, 32, stride=4 * ROWS)


def store_side(rows_ref, row, result):
    for q in range(4):
        rows_ref[side_rows(q, row), :] = result[q * 32 : (q + 1) * 32]


def load_side(rows_ref, row):
    return jnp.concatenate([rows_ref[side_rows(q, row), :] for q in range(4)], axis=0)


def columns_of(me, offsets):
    return [pl.multiple_of((me ^ o) * ROWS, ROWS) for o in offsets]


def pick_columns(full_ref, starts):
    columns = [full_ref[:, pl.ds(s, ROWS), :] for s in starts]
    return jnp.concatenate(columns, axis=1).reshape(PIECE, 128)


def pack_kernel(me_ref, cot_ref, mask_ref, after_ref, own_ref, core_ref, far_ref, full_ref):
    me = me_ref[0]
    full_ref[...] = cot_ref[...].astype(F32)
    mask = jnp.concatenate([mask_ref[...].astype(F32), jnp.zeros((ROWS, 128), F32)], axis=0)
    places = [(own_ref, 0), (core_ref, 0), (far_ref, 0), (far_ref, HEAD)]
    for (ref, place), offset in zip(places, LEFT_OFFSETS):
        piece = pick_columns(full_ref, columns_of(me ^ offset, RIGHT_OFFSETS))
        ref[place : place + PIECE, :] = piece.astype(BF16)
        ref[place + PIECE : place + HEAD, :] = mask.astype(BF16)


def split_sum(values, ones):
    high = values.astype(BF16)
    low = (values - high.astype(F32)).astype(BF16)
    return dot(high, ones, NN) + dot(low, ones, NN)


def scale_in(x, params_ref):
    return norm(x.astype(F32), 1)[0] * params_ref[0:1, :] + params_ref[1:2, :]


def project(weight_t, scaled, row):
    return dot(weight_t, scaled[row * 128 : (row + 1) * 128], NT)


def make_side(projected):
    return sigmoid(projected[:128]) * projected[128:]


def block_gate(me_ref, scaled_ref, weight_ref):
    picked = pick_columns(scaled_ref, columns_of(me_ref[0], RIGHT_OFFSETS))
    return sigmoid(dot(picked.astype(BF16), weight_ref[:, 512:640], NN))


def own_kernel(
    me_ref,
    x_ref,
    weight_ref,
    params_ref,
    left_ref,
    right_ref,
    sig_ref,
    weight_t_ref,
    block_ref,
    mid_ref,
    rows_ref,
    scaled_ref,
):
    weight_t_ref[...] = weight_ref[:, :512].astype(F32).T.astype(BF16)
    scaled = scale_in(x_ref[...], params_ref)
    scaled_ref[...] = scaled.reshape(scaled_ref.shape)
    scaled = scaled.astype(BF16)
    for row in range(ROWS):
        projected = project(weight_t_ref[...], scaled, row)
        store_side(rows_ref.at[0], row, make_side(projected[:256]))
        store_side(rows_ref.at[1], row, make_side(projected[256:]))
    left_ref[...] = rows_ref[0].astype(BF16)
    right_ref[...] = rows_ref[1].astype(BF16)
    sig_ref[...] = block_gate(me_ref, scaled_ref, weight_ref)

    repeat = lax.broadcasted_iota(jnp.int32, (512, 128), 0)
    lane = lax.broadcasted_iota(jnp.int32, (512, 128), 1)
    spread = jnp.where((repeat >> 2) == lane, 1.0, 0.0).astype(BF16)
    tall = dot(spread, weight_ref[:, 640:], NN)
    for m in range(4):
        block_ref[:, m * 128 : (m + 1) * 128] = jnp.where((repeat & 3) == m, tall, 0.0).astype(BF16)
    rows = lax.broadcasted_iota(jnp.int32, (ROWS, 128), 0)
    both = jnp.where(rows == 0, params_ref[2:3, :], params_ref[3:4, :])
    wide = jnp.zeros((ROWS, 512), F32)
    for _ in range(3):
        term = both.astype(BF16)
        wide = wide + dot(term, spread, NT)
        both = both - term.astype(F32)
    mid_ref[...] = wide


def peer_kernel(me_ref, left_in, *refs):
    right_in, rest = refs[:-8], refs[-8:]
    weight_t_ref, weight_ref, params_ref, left_ref, right_ref, sig_ref, rows_ref, scaled_ref = rest
    scaled = scale_in(left_in[...], params_ref)
    scaled_ref[...] = scaled.reshape(scaled_ref.shape)
    scaled = scaled.astype(BF16)
    for row in range(ROWS):
        projected = project(weight_t_ref[:256, :], scaled, row)
        store_side(rows_ref.at[0], row, make_side(projected))
    scaled = [scale_in(r[...], params_ref).astype(BF16) for r in right_in]
    for row in range(ROWS):
        part, place = divmod(row, ROWS // len(right_in))
        projected = project(weight_t_ref[256:, :], scaled[part], place)
        store_side(rows_ref.at[1], row, make_side(projected))
    left_ref[...] = rows_ref[0].astype(BF16)
    right_ref[...] = rows_ref[1].astype(BF16)
    sig_ref[...] = block_gate(me_ref, scaled_ref, weight_ref)


def left_kernel(
    me_ref, x_ref, weight_t_ref, weight_ref, params_ref, left_ref, sig_ref, rows_ref, scaled_ref
):
    scaled = scale_in(x_ref[...], params_ref)
    scaled_ref[...] = scaled.reshape(scaled_ref.shape)
    scaled = scaled.astype(BF16)
    for row in range(ROWS):
        projected = project(weight_t_ref[:256, :], scaled, row)
        store_side(rows_ref, row, make_side(projected))
    left_ref[...] = rows_ref[...].astype(BF16)
    sig_ref[...] = block_gate(me_ref, scaled_ref, weight_ref)


def right_kernel(first, last):
    def kernel(x_ref, weight_t_ref, params_ref, rest_ref, right_ref, rows_ref):
        if last:
            rows_ref[...] = rest_ref[...]
        else:
            rows_ref[...] = jnp.zeros_like(rows_ref)
        scaled = scale_in(x_ref[...], params_ref).astype(BF16)
        for row in range(ROWS // 2):
            projected = project(weight_t_ref[256:, :], scaled, row)
            store_side(rows_ref, first + row, make_side(projected))
        right_ref[...] = rows_ref[...].astype(right_ref.dtype)

    return kernel


GROUPS = SIDE // 32


def quarters():
    lane = lax.broadcasted_iota(jnp.int32, (ROWS, 128), 1)
    return [((lane >> 3) & 3) == q for q in range(4)]


def slab(side_refs, g):
    return jnp.concatenate([r[g * 32 : (g + 1) * 32, :] for r in side_refs], axis=0)


def block_kernel(*refs):
    me_ref, left_refs, right_refs, sig_refs = refs[0], refs[1:5], refs[5:9], refs[9:13]
    own_ref, core_in, far_in, block_ref, mid_ref = refs[13:18]
    pieces = [(own_ref, 0), (core_in, 0), (far_in, 0), (core_in, HEAD)]
    out_refs, pairs_ref = refs[18:22], refs[22]
    me = me_ref[0]
    of_quarter = quarters()

    masks = [ref[at + PIECE : at + HEAD, :].astype(F32) for ref, at in pieces]
    valid = jnp.max(jnp.concatenate(masks, axis=0), axis=0, keepdims=True)
    src = lax.broadcasted_iota(jnp.int32, (128, 128), 0)
    dst = lax.broadcasted_iota(jnp.int32, (128, 128), 1)
    pick = jnp.zeros((128, 128), F32)
    for n, offset in enumerate(RIGHT_OFFSETS):
        wanted = (me ^ offset) * ROWS + (dst & 7)
        pick = jnp.where((src == wanted) & ((dst >> 5) == n), 1.0, pick)
    spread = jnp.broadcast_to(valid, (ROWS, 128)).astype(BF16)
    column_valid = dot(spread, pick.astype(BF16), NN)
    pair_valid = [jnp.max(k[:ROWS], axis=1, keepdims=True) * column_valid for k in masks]
    valid = jnp.broadcast_to(valid, (128, 128)).astype(BF16)

    for g in range(GROUPS):
        full = dot(slab(left_refs, g) * valid, slab(right_refs, g), NT).reshape(4, 4, ROWS, 128)
        for m in range(4):
            kept = full[m, 3]
            for q in range(3):
                kept = jnp.where(of_quarter[q], full[m, q], kept)
            pairs_ref[g * 32 + m * ROWS : g * 32 + (m + 1) * ROWS, :] = kept * pair_valid[m]

    turned = []
    for row in range(ROWS):
        turn = pairs_ref[pl.ds(row, 128, stride=ROWS), :].T.reshape(4, 4, ROWS, 128)
        turned.append(jnp.concatenate([turn[:, q].reshape(32, 128) for q in range(4)], axis=1))
    mixed = jnp.concatenate(turned, axis=0).astype(BF16).astype(F32)

    ones = jnp.where((src & 3) == (dst & 3), 1.0, 0.0).astype(BF16)

    def channel_mean(values):
        total = values[:, :128] + values[:, 128:256] + values[:, 256:384] + values[:, 384:]
        mean = split_sum(total, ones) * (1.0 / 128.0)
        return jnp.concatenate([mean] * 4, axis=1)

    mid_gain, mid_bias = mid_ref[0:1, :], mid_ref[1:2, :]
    center = mixed - channel_mean(mixed)
    inverse = lax.rsqrt(channel_mean(center * center) + EPSILON)
    normed = center * inverse
    scaled = (normed * mid_gain + mid_bias).astype(BF16)
    update = dot(scaled, block_ref[...], NN)
    grad_update = []
    for m in range(4):
        sig = sig_refs[m][...]
        out = sig * update[:, m * 128 : (m + 1) * 128]
        out_refs[m][...] = out.astype(BF16)
        ref, at = pieces[m]
        cot = ref[at : at + PIECE, :].astype(F32)
        grad_update.append((cot * sig).astype(BF16))
    grad_hat = dot(jnp.concatenate(grad_update, axis=1), block_ref[...], NT) * mid_gain
    first = channel_mean(grad_hat)
    second = channel_mean(grad_hat * normed)
    grad_mixed = inverse * (grad_hat - first - normed * second)

    mask = jnp.concatenate(pair_valid, axis=0)
    for row in range(ROWS):
        part = grad_mixed[row * 32 : (row + 1) * 32]
        parts = [part[:, q * 128 : (q + 1) * 128].reshape(4, 1, ROWS, 128) for q in range(4)]
        turn = jnp.concatenate(parts, axis=1).reshape(128, 128)
        pairs_ref[pl.ds(row, 128, stride=ROWS), :] = turn.T
    for g in range(GROUPS):
        pairs_ref[g * 32 : (g + 1) * 32, :] = pairs_ref[g * 32 : (g + 1) * 32, :] * mask


def spread_group(pairs_ref, g, of_quarter):
    rows = []
    for m in range(4):
        part = pairs_ref[g * 32 + m * ROWS : g * 32 + (m + 1) * ROWS, :]
        rows += [jnp.where(of_quarter[q], part, 0.0) for q in range(4)]
    return jnp.concatenate(rows, axis=0).astype(BF16)


def grad_right_kernel(half):
    def kernel(pairs_ref, *refs):
        left_refs, out_refs = refs[:4], refs[4:]
        of_quarter = quarters()
        for g in range(GROUPS // 2):
            spread = spread_group(pairs_ref, half * GROUPS // 2 + g, of_quarter)
            grad = dot(spread, slab(left_refs, half * GROUPS // 2 + g), TN).astype(BF16)
            for n in range(4):
                out_refs[n][g * 32 : (g + 1) * 32, :] = grad[n * 32 : (n + 1) * 32]

    return kernel


def grad_left_kernel(pairs_ref, *refs):
    right_refs, (out_near, out_both), lefts = refs[:4], refs[4:6], refs[7:]
    of_quarter = quarters()
    for g in range(GROUPS):
        spread = spread_group(pairs_ref, g, of_quarter)
        grad = dot(spread, slab(right_refs, g), NN).astype(BF16)
        for m, ref in enumerate(lefts):
            ref[g * 32 : (g + 1) * 32, :] = grad[m * 32 : (m + 1) * 32]
    lefts[1][SIDE:, :] = out_near[...]
    lefts[3][SIDE:, :] = out_both[...]


def halves_kernel(x_ref, first_ref, second_ref):
    first_ref[...] = x_ref[: SIDE // 2, :]
    second_ref[...] = x_ref[SIDE // 2 :, :]


def pass_kernel(message_ref, *refs):
    refs[-1][...] = message_ref[...]


def join_kernel(mine_ref, got_ref, both_ref):
    both_ref[:HEAD, :] = mine_ref[...]
    both_ref[HEAD:, :] = got_ref[HEAD:, :]


def add_kernel(mine_ref, got_ref, *refs):
    sum_ref = refs[-1]
    sum_ref[...] = (mine_ref[...].astype(F32) + got_ref[...].astype(F32)).astype(BF16)


def early_kernel(mine_ref, got_ref, sum_ref):
    sum_ref[...] = mine_ref[...].astype(F32) + got_ref[:SIDE, :].astype(F32)


def near_kernel(first_ref, second_ref, *refs):
    both_ref = refs[-1]
    both_ref[: SIDE // 2, :] = first_ref[...]
    both_ref[SIDE // 2 :, :] = second_ref[...]


def add_left_kernel(mine_ref, piece_ref, got_ref, sum_ref, out_ref):
    sum_ref[...] = (mine_ref[...].astype(F32) + got_ref[:SIDE, :].astype(F32)).astype(BF16)
    out_ref[:PIECE, :] = piece_ref[...]
    out_ref[PIECE:, :] = got_ref[SIDE:, :]


def factor_kernel(
    x_ref,
    cot_ref,
    mask_ref,
    weight_ref,
    params_ref,
    weight_t_ref,
    factor_ref,
    normed_ref,
    inverse_ref,
    open_ref,
    gain_t_ref,
):
    gain_t = jnp.broadcast_to(params_ref[0:1, :], (128, 128)).T
    bias_t = jnp.broadcast_to(params_ref[1:2, :], (128, 128)).T
    gain_t_ref[...] = gain_t
    scaled = scale_in(x_ref[...], params_ref).astype(BF16)
    gate_sig = sigmoid(dot(scaled, weight_ref[:, 512:640], NN)).reshape(cot_ref.shape)
    open_ref[...] = cot_ref[...].astype(F32) * (1.0 - gate_sig)
    for row in range(ROWS):
        x = x_ref[row * 128 : (row + 1) * 128, :]
        normed, inverse = norm(x.astype(F32).T, 0)
        normed_ref[row] = normed
        inverse_ref[row : row + 1, :] = inverse
        scaled = (normed * gain_t + bias_t).astype(BF16)
        projected = dot(weight_t_ref[...], scaled, NN)
        keep = mask_ref[row : row + 1].astype(F32)
        for side in range(2):
            base = 256 * side
            gate = sigmoid(projected[base : base + 128])
            value = projected[base + 128 : base + 256]
            factor_ref[row, base : base + 128, :] = keep * value * gate * (1.0 - gate)
            factor_ref[row, base + 128 : base + 256, :] = keep * gate


def out_kernel(me_ref, own_ref, near_ref, far_ref, open_ref, weight_ref, out_ref, grad_ref, full_ref):
    places = [(own_ref, 0), (near_ref, SIDE), (far_ref, 0), (far_ref, PIECE)]
    for (ref, at), offset in zip(places, LEFT_OFFSETS):
        piece = ref[at : at + PIECE, :].astype(F32).reshape(ROWS, 4, ROWS, 128)
        for n, start in enumerate(columns_of(me_ref[0] ^ offset, RIGHT_OFFSETS)):
            full_ref[:, pl.ds(start, ROWS), :] = piece[:, n]
    for row in range(ROWS):
        out = full_ref[row]
        out_ref[row] = out.astype(BF16)
        grad_gate = (open_ref[row] * out).astype(BF16)
        grad_ref[row] = dot(weight_ref[:, 512:640], grad_gate, NT)


def right_terms(rows_ref, factor_ref, row, half):
    parts = []
    nothing = jnp.zeros((16, 128), BF16)
    for place in (256, 384):
        for q in range(4):
            grad = rows_ref[pl.ds(q * ROWS + row, 16, stride=4 * ROWS), :]
            at = place + q * 32 + half * 16
            term = (grad * factor_ref[row, at : at + 16, :]).astype(BF16)
            parts += [nothing, term] if half else [term, nothing]
    return jnp.concatenate(parts, axis=0)


def partial_kernel(*refs):
    left_ref, left_got_ref, own_ref, near_ref, got_ref = refs[:5]
    factor_ref, gate_ref, weight_ref, sum_ref, left_rows, right_rows = refs[5:]
    left_rows[...] = left_ref[...] + left_got_ref[...].astype(F32)
    right = own_ref[...].astype(F32) + near_ref[: SIDE // 2, :].astype(F32)
    right_rows[...] = right + got_ref[...].astype(F32)
    for row in range(ROWS):
        grad = load_side(left_rows, row)
        parts = [(grad * factor_ref[row, a : a + 128, :]).astype(BF16) for a in (0, 128)]
        parts.append(right_terms(right_rows, factor_ref, row, 0))
        grad_projected = jnp.concatenate(parts, axis=0)
        sum_ref[row] = dot(weight_ref[:, :512], grad_projected, NN) + gate_ref[row]


def pair_kernel(
    own_ref,
    near_ref,
    got_ref,
    factor_ref,
    sum_ref,
    normed_ref,
    inverse_ref,
    gain_t_ref,
    weight_ref,
    out_ref,
    right_rows,
):
    right = own_ref[...].astype(F32) + near_ref[SIDE // 2 :, :].astype(F32)
    right_rows[...] = right + got_ref[...].astype(F32)
    for row in range(ROWS):
        terms = right_terms(right_rows, factor_ref, row, 1)
        grad_scaled = dot(weight_ref[:, 256:512], terms, NN) + sum_ref[row]
        normed = normed_ref[row]
        grad_hat = grad_scaled * gain_t_ref[...]
        first = jnp.mean(grad_hat, axis=0, keepdims=True)
        second = jnp.mean(grad_hat * normed, axis=0, keepdims=True)
        grad = inverse_ref[row : row + 1, :] * (grad_hat - first - normed * second)
        out_ref[row] = grad.T.astype(BF16)


def swap(values, offset):
    return lax.ppermute(values, "row", [(s, s ^ offset) for s in range(16)])


def blocks_device(
    pair_rep,
    pair_mask,
    cotangent,
    in_gain,
    in_bias,
    proj_weight,
    gate_weight,
    mid_gain,
    mid_bias,
    out_weight,
):
    me = lax.axis_index("row").astype(jnp.int32).reshape(1)
    half = SIDE // 2
    cube = (ROWS, 128, 128)
    side, piece = ((SIDE, 128), BF16), ((PIECE, 128), BF16)
    halves, core = ((half, 128), BF16), ((SIDE + PIECE, 128), BF16)
    sig = ((PIECE, 128), F32)
    rows_scratch = pltpu.VMEM((2, SIDE, 128), F32)
    cube_scratch = pltpu.VMEM(cube, F32)

    def after(message, *others):
        return call(pass_kernel, [(message.shape, BF16)], vmem=[message, *others])[0]

    flat = pair_rep.reshape(SIDE, 128)
    weights = jnp.zeros((), BF16)
    for at, weight in ((0, proj_weight), (512, gate_weight), (640, out_weight)):
        weights = weights + jnp.pad(weight, ((0, 0), (at, 768 - at - weight.shape[1])))
    params = jnp.stack([in_gain, in_bias, mid_gain, mid_bias])

    first, second = call(halves_kernel, [halves] * 2, vmem=[flat])
    z_first, z_second = swap(first, Z_HIGH), swap(second, Z_HIGH)
    whole = after(flat, second)
    far = swap(whole, Z_LOW)
    x_near = swap(whole, CHIP_X)
    near = swap(whole, CORE)
    left_0, right_0, sig_0, weight_t, block_weight, mid = call(
        own_kernel,
        [side, side, sig, ((512, 128), BF16), ((512, 512), BF16), ((ROWS, 512), F32)],
        smem=[me],
        vmem=[whole, weights, params],
        scratch=[rows_scratch, cube_scratch],
        weight=WAIT,
    )

    def peer(*messages):
        return call(
            peer_kernel,
            [side, side, sig],
            smem=[me],
            vmem=[*messages, weight_t, weights, params],
            scratch=[rows_scratch, cube_scratch],
            weight=WAIT,
        )

    left_1, right_1, sig_1 = peer(near, x_near)
    own_piece, core_piece, far_piece = call(
        pack_kernel,
        [((HEAD, 128), BF16), ((HEAD, 128), BF16), ((2 * HEAD, 128), BF16)],
        smem=[me],
        vmem=[cotangent, pair_mask, x_near],
        scratch=[cube_scratch],
    )
    far_got = swap(far_piece, Z_LOW)
    both = swap(far, CORE)
    x_second = swap(z_second, CHIP_X)
    x_first = swap(after(z_first, x_second, left_0), CHIP_X)
    (joined,) = call(join_kernel, [((2 * HEAD, 128), BF16)], vmem=[core_piece, far_got])
    core_pieces = swap(joined, CORE)
    left_2, right_2, sig_2 = peer(far, z_first, z_second)
    left_3, sig_3 = call(
        left_kernel,
        [side, sig],
        smem=[me],
        vmem=[both, weight_t, weights, params],
        scratch=[pltpu.VMEM((SIDE, 128), F32), cube_scratch],
        weight=WAIT,
    )

    def right_half(first, last, *operands):
        return call(
            right_kernel(first, last),
            [((SIDE, 128), BF16 if last else F32)],
            vmem=operands,
            scratch=[pltpu.VMEM((SIDE, 128), F32)],
            weight=WAIT // 4,
        )[0]

    right_part = right_half(ROWS // 2, False, x_second, weight_t, params, left_3)
    right_3 = right_half(0, True, x_first, weight_t, params, right_part)

    lefts, rights = [left_0, left_1, left_2, left_3], [right_0, right_1, right_2, right_3]
    out_0, out_1, out_2, out_3, pairs = call(
        block_kernel,
        [piece] * 4 + [((SIDE, 128), F32)],
        smem=[me],
        vmem=lefts
        + rights
        + [sig_0, sig_1, sig_2, sig_3]
        + [own_piece, core_pieces, far_got, block_weight, mid],
    )
    right_a = call(grad_right_kernel(0), [halves] * 4, vmem=[pairs, *lefts])
    x_got = [swap(right_a[3], CHIP_X)]
    grad_left_0, near_back, grad_left_2, both_back = call(
        grad_left_kernel,
        [side, core, side, core],
        vmem=[pairs, *rights, out_1, out_3, right_a[3]],
    )
    both_got = swap(both_back, CORE)
    right_b = call(grad_right_kernel(1), [halves] * 4, vmem=[pairs, *lefts], weight=WAIT)
    left_sum, out_far = call(
        add_left_kernel,
        [side, ((2 * PIECE, 128), BF16)],
        vmem=[grad_left_2, out_2, both_got],
    )
    x_got.append(swap(after(right_b[3], left_sum), CHIP_X))
    near_got = swap(after(near_back, left_sum), CORE)
    (left_part,) = call(early_kernel, [((SIDE, 128), F32)], vmem=[grad_left_0, near_got])
    left_got = swap(left_sum, Z_LOW)
    out_far = swap(out_far, Z_LOW)
    (total,) = call(add_kernel, [halves], vmem=[right_a[2], x_got[0], left_sum])
    z_got = [swap(total, Z_HIGH)]
    (total,) = call(add_kernel, [halves], vmem=[right_b[2], x_got[1], left_sum])
    z_got.append(swap(total, Z_HIGH))
    (right_back,) = call(near_kernel, [side], vmem=[right_a[1], right_b[1], total, left_part])
    right_near = swap(right_back, CHIP_X)

    factors, normed, inverse, open_part, gain_t = call(
        factor_kernel,
        [((ROWS, 512, 128), F32), (cube, F32), ((ROWS, 128), F32), (cube, F32), ((128, 128), F32)],
        vmem=[whole, cotangent, pair_mask, weights, params, weight_t],
        weight=WAIT,
    )
    output, gate_part = call(
        out_kernel,
        [(cube, BF16), (cube, F32)],
        smem=[me],
        vmem=[out_0, near_got, out_far, open_part, weights],
        scratch=[cube_scratch],
    )
    half_scratch = pltpu.VMEM((half, 128), F32)
    (partial,) = call(
        partial_kernel,
        [(cube, F32)],
        vmem=[left_part, left_got, right_a[0], right_near, z_got[0]]
        + [factors, gate_part, weights],
        scratch=[pltpu.VMEM((SIDE, 128), F32), half_scratch],
        weight=WAIT // 4,
    )
    (grad_pair,) = call(
        pair_kernel,
        [(cube, BF16)],
        vmem=[right_b[0], right_near, z_got[1]]
        + [factors, partial, normed, inverse, gain_t, weights],
        scratch=[half_scratch],
    )
    return (output, grad_pair)


def norm_stats(values, reduce_axis):
    center = values - jnp.mean(values, axis=reduce_axis, keepdims=True)
    inverse = lax.rsqrt(jnp.mean(center * center, axis=reduce_axis, keepdims=True) + EPSILON)
    return (center * inverse, inverse)


def norm_back(grad_hat, normed, inverse, reduce_axis):
    first = jnp.mean(grad_hat, axis=reduce_axis, keepdims=True)
    second = jnp.mean(grad_hat * normed, axis=reduce_axis, keepdims=True)
    return inverse * (grad_hat - first - normed * second)


def forward_products(left_chan, right_chan):
    return jnp.einsum("hik,hjk->hij", left_chan, right_chan, preferred_element_type=jnp.float32)


def backward_products(grad_full, left_chan, right_chan):
    grad_left = jnp.einsum(
        "hij,hjk->hik", grad_full, right_chan, preferred_element_type=jnp.float32
    )
    grad_right = jnp.einsum(
        "hij,hik->hjk", grad_full, left_chan, preferred_element_type=jnp.float32
    )
    return jnp.stack([grad_left, grad_right]).astype(jnp.bfloat16)


def channels_device(
    pair_rep,
    pair_mask,
    cotangent,
    in_gain,
    in_bias,
    proj_weight,
    gate_weight,
    mid_gain,
    mid_bias,
    out_weight,
):
    width = pair_rep.shape[2]
    hidden = out_weight.shape[0]
    weights_four = proj_weight.reshape(width, 2, 2, hidden)
    mask_float = pair_mask.astype(jnp.float32)
    normed_in, inverse_in = norm_stats(pair_rep.astype(jnp.float32), 2)
    scaled_in = (normed_in * in_gain + in_bias).astype(jnp.bfloat16)
    gate_pre = jnp.einsum(
        "ijc,csh->shij", scaled_in, weights_four[:, :, 0], preferred_element_type=jnp.float32
    )
    value_pre = jnp.einsum(
        "ijc,csh->shij", scaled_in, weights_four[:, :, 1], preferred_element_type=jnp.float32
    )
    sigmoid_gate = jax.nn.sigmoid(gate_pre)
    both_sides = (sigmoid_gate * value_pre * mask_float).astype(jnp.bfloat16)
    gate_sig = jax.nn.sigmoid(
        jnp.einsum("ijc,cd->ijd", scaled_in, gate_weight, preferred_element_type=jnp.float32)
    )
    sides_chan = lax.all_to_all(both_sides, "row", split_axis=1, concat_axis=2, tiled=True)
    partial_sum = forward_products(sides_chan[0], sides_chan[1])
    product = lax.psum_scatter(partial_sum, "col", scatter_dimension=2, tiled=True).astype(
        jnp.bfloat16
    )
    mixed_pair = lax.all_to_all(product, "row", split_axis=1, concat_axis=0, tiled=True)
    normed_mid, inverse_mid = norm_stats(mixed_pair.astype(jnp.float32), 0)
    scaled_mid = (normed_mid * mid_gain[:, None, None] + mid_bias[:, None, None]).astype(
        jnp.bfloat16
    )
    update = jnp.einsum("hij,hc->ijc", scaled_mid, out_weight, preferred_element_type=jnp.float32)
    output = (gate_sig * update).astype(jnp.bfloat16)
    grad_out = cotangent.astype(jnp.float32)
    grad_update = (grad_out * gate_sig).astype(jnp.bfloat16)
    grad_gate = (grad_out * update * gate_sig * (1.0 - gate_sig)).astype(jnp.bfloat16)
    grad_scaled_mid = jnp.einsum(
        "ijc,hc->hij", grad_update, out_weight, preferred_element_type=jnp.float32
    )
    grad_mixed = norm_back(
        grad_scaled_mid * mid_gain[:, None, None], normed_mid, inverse_mid, 0
    ).astype(jnp.bfloat16)
    grad_chan = lax.all_to_all(grad_mixed, "row", split_axis=0, concat_axis=1, tiled=True)
    grad_full = lax.all_gather(grad_chan, "col", axis=2, tiled=True)
    grad_local = backward_products(grad_full, sides_chan[0], sides_chan[1])
    grad_sides = lax.all_to_all(grad_local, "row", split_axis=2, concat_axis=1, tiled=True)
    side_float = grad_sides.astype(jnp.float32) * mask_float
    grad_value = (side_float * sigmoid_gate).astype(jnp.bfloat16)
    grad_gate_pre = (side_float * value_pre * sigmoid_gate * (1.0 - sigmoid_gate)).astype(
        jnp.bfloat16
    )
    grad_scaled = jnp.einsum(
        "shij,csh->ijc", grad_gate_pre, weights_four[:, :, 0], preferred_element_type=jnp.float32
    )
    grad_scaled = grad_scaled + jnp.einsum(
        "shij,csh->ijc", grad_value, weights_four[:, :, 1], preferred_element_type=jnp.float32
    )
    grad_scaled = grad_scaled + jnp.einsum(
        "ijd,cd->ijc", grad_gate, gate_weight, preferred_element_type=jnp.float32
    )
    grad_pair = norm_back(grad_scaled * in_gain, normed_in, inverse_in, 2).astype(jnp.bfloat16)
    return (output, grad_pair)


def solution(mesh):
    blocks = mesh.shape["row"] == 16 and mesh.shape["col"] == 1
    placed = (
        P(("grp", "row"), "col", None),
        P(("grp", "row"), "col"),
        P(("grp", "row"), "col", None),
        P(),
        P(),
        P(),
        P(),
        P(),
        P(),
        P(),
    )
    return jax.shard_map(
        blocks_device if blocks else channels_device,
        mesh=mesh,
        in_specs=placed,
        out_specs=(P(("grp", "row"), "col", None), P(("grp", "row"), "col", None)),
        check_vma=False,
    )
```

```python
import jax
import jax.numpy as jnp
from jax import lax
from jax.experimental import pallas as pl
from jax.experimental.pallas import tpu as pltpu
from jax.sharding import PartitionSpec as P

EPSILON = 1e-05
CORE, CHIP_X, Z_LOW, Z_HIGH = 1, 2, 4, 8
LEFT_OFFSETS = (0, CORE, Z_LOW, Z_LOW | CORE)
RIGHT_OFFSETS = (0, CHIP_X, Z_HIGH, Z_HIGH | CHIP_X)
ROWS = 8
SIDE = 1024
PIECE = 256
HEAD = PIECE + 16
VMEM_BYTES = 48 * 2**20
WAIT = 5 * 10**9

NT = (((1,), (1,)), ((), ()))
NN = (((1,), (0,)), ((), ()))
TN = (((0,), (0,)), ((), ()))
F32, BF16 = jnp.float32, jnp.bfloat16


def dot(a, b, dims):
    return lax.dot_general(a, b, dims, preferred_element_type=F32)


def norm(values, axis):
    center = values - jnp.mean(values, axis=axis, keepdims=True)
    inverse = lax.rsqrt(jnp.mean(center * center, axis=axis, keepdims=True) + EPSILON)
    return center * inverse, inverse


def sigmoid(x):
    return 0.5 * jnp.tanh(0.5 * x) + 0.5


def call(kernel, outs, smem=(), vmem=(), scratch=(), weight=2**26):
    vmem_spec = pl.BlockSpec(memory_space=pltpu.VMEM)
    specs = [pl.BlockSpec(memory_space=pltpu.SMEM)] * len(smem)
    specs += [vmem_spec] * len(vmem)
    return pl.pallas_call(
        kernel,
        out_shape=[jax.ShapeDtypeStruct(s, d) for s, d in outs],
        in_specs=specs,
        out_specs=[vmem_spec] * len(outs),
        scratch_shapes=list(scratch),
        compiler_params=pltpu.CompilerParams(vmem_limit_bytes=VMEM_BYTES),
        cost_estimate=pl.CostEstimate(flops=weight, bytes_accessed=2**18, transcendentals=0),
    )(*smem, *vmem)


def side_rows(quarter, row):
    return pl.ds(quarter * ROWS + row, 32, stride=4 * ROWS)


def store_side(rows_ref, row, result):
    for q in range(4):
        rows_ref[side_rows(q, row), :] = result[q * 32 : (q + 1) * 32]


def load_side(rows_ref, row):
    return jnp.concatenate([rows_ref[side_rows(q, row), :] for q in range(4)], axis=0)


def columns_of(me, offsets):
    return [pl.multiple_of((me ^ o) * ROWS, ROWS) for o in offsets]


def pick_columns(full_ref, starts):
    columns = [full_ref[:, pl.ds(s, ROWS), :] for s in starts]
    return jnp.concatenate(columns, axis=1).reshape(PIECE, 128)


def pack_kernel(me_ref, cot_ref, mask_ref, after_ref, own_ref, core_ref, far_ref, full_ref):
    me = me_ref[0]
    full_ref[...] = cot_ref[...].astype(F32)
    mask = jnp.concatenate([mask_ref[...].astype(F32), jnp.zeros((ROWS, 128), F32)], axis=0)
    places = [(own_ref, 0), (core_ref, 0), (far_ref, 0), (far_ref, HEAD)]
    for (ref, place), offset in zip(places, LEFT_OFFSETS):
        piece = pick_columns(full_ref, columns_of(me ^ offset, RIGHT_OFFSETS))
        ref[place : place + PIECE, :] = piece.astype(BF16)
        ref[place + PIECE : place + HEAD, :] = mask.astype(BF16)


def split_sum(values, ones):
    high = values.astype(BF16)
    low = (values - high.astype(F32)).astype(BF16)
    return dot(high, ones, NN) + dot(low, ones, NN)


def scale_in(x, params_ref):
    return norm(x.astype(F32), 1)[0] * params_ref[0:1, :] + params_ref[1:2, :]


def project(weight_t, scaled, row):
    return dot(weight_t, scaled[row * 128 : (row + 1) * 128], NT)


def make_side(projected):
    return sigmoid(projected[:128]) * projected[128:]


def block_gate(me_ref, scaled_ref, weight_ref):
    picked = pick_columns(scaled_ref, columns_of(me_ref[0], RIGHT_OFFSETS))
    return sigmoid(dot(picked.astype(BF16), weight_ref[:, 512:640], NN))


def own_kernel(
    me_ref,
    x_ref,
    weight_ref,
    params_ref,
    left_ref,
    right_ref,
    sig_ref,
    weight_t_ref,
    block_ref,
    mid_ref,
    rows_ref,
    scaled_ref,
):
    weight_t_ref[...] = weight_ref[:, :512].astype(F32).T.astype(BF16)
    scaled = scale_in(x_ref[...], params_ref)
    scaled_ref[...] = scaled.reshape(scaled_ref.shape)
    scaled = scaled.astype(BF16)
    for row in range(ROWS):
        projected = project(weight_t_ref[...], scaled, row)
        store_side(rows_ref.at[0], row, make_side(projected[:256]))
        store_side(rows_ref.at[1], row, make_side(projected[256:]))
    left_ref[...] = rows_ref[0].astype(BF16)
    right_ref[...] = rows_ref[1].astype(BF16)
    sig_ref[...] = block_gate(me_ref, scaled_ref, weight_ref)

    repeat = lax.broadcasted_iota(jnp.int32, (512, 128), 0)
    lane = lax.broadcasted_iota(jnp.int32, (512, 128), 1)
    spread = jnp.where((repeat >> 2) == lane, 1.0, 0.0).astype(BF16)
    tall = dot(spread, weight_ref[:, 640:], NN)
    for m in range(4):
        block_ref[:, m * 128 : (m + 1) * 128] = jnp.where((repeat & 3) == m, tall, 0.0).astype(BF16)
    rows = lax.broadcasted_iota(jnp.int32, (ROWS, 128), 0)
    both = jnp.where(rows == 0, params_ref[2:3, :], params_ref[3:4, :])
    wide = jnp.zeros((ROWS, 512), F32)
    for _ in range(3):
        term = both.astype(BF16)
        wide = wide + dot(term, spread, NT)
        both = both - term.astype(F32)
    mid_ref[...] = wide


def peer_kernel(me_ref, left_in, *refs):
    right_in, rest = refs[:-8], refs[-8:]
    weight_t_ref, weight_ref, params_ref, left_ref, right_ref, sig_ref, rows_ref, scaled_ref = rest
    scaled = scale_in(left_in[...], params_ref)
    scaled_ref[...] = scaled.reshape(scaled_ref.shape)
    scaled = scaled.astype(BF16)
    for row in range(ROWS):
        projected = project(weight_t_ref[:256, :], scaled, row)
        store_side(rows_ref.at[0], row, make_side(projected))
    scaled = [scale_in(r[...], params_ref).astype(BF16) for r in right_in]
    for row in range(ROWS):
        part, place = divmod(row, ROWS // len(right_in))
        projected = project(weight_t_ref[256:, :], scaled[part], place)
        store_side(rows_ref.at[1], row, make_side(projected))
    left_ref[...] = rows_ref[0].astype(BF16)
    right_ref[...] = rows_ref[1].astype(BF16)
    sig_ref[...] = block_gate(me_ref, scaled_ref, weight_ref)


def left_kernel(
    me_ref, x_ref, weight_t_ref, weight_ref, params_ref, left_ref, sig_ref, rows_ref, scaled_ref
):
    scaled = scale_in(x_ref[...], params_ref)
    scaled_ref[...] = scaled.reshape(scaled_ref.shape)
    scaled = scaled.astype(BF16)
    for row in range(ROWS):
        projected = project(weight_t_ref[:256, :], scaled, row)
        store_side(rows_ref, row, make_side(projected))
    left_ref[...] = rows_ref[...].astype(BF16)
    sig_ref[...] = block_gate(me_ref, scaled_ref, weight_ref)


def right_kernel(first, last):
    def kernel(x_ref, weight_t_ref, params_ref, rest_ref, right_ref, rows_ref):
        if last:
            rows_ref[...] = rest_ref[...]
        else:
            rows_ref[...] = jnp.zeros_like(rows_ref)
        scaled = scale_in(x_ref[...], params_ref).astype(BF16)
        for row in range(ROWS // 2):
            projected = project(weight_t_ref[256:, :], scaled, row)
            store_side(rows_ref, first + row, make_side(projected))
        right_ref[...] = rows_ref[...].astype(right_ref.dtype)

    return kernel


GROUPS = SIDE // 32


def quarters():
    lane = lax.broadcasted_iota(jnp.int32, (ROWS, 128), 1)
    return [((lane >> 3) & 3) == q for q in range(4)]


def slab(side_refs, g):
    return jnp.concatenate([r[g * 32 : (g + 1) * 32, :] for r in side_refs], axis=0)


def block_kernel(*refs):
    me_ref, left_refs, right_refs, sig_refs = refs[0], refs[1:5], refs[5:9], refs[9:13]
    own_ref, core_in, far_in, block_ref, mid_ref = refs[13:18]
    pieces = [(own_ref, 0), (core_in, 0), (far_in, 0), (core_in, HEAD)]
    own_out, near_out, far_out, pairs_ref = refs[18:22]
    outs = [(own_out, 0), (near_out, 0), (far_out, 0), (far_out, PIECE)]
    me = me_ref[0]
    of_quarter = quarters()

    masks = [ref[at + PIECE : at + HEAD, :].astype(F32) for ref, at in pieces]
    valid = jnp.max(jnp.concatenate(masks, axis=0), axis=0, keepdims=True)
    src = lax.broadcasted_iota(jnp.int32, (128, 128), 0)
    dst = lax.broadcasted_iota(jnp.int32, (128, 128), 1)
    pick = jnp.zeros((128, 128), F32)
    for n, offset in enumerate(RIGHT_OFFSETS):
        wanted = (me ^ offset) * ROWS + (dst & 7)
        pick = jnp.where((src == wanted) & ((dst >> 5) == n), 1.0, pick)
    spread = jnp.broadcast_to(valid, (ROWS, 128)).astype(BF16)
    column_valid = dot(spread, pick.astype(BF16), NN)
    pair_valid = [jnp.max(k[:ROWS], axis=1, keepdims=True) * column_valid for k in masks]
    valid = jnp.broadcast_to(valid, (128, 128)).astype(BF16)

    for g in range(GROUPS):
        full = dot(slab(left_refs, g) * valid, slab(right_refs, g), NT).reshape(4, 4, ROWS, 128)
        for m in range(4):
            kept = full[m, 3]
            for q in range(3):
                kept = jnp.where(of_quarter[q], full[m, q], kept)
            pairs_ref[g * 32 + m * ROWS : g * 32 + (m + 1) * ROWS, :] = kept * pair_valid[m]

    turned = []
    for row in range(ROWS):
        turn = pairs_ref[pl.ds(row, 128, stride=ROWS), :].T.reshape(4, 4, ROWS, 128)
        turned.append(jnp.concatenate([turn[:, q].reshape(32, 128) for q in range(4)], axis=1))
    mixed = jnp.concatenate(turned, axis=0).astype(BF16).astype(F32)

    ones = jnp.where((src & 3) == (dst & 3), 1.0, 0.0).astype(BF16)

    def channel_mean(values):
        total = values[:, :128] + values[:, 128:256] + values[:, 256:384] + values[:, 384:]
        mean = split_sum(total, ones) * (1.0 / 128.0)
        return jnp.concatenate([mean] * 4, axis=1)

    mid_gain, mid_bias = mid_ref[0:1, :], mid_ref[1:2, :]
    center = mixed - channel_mean(mixed)
    inverse = lax.rsqrt(channel_mean(center * center) + EPSILON)
    normed = center * inverse
    scaled = (normed * mid_gain + mid_bias).astype(BF16)
    update = dot(scaled, block_ref[...], NN)
    grad_update = []
    for m in range(4):
        sig = sig_refs[m][...]
        out = sig * update[:, m * 128 : (m + 1) * 128]
        ref, at = outs[m]
        ref[at : at + PIECE, :] = out.astype(BF16)
        ref, at = pieces[m]
        cot = ref[at : at + PIECE, :].astype(F32)
        grad_update.append((cot * sig).astype(BF16))
    grad_hat = dot(jnp.concatenate(grad_update, axis=1), block_ref[...], NT) * mid_gain
    first = channel_mean(grad_hat)
    second = channel_mean(grad_hat * normed)
    grad_mixed = inverse * (grad_hat - first - normed * second)

    mask = jnp.concatenate(pair_valid, axis=0)
    for row in range(ROWS):
        part = grad_mixed[row * 32 : (row + 1) * 32]
        parts = [part[:, q * 128 : (q + 1) * 128].reshape(4, 1, ROWS, 128) for q in range(4)]
        turn = jnp.concatenate(parts, axis=1).reshape(128, 128)
        pairs_ref[pl.ds(row, 128, stride=ROWS), :] = turn.T
    for g in range(GROUPS):
        pairs_ref[g * 32 : (g + 1) * 32, :] = pairs_ref[g * 32 : (g + 1) * 32, :] * mask


def spread_group(pairs_ref, g, of_quarter):
    rows = []
    for m in range(4):
        part = pairs_ref[g * 32 + m * ROWS : g * 32 + (m + 1) * ROWS, :]
        rows += [jnp.where(of_quarter[q], part, 0.0) for q in range(4)]
    return jnp.concatenate(rows, axis=0).astype(BF16)


def grad_right_kernel(half):
    def kernel(pairs_ref, *refs):
        left_refs, out_refs = refs[:4], refs[-4:]
        of_quarter = quarters()
        for g in range(GROUPS // 2):
            spread = spread_group(pairs_ref, half * GROUPS // 2 + g, of_quarter)
            grad = dot(spread, slab(left_refs, half * GROUPS // 2 + g), TN).astype(BF16)
            for n in range(4):
                out_refs[n][g * 32 : (g + 1) * 32, :] = grad[n * 32 : (n + 1) * 32]

    return kernel


def grad_left_kernel(pairs_ref, *refs):
    right_refs, lefts = refs[:4], refs[5:]
    of_quarter = quarters()
    for g in range(GROUPS):
        spread = spread_group(pairs_ref, g, of_quarter)
        grad = dot(spread, slab(right_refs, g), NN).astype(BF16)
        for m, ref in enumerate(lefts):
            ref[g * 32 : (g + 1) * 32, :] = grad[m * 32 : (m + 1) * 32]


def halves_kernel(x_ref, first_ref, second_ref):
    first_ref[...] = x_ref[: SIDE // 2, :]
    second_ref[...] = x_ref[SIDE // 2 :, :]


def pass_kernel(message_ref, *refs):
    refs[-1][...] = message_ref[...]


def join_kernel(mine_ref, got_ref, both_ref):
    both_ref[:HEAD, :] = mine_ref[...]
    both_ref[HEAD:, :] = got_ref[HEAD:, :]


def add_kernel(mine_ref, got_ref, *refs):
    sum_ref = refs[-1]
    sum_ref[...] = (mine_ref[...].astype(F32) + got_ref[...].astype(F32)).astype(BF16)


def early_kernel(mine_ref, got_ref, sum_ref):
    sum_ref[...] = mine_ref[...].astype(F32) + got_ref[:SIDE, :].astype(F32)


def near_kernel(first_ref, second_ref, *refs):
    both_ref = refs[-1]
    both_ref[: SIDE // 2, :] = first_ref[...]
    both_ref[SIDE // 2 :, :] = second_ref[...]


def back_kernel(left_ref, own_ref, far_ref, after_ref, both_ref):
    both_ref[:SIDE, :] = left_ref[...]
    both_ref[SIDE : SIDE + PIECE, :] = own_ref[...]
    both_ref[SIDE + PIECE :, :] = far_ref[PIECE:, :]


def factor_kernel(
    x_ref,
    cot_ref,
    mask_ref,
    weight_ref,
    params_ref,
    weight_t_ref,
    factor_ref,
    normed_ref,
    inverse_ref,
    open_ref,
    gain_t_ref,
):
    gain_t = jnp.broadcast_to(params_ref[0:1, :], (128, 128)).T
    bias_t = jnp.broadcast_to(params_ref[1:2, :], (128, 128)).T
    gain_t_ref[...] = gain_t
    scaled = scale_in(x_ref[...], params_ref).astype(BF16)
    gate_sig = sigmoid(dot(scaled, weight_ref[:, 512:640], NN)).reshape(cot_ref.shape)
    open_ref[...] = cot_ref[...].astype(F32) * (1.0 - gate_sig)
    for row in range(ROWS):
        x = x_ref[row * 128 : (row + 1) * 128, :]
        normed, inverse = norm(x.astype(F32).T, 0)
        normed_ref[row] = normed
        inverse_ref[row : row + 1, :] = inverse
        scaled = (normed * gain_t + bias_t).astype(BF16)
        projected = dot(weight_t_ref[...], scaled, NN)
        keep = mask_ref[row : row + 1].astype(F32)
        for side in range(2):
            base = 256 * side
            gate = sigmoid(projected[base : base + 128])
            value = projected[base + 128 : base + 256]
            factor_ref[row, base : base + 128, :] = keep * value * gate * (1.0 - gate)
            factor_ref[row, base + 128 : base + 256, :] = keep * gate


def out_kernel(me_ref, own_ref, near_ref, far_ref, open_ref, weight_ref, out_ref, grad_ref, full_ref):
    places = [(own_ref, 0), (near_ref, SIDE), (far_ref, 0), (near_ref, SIDE + PIECE)]
    for (ref, at), offset in zip(places, LEFT_OFFSETS):
        piece = ref[at : at + PIECE, :].astype(F32).reshape(ROWS, 4, ROWS, 128)
        for n, start in enumerate(columns_of(me_ref[0] ^ offset, RIGHT_OFFSETS)):
            full_ref[:, pl.ds(start, ROWS), :] = piece[:, n]
    for row in range(ROWS):
        out = full_ref[row]
        out_ref[row] = out.astype(BF16)
        grad_gate = (open_ref[row] * out).astype(BF16)
        grad_ref[row] = dot(weight_ref[:, 512:640], grad_gate, NT)


def right_terms(rows_ref, factor_ref, row, half):
    parts = []
    nothing = jnp.zeros((16, 128), BF16)
    for place in (256, 384):
        for q in range(4):
            grad = rows_ref[pl.ds(q * ROWS + row, 16, stride=4 * ROWS), :]
            at = place + q * 32 + half * 16
            term = (grad * factor_ref[row, at : at + 16, :]).astype(BF16)
            parts += [nothing, term] if half else [term, nothing]
    return jnp.concatenate(parts, axis=0)


def partial_kernel(*refs):
    left_ref, left_got_ref, own_ref, near_ref, got_ref = refs[:5]
    factor_ref, gate_ref, weight_ref, sum_ref, left_rows, right_rows = refs[5:]
    left_rows[...] = left_ref[...] + left_got_ref[...].astype(F32)
    right = own_ref[...].astype(F32) + near_ref[: SIDE // 2, :].astype(F32)
    right_rows[...] = right + got_ref[...].astype(F32)
    for row in range(ROWS):
        grad = load_side(left_rows, row)
        parts = [(grad * factor_ref[row, a : a + 128, :]).astype(BF16) for a in (0, 128)]
        parts.append(right_terms(right_rows, factor_ref, row, 0))
        grad_projected = jnp.concatenate(parts, axis=0)
        sum_ref[row] = dot(weight_ref[:, :512], grad_projected, NN) + gate_ref[row]


def pair_kernel(
    own_ref,
    near_ref,
    got_ref,
    factor_ref,
    sum_ref,
    normed_ref,
    inverse_ref,
    gain_t_ref,
    weight_ref,
    out_ref,
    right_rows,
):
    right = own_ref[...].astype(F32) + near_ref[SIDE // 2 :, :].astype(F32)
    right_rows[...] = right + got_ref[...].astype(F32)
    for row in range(ROWS):
        terms = right_terms(right_rows, factor_ref, row, 1)
        grad_scaled = dot(weight_ref[:, 256:512], terms, NN) + sum_ref[row]
        normed = normed_ref[row]
        grad_hat = grad_scaled * gain_t_ref[...]
        first = jnp.mean(grad_hat, axis=0, keepdims=True)
        second = jnp.mean(grad_hat * normed, axis=0, keepdims=True)
        grad = inverse_ref[row : row + 1, :] * (grad_hat - first - normed * second)
        out_ref[row] = grad.T.astype(BF16)


def swap(values, offset):
    return lax.ppermute(values, "row", [(s, s ^ offset) for s in range(16)])


def blocks_device(
    pair_rep,
    pair_mask,
    cotangent,
    in_gain,
    in_bias,
    proj_weight,
    gate_weight,
    mid_gain,
    mid_bias,
    out_weight,
):
    me = lax.axis_index("row").astype(jnp.int32).reshape(1)
    half = SIDE // 2
    cube = (ROWS, 128, 128)
    side, piece = ((SIDE, 128), BF16), ((PIECE, 128), BF16)
    halves, core = ((half, 128), BF16), ((SIDE + 2 * PIECE, 128), BF16)
    sig = ((PIECE, 128), F32)
    rows_scratch = pltpu.VMEM((2, SIDE, 128), F32)
    cube_scratch = pltpu.VMEM(cube, F32)

    def after(message, *others):
        return call(pass_kernel, [(message.shape, BF16)], vmem=[message, *others])[0]

    flat = pair_rep.reshape(SIDE, 128)
    weights = jnp.zeros((), BF16)
    for at, weight in ((0, proj_weight), (512, gate_weight), (640, out_weight)):
        weights = weights + jnp.pad(weight, ((0, 0), (at, 768 - at - weight.shape[1])))
    params = jnp.stack([in_gain, in_bias, mid_gain, mid_bias])

    first, second = call(halves_kernel, [halves] * 2, vmem=[flat])
    z_first, z_second = swap(first, Z_HIGH), swap(second, Z_HIGH)
    whole = after(flat, second)
    far = swap(whole, Z_LOW)
    x_near = swap(whole, CHIP_X)
    near = swap(whole, CORE)
    left_0, right_0, sig_0, weight_t, block_weight, mid = call(
        own_kernel,
        [side, side, sig, ((512, 128), BF16), ((512, 512), BF16), ((ROWS, 512), F32)],
        smem=[me],
        vmem=[whole, weights, params],
        scratch=[rows_scratch, cube_scratch],
        weight=WAIT,
    )

    def peer(*messages):
        return call(
            peer_kernel,
            [side, side, sig],
            smem=[me],
            vmem=[*messages, weight_t, weights, params],
            scratch=[rows_scratch, cube_scratch],
            weight=WAIT,
        )

    left_1, right_1, sig_1 = peer(near, x_near)
    own_piece, core_piece, far_piece = call(
        pack_kernel,
        [((HEAD, 128), BF16), ((HEAD, 128), BF16), ((2 * HEAD, 128), BF16)],
        smem=[me],
        vmem=[cotangent, pair_mask, x_near],
        scratch=[cube_scratch],
    )
    far_got = swap(far_piece, Z_LOW)
    both = swap(far, CORE)
    x_second = swap(after(z_second, left_0), CHIP_X)
    x_first = swap(after(z_first, x_second, left_0), CHIP_X)
    (joined,) = call(join_kernel, [((2 * HEAD, 128), BF16)], vmem=[core_piece, far_got])
    core_pieces = swap(joined, CORE)
    left_2, right_2, sig_2 = peer(far, z_first, z_second)
    left_3, sig_3 = call(
        left_kernel,
        [side, sig],
        smem=[me],
        vmem=[both, weight_t, weights, params],
        scratch=[pltpu.VMEM((SIDE, 128), F32), cube_scratch],
        weight=WAIT,
    )

    def right_half(first, last, *operands):
        return call(
            right_kernel(first, last),
            [((SIDE, 128), BF16 if last else F32)],
            vmem=operands,
            scratch=[pltpu.VMEM((SIDE, 128), F32)],
            weight=WAIT // 4,
        )[0]

    right_part = right_half(ROWS // 2, False, x_second, weight_t, params, left_3)
    right_3 = right_half(0, True, x_first, weight_t, params, right_part)

    lefts, rights = [left_0, left_1, left_2, left_3], [right_0, right_1, right_2, right_3]
    out_0, out_1, out_far, pairs = call(
        block_kernel,
        [piece, piece, ((2 * PIECE, 128), BF16), ((SIDE, 128), F32)],
        smem=[me],
        vmem=lefts
        + rights
        + [sig_0, sig_1, sig_2, sig_3]
        + [own_piece, core_pieces, far_got, block_weight, mid],
    )
    out_far = swap(out_far, Z_LOW)
    right_a = call(grad_right_kernel(0), [halves] * 4, vmem=[pairs, *lefts])
    x_got = [swap(right_a[3], CHIP_X)]
    left_parts = call(
        grad_left_kernel, [side] * 4, vmem=[pairs, *rights, right_a[3]]
    )
    both_got = swap(left_parts[3], CORE)
    (left_sum,) = call(add_kernel, [side], vmem=[left_parts[2], both_got])
    left_got = swap(left_sum, Z_LOW)
    (total,) = call(add_kernel, [halves], vmem=[right_a[2], x_got[0], left_sum])
    z_got = [swap(total, Z_HIGH)]
    right_b = call(grad_right_kernel(1), [halves] * 4, vmem=[pairs, *lefts], weight=WAIT)
    x_got.append(swap(after(right_b[3], left_sum), CHIP_X))
    (total,) = call(add_kernel, [halves], vmem=[right_b[2], x_got[1], left_sum])
    z_got.append(swap(total, Z_HIGH))
    (near_back,) = call(back_kernel, [core], vmem=[left_parts[1], out_1, out_far, total])
    near_got = swap(near_back, CORE)
    (left_part,) = call(early_kernel, [((SIDE, 128), F32)], vmem=[left_parts[0], near_got])
    (right_back,) = call(near_kernel, [side], vmem=[right_a[1], right_b[1], total])
    right_near = swap(right_back, CHIP_X)

    factors, normed, inverse, open_part, gain_t = call(
        factor_kernel,
        [((ROWS, 512, 128), F32), (cube, F32), ((ROWS, 128), F32), (cube, F32), ((128, 128), F32)],
        vmem=[whole, cotangent, pair_mask, weights, params, weight_t],
        weight=WAIT,
    )
    output, gate_part = call(
        out_kernel,
        [(cube, BF16), (cube, F32)],
        smem=[me],
        vmem=[out_0, near_got, out_far, open_part, weights],
        scratch=[cube_scratch],
    )
    half_scratch = pltpu.VMEM((half, 128), F32)
    (partial,) = call(
        partial_kernel,
        [(cube, F32)],
        vmem=[left_part, left_got, right_a[0], right_near, z_got[0]]
        + [factors, gate_part, weights],
        scratch=[pltpu.VMEM((SIDE, 128), F32), half_scratch],
        weight=WAIT // 4,
    )
    (grad_pair,) = call(
        pair_kernel,
        [(cube, BF16)],
        vmem=[right_b[0], right_near, z_got[1]]
        + [factors, partial, normed, inverse, gain_t, weights],
        scratch=[half_scratch],
    )
    return (output, grad_pair)


def norm_stats(values, reduce_axis):
    center = values - jnp.mean(values, axis=reduce_axis, keepdims=True)
    inverse = lax.rsqrt(jnp.mean(center * center, axis=reduce_axis, keepdims=True) + EPSILON)
    return (center * inverse, inverse)


def norm_back(grad_hat, normed, inverse, reduce_axis):
    first = jnp.mean(grad_hat, axis=reduce_axis, keepdims=True)
    second = jnp.mean(grad_hat * normed, axis=reduce_axis, keepdims=True)
    return inverse * (grad_hat - first - normed * second)


def forward_products(left_chan, right_chan):
    return jnp.einsum("hik,hjk->hij", left_chan, right_chan, preferred_element_type=jnp.float32)


def backward_products(grad_full, left_chan, right_chan):
    grad_left = jnp.einsum(
        "hij,hjk->hik", grad_full, right_chan, preferred_element_type=jnp.float32
    )
    grad_right = jnp.einsum(
        "hij,hik->hjk", grad_full, left_chan, preferred_element_type=jnp.float32
    )
    return jnp.stack([grad_left, grad_right]).astype(jnp.bfloat16)


def channels_device(
    pair_rep,
    pair_mask,
    cotangent,
    in_gain,
    in_bias,
    proj_weight,
    gate_weight,
    mid_gain,
    mid_bias,
    out_weight,
):
    width = pair_rep.shape[2]
    hidden = out_weight.shape[0]
    weights_four = proj_weight.reshape(width, 2, 2, hidden)
    mask_float = pair_mask.astype(jnp.float32)
    normed_in, inverse_in = norm_stats(pair_rep.astype(jnp.float32), 2)
    scaled_in = (normed_in * in_gain + in_bias).astype(jnp.bfloat16)
    gate_pre = jnp.einsum(
        "ijc,csh->shij", scaled_in, weights_four[:, :, 0], preferred_element_type=jnp.float32
    )
    value_pre = jnp.einsum(
        "ijc,csh->shij", scaled_in, weights_four[:, :, 1], preferred_element_type=jnp.float32
    )
    sigmoid_gate = jax.nn.sigmoid(gate_pre)
    both_sides = (sigmoid_gate * value_pre * mask_float).astype(jnp.bfloat16)
    gate_sig = jax.nn.sigmoid(
        jnp.einsum("ijc,cd->ijd", scaled_in, gate_weight, preferred_element_type=jnp.float32)
    )
    sides_chan = lax.all_to_all(both_sides, "row", split_axis=1, concat_axis=2, tiled=True)
    partial_sum = forward_products(sides_chan[0], sides_chan[1])
    product = lax.psum_scatter(partial_sum, "col", scatter_dimension=2, tiled=True).astype(
        jnp.bfloat16
    )
    mixed_pair = lax.all_to_all(product, "row", split_axis=1, concat_axis=0, tiled=True)
    normed_mid, inverse_mid = norm_stats(mixed_pair.astype(jnp.float32), 0)
    scaled_mid = (normed_mid * mid_gain[:, None, None] + mid_bias[:, None, None]).astype(
        jnp.bfloat16
    )
    update = jnp.einsum("hij,hc->ijc", scaled_mid, out_weight, preferred_element_type=jnp.float32)
    output = (gate_sig * update).astype(jnp.bfloat16)
    grad_out = cotangent.astype(jnp.float32)
    grad_update = (grad_out * gate_sig).astype(jnp.bfloat16)
    grad_gate = (grad_out * update * gate_sig * (1.0 - gate_sig)).astype(jnp.bfloat16)
    grad_scaled_mid = jnp.einsum(
        "ijc,hc->hij", grad_update, out_weight, preferred_element_type=jnp.float32
    )
    grad_mixed = norm_back(
        grad_scaled_mid * mid_gain[:, None, None], normed_mid, inverse_mid, 0
    ).astype(jnp.bfloat16)
    grad_chan = lax.all_to_all(grad_mixed, "row", split_axis=0, concat_axis=1, tiled=True)
    grad_full = lax.all_gather(grad_chan, "col", axis=2, tiled=True)
    grad_local = backward_products(grad_full, sides_chan[0], sides_chan[1])
    grad_sides = lax.all_to_all(grad_local, "row", split_axis=2, concat_axis=1, tiled=True)
    side_float = grad_sides.astype(jnp.float32) * mask_float
    grad_value = (side_float * sigmoid_gate).astype(jnp.bfloat16)
    grad_gate_pre = (side_float * value_pre * sigmoid_gate * (1.0 - sigmoid_gate)).astype(
        jnp.bfloat16
    )
    grad_scaled = jnp.einsum(
        "shij,csh->ijc", grad_gate_pre, weights_four[:, :, 0], preferred_element_type=jnp.float32
    )
    grad_scaled = grad_scaled + jnp.einsum(
        "shij,csh->ijc", grad_value, weights_four[:, :, 1], preferred_element_type=jnp.float32
    )
    grad_scaled = grad_scaled + jnp.einsum(
        "ijd,cd->ijc", grad_gate, gate_weight, preferred_element_type=jnp.float32
    )
    grad_pair = norm_back(grad_scaled * in_gain, normed_in, inverse_in, 2).astype(jnp.bfloat16)
    return (output, grad_pair)


def solution(mesh):
    blocks = mesh.shape["row"] == 16 and mesh.shape["col"] == 1
    placed = (
        P(("grp", "row"), "col", None),
        P(("grp", "row"), "col"),
        P(("grp", "row"), "col", None),
        P(),
        P(),
        P(),
        P(),
        P(),
        P(),
        P(),
    )
    return jax.shard_map(
        blocks_device if blocks else channels_device,
        mesh=mesh,
        in_specs=placed,
        out_specs=(P(("grp", "row"), "col", None), P(("grp", "row"), "col", None)),
        check_vma=False,
    )
```

```python
import jax
import jax.numpy as jnp
from jax import lax
from jax.experimental import pallas as pl
from jax.experimental.pallas import tpu as pltpu
from jax.sharding import PartitionSpec as P

EPSILON = 1e-05
CORE, CHIP_X, Z_LOW, Z_HIGH = 1, 2, 4, 8
LEFT_OFFSETS = (0, CORE, Z_LOW, Z_LOW | CORE)
RIGHT_OFFSETS = (0, CHIP_X, Z_HIGH, Z_HIGH | CHIP_X)
ROWS = 8
SIDE = 1024
PIECE = 256
HEAD = PIECE + 16
VMEM_BYTES = 48 * 2**20
WAIT = 5 * 10**9

NT = (((1,), (1,)), ((), ()))
NN = (((1,), (0,)), ((), ()))
TN = (((0,), (0,)), ((), ()))
F32, BF16 = jnp.float32, jnp.bfloat16


def dot(a, b, dims):
    return lax.dot_general(a, b, dims, preferred_element_type=F32)


def norm(values, axis):
    center = values - jnp.mean(values, axis=axis, keepdims=True)
    inverse = lax.rsqrt(jnp.mean(center * center, axis=axis, keepdims=True) + EPSILON)
    return center * inverse, inverse


def sigmoid(x):
    return 0.5 * jnp.tanh(0.5 * x) + 0.5


def call(kernel, outs, smem=(), vmem=(), scratch=(), weight=2**26):
    vmem_spec = pl.BlockSpec(memory_space=pltpu.VMEM)
    specs = [pl.BlockSpec(memory_space=pltpu.SMEM)] * len(smem)
    specs += [vmem_spec] * len(vmem)
    return pl.pallas_call(
        kernel,
        out_shape=[jax.ShapeDtypeStruct(s, d) for s, d in outs],
        in_specs=specs,
        out_specs=[vmem_spec] * len(outs),
        scratch_shapes=list(scratch),
        compiler_params=pltpu.CompilerParams(vmem_limit_bytes=VMEM_BYTES),
        cost_estimate=pl.CostEstimate(flops=weight, bytes_accessed=2**18, transcendentals=0),
    )(*smem, *vmem)


def side_rows(quarter, row):
    return pl.ds(quarter * ROWS + row, 32, stride=4 * ROWS)


def store_side(rows_ref, row, result):
    for q in range(4):
        rows_ref[side_rows(q, row), :] = result[q * 32 : (q + 1) * 32]


def load_side(rows_ref, row):
    return jnp.concatenate([rows_ref[side_rows(q, row), :] for q in range(4)], axis=0)


def columns_of(me, offsets):
    return [pl.multiple_of((me ^ o) * ROWS, ROWS) for o in offsets]


def pick_columns(full_ref, starts):
    columns = [full_ref[:, pl.ds(s, ROWS), :] for s in starts]
    return jnp.concatenate(columns, axis=1).reshape(PIECE, 128)


def pack_kernel(me_ref, cot_ref, mask_ref, after_ref, own_ref, core_ref, far_ref, full_ref):
    me = me_ref[0]
    full_ref[...] = cot_ref[...].astype(F32)
    mask = jnp.concatenate([mask_ref[...].astype(F32), jnp.zeros((ROWS, 128), F32)], axis=0)
    places = [(own_ref, 0), (core_ref, 0), (far_ref, 0), (far_ref, HEAD)]
    for (ref, place), offset in zip(places, LEFT_OFFSETS):
        piece = pick_columns(full_ref, columns_of(me ^ offset, RIGHT_OFFSETS))
        ref[place : place + PIECE, :] = piece.astype(BF16)
        ref[place + PIECE : place + HEAD, :] = mask.astype(BF16)


def split_sum(values, ones):
    high = values.astype(BF16)
    low = (values - high.astype(F32)).astype(BF16)
    return dot(high, ones, NN) + dot(low, ones, NN)


def scale_in(x, params_ref):
    return norm(x.astype(F32), 1)[0] * params_ref[0:1, :] + params_ref[1:2, :]


def project(weight_t, scaled, row):
    return dot(weight_t, scaled[row * 128 : (row + 1) * 128], NT)


def make_side(projected):
    return sigmoid(projected[:128]) * projected[128:]


def block_gate(me_ref, scaled_ref, weight_ref):
    picked = pick_columns(scaled_ref, columns_of(me_ref[0], RIGHT_OFFSETS))
    return sigmoid(dot(picked.astype(BF16), weight_ref[:, 512:640], NN))


def own_kernel(
    me_ref,
    x_ref,
    weight_ref,
    params_ref,
    left_ref,
    right_ref,
    sig_ref,
    weight_t_ref,
    block_ref,
    mid_ref,
    rows_ref,
    scaled_ref,
):
    weight_t_ref[...] = weight_ref[:, :512].astype(F32).T.astype(BF16)
    scaled = scale_in(x_ref[...], params_ref)
    scaled_ref[...] = scaled.reshape(scaled_ref.shape)
    scaled = scaled.astype(BF16)
    for row in range(ROWS):
        projected = project(weight_t_ref[...], scaled, row)
        store_side(rows_ref.at[0], row, make_side(projected[:256]))
        store_side(rows_ref.at[1], row, make_side(projected[256:]))
    left_ref[...] = rows_ref[0].astype(BF16)
    right_ref[...] = rows_ref[1].astype(BF16)
    sig_ref[...] = block_gate(me_ref, scaled_ref, weight_ref)

    repeat = lax.broadcasted_iota(jnp.int32, (512, 128), 0)
    lane = lax.broadcasted_iota(jnp.int32, (512, 128), 1)
    spread = jnp.where((repeat >> 2) == lane, 1.0, 0.0).astype(BF16)
    tall = dot(spread, weight_ref[:, 640:], NN)
    for m in range(4):
        block_ref[:, m * 128 : (m + 1) * 128] = jnp.where((repeat & 3) == m, tall, 0.0).astype(BF16)
    rows = lax.broadcasted_iota(jnp.int32, (ROWS, 128), 0)
    both = jnp.where(rows == 0, params_ref[2:3, :], params_ref[3:4, :])
    wide = jnp.zeros((ROWS, 512), F32)
    for _ in range(3):
        term = both.astype(BF16)
        wide = wide + dot(term, spread, NT)
        both = both - term.astype(F32)
    mid_ref[...] = wide


def peer_kernel(me_ref, left_in, *refs):
    right_in, rest = refs[:-8], refs[-8:]
    weight_t_ref, weight_ref, params_ref, left_ref, right_ref, sig_ref, rows_ref, scaled_ref = rest
    scaled = scale_in(left_in[...], params_ref)
    scaled_ref[...] = scaled.reshape(scaled_ref.shape)
    scaled = scaled.astype(BF16)
    for row in range(ROWS):
        projected = project(weight_t_ref[:256, :], scaled, row)
        store_side(rows_ref.at[0], row, make_side(projected))
    scaled = [scale_in(r[...], params_ref).astype(BF16) for r in right_in]
    for row in range(ROWS):
        part, place = divmod(row, ROWS // len(right_in))
        projected = project(weight_t_ref[256:, :], scaled[part], place)
        store_side(rows_ref.at[1], row, make_side(projected))
    left_ref[...] = rows_ref[0].astype(BF16)
    right_ref[...] = rows_ref[1].astype(BF16)
    sig_ref[...] = block_gate(me_ref, scaled_ref, weight_ref)


def left_kernel(
    me_ref, x_ref, weight_t_ref, weight_ref, params_ref, left_ref, sig_ref, rows_ref, scaled_ref
):
    scaled = scale_in(x_ref[...], params_ref)
    scaled_ref[...] = scaled.reshape(scaled_ref.shape)
    scaled = scaled.astype(BF16)
    for row in range(ROWS):
        projected = project(weight_t_ref[:256, :], scaled, row)
        store_side(rows_ref, row, make_side(projected))
    left_ref[...] = rows_ref[...].astype(BF16)
    sig_ref[...] = block_gate(me_ref, scaled_ref, weight_ref)


def right_kernel(first, last):
    def kernel(x_ref, weight_t_ref, params_ref, rest_ref, right_ref, rows_ref):
        if last:
            rows_ref[...] = rest_ref[...]
        else:
            rows_ref[...] = jnp.zeros_like(rows_ref)
        scaled = scale_in(x_ref[...], params_ref).astype(BF16)
        for row in range(ROWS // 2):
            projected = project(weight_t_ref[256:, :], scaled, row)
            store_side(rows_ref, first + row, make_side(projected))
        right_ref[...] = rows_ref[...].astype(right_ref.dtype)

    return kernel


GROUPS = SIDE // 32


def quarters():
    lane = lax.broadcasted_iota(jnp.int32, (ROWS, 128), 1)
    return [((lane >> 3) & 3) == q for q in range(4)]


def slab(side_refs, g):
    return jnp.concatenate([r[g * 32 : (g + 1) * 32, :] for r in side_refs], axis=0)


def block_kernel(*refs):
    me_ref, left_refs, right_refs, sig_refs = refs[0], refs[1:5], refs[5:9], refs[9:13]
    own_ref, core_in, far_in, block_ref, mid_ref = refs[13:18]
    pieces = [(own_ref, 0), (core_in, 0), (far_in, 0), (core_in, HEAD)]
    out_refs, pairs_ref = refs[18:22], refs[22]
    me = me_ref[0]
    of_quarter = quarters()

    masks = [ref[at + PIECE : at + HEAD, :].astype(F32) for ref, at in pieces]
    valid = jnp.max(jnp.concatenate(masks, axis=0), axis=0, keepdims=True)
    src = lax.broadcasted_iota(jnp.int32, (128, 128), 0)
    dst = lax.broadcasted_iota(jnp.int32, (128, 128), 1)
    pick = jnp.zeros((128, 128), F32)
    for n, offset in enumerate(RIGHT_OFFSETS):
        wanted = (me ^ offset) * ROWS + (dst & 7)
        pick = jnp.where((src == wanted) & ((dst >> 5) == n), 1.0, pick)
    spread = jnp.broadcast_to(valid, (ROWS, 128)).astype(BF16)
    column_valid = dot(spread, pick.astype(BF16), NN)
    pair_valid = [jnp.max(k[:ROWS], axis=1, keepdims=True) * column_valid for k in masks]
    valid = jnp.broadcast_to(valid, (128, 128)).astype(BF16)

    for g in range(GROUPS):
        full = dot(slab(left_refs, g) * valid, slab(right_refs, g), NT).reshape(4, 4, ROWS, 128)
        for m in range(4):
            kept = full[m, 3]
            for q in range(3):
                kept = jnp.where(of_quarter[q], full[m, q], kept)
            pairs_ref[g * 32 + m * ROWS : g * 32 + (m + 1) * ROWS, :] = kept * pair_valid[m]

    turned = []
    for row in range(ROWS):
        turn = pairs_ref[pl.ds(row, 128, stride=ROWS), :].T.reshape(4, 4, ROWS, 128)
        turned.append(jnp.concatenate([turn[:, q].reshape(32, 128) for q in range(4)], axis=1))
    mixed = jnp.concatenate(turned, axis=0).astype(BF16).astype(F32)

    ones = jnp.where((src & 3) == (dst & 3), 1.0, 0.0).astype(BF16)

    def channel_mean(values):
        total = values[:, :128] + values[:, 128:256] + values[:, 256:384] + values[:, 384:]
        mean = split_sum(total, ones) * (1.0 / 128.0)
        return jnp.concatenate([mean] * 4, axis=1)

    mid_gain, mid_bias = mid_ref[0:1, :], mid_ref[1:2, :]
    center = mixed - channel_mean(mixed)
    inverse = lax.rsqrt(channel_mean(center * center) + EPSILON)
    normed = center * inverse
    scaled = (normed * mid_gain + mid_bias).astype(BF16)
    update = dot(scaled, block_ref[...], NN)
    grad_update = []
    for m in range(4):
        sig = sig_refs[m][...]
        out = sig * update[:, m * 128 : (m + 1) * 128]
        out_refs[m][...] = out.astype(BF16)
        ref, at = pieces[m]
        cot = ref[at : at + PIECE, :].astype(F32)
        grad_update.append((cot * sig).astype(BF16))
    grad_hat = dot(jnp.concatenate(grad_update, axis=1), block_ref[...], NT) * mid_gain
    first = channel_mean(grad_hat)
    second = channel_mean(grad_hat * normed)
    grad_mixed = inverse * (grad_hat - first - normed * second)

    mask = jnp.concatenate(pair_valid, axis=0)
    for row in range(ROWS):
        part = grad_mixed[row * 32 : (row + 1) * 32]
        parts = [part[:, q * 128 : (q + 1) * 128].reshape(4, 1, ROWS, 128) for q in range(4)]
        turn = jnp.concatenate(parts, axis=1).reshape(128, 128)
        pairs_ref[pl.ds(row, 128, stride=ROWS), :] = turn.T
    for g in range(GROUPS):
        pairs_ref[g * 32 : (g + 1) * 32, :] = pairs_ref[g * 32 : (g + 1) * 32, :] * mask


def spread_group(pairs_ref, g, of_quarter):
    rows = []
    for m in range(4):
        part = pairs_ref[g * 32 + m * ROWS : g * 32 + (m + 1) * ROWS, :]
        rows += [jnp.where(of_quarter[q], part, 0.0) for q in range(4)]
    return jnp.concatenate(rows, axis=0).astype(BF16)


def grad_right_kernel(half):
    def kernel(pairs_ref, *refs):
        left_refs, out_refs = refs[:4], refs[4:]
        of_quarter = quarters()
        for g in range(GROUPS // 2):
            spread = spread_group(pairs_ref, half * GROUPS // 2 + g, of_quarter)
            grad = dot(spread, slab(left_refs, half * GROUPS // 2 + g), TN).astype(BF16)
            for n in range(4):
                out_refs[n][g * 32 : (g + 1) * 32, :] = grad[n * 32 : (n + 1) * 32]

    return kernel


def grad_left_kernel(pairs_ref, *refs):
    right_refs, (out_near, out_both), lefts = refs[:4], refs[4:6], refs[7:]
    of_quarter = quarters()
    for g in range(GROUPS):
        spread = spread_group(pairs_ref, g, of_quarter)
        grad = dot(spread, slab(right_refs, g), NN).astype(BF16)
        for m, ref in enumerate(lefts):
            ref[g * 32 : (g + 1) * 32, :] = grad[m * 32 : (m + 1) * 32]
    lefts[1][SIDE:, :] = out_near[...]
    lefts[3][SIDE:, :] = out_both[...]


def halves_kernel(x_ref, first_ref, second_ref):
    first_ref[...] = x_ref[: SIDE // 2, :]
    second_ref[...] = x_ref[SIDE // 2 :, :]


def pass_kernel(message_ref, *refs):
    refs[-1][...] = message_ref[...]


def join_kernel(mine_ref, got_ref, both_ref):
    both_ref[:HEAD, :] = mine_ref[...]
    both_ref[HEAD:, :] = got_ref[HEAD:, :]


def add_kernel(mine_ref, got_ref, *refs):
    sum_ref = refs[-1]
    sum_ref[...] = (mine_ref[...].astype(F32) + got_ref[...].astype(F32)).astype(BF16)


def near_kernel(first_ref, second_ref, after_ref, both_ref):
    both_ref[: SIDE // 2, :] = first_ref[...]
    both_ref[SIDE // 2 :, :] = second_ref[...]


def add_left_kernel(mine_ref, piece_ref, got_ref, sum_ref, out_ref):
    sum_ref[...] = (mine_ref[...].astype(F32) + got_ref[:SIDE, :].astype(F32)).astype(BF16)
    out_ref[:PIECE, :] = piece_ref[...]
    out_ref[PIECE:, :] = got_ref[SIDE:, :]


def factor_kernel(
    x_ref,
    cot_ref,
    mask_ref,
    weight_ref,
    params_ref,
    weight_t_ref,
    factor_ref,
    normed_ref,
    inverse_ref,
    open_ref,
    gain_t_ref,
):
    gain_t = jnp.broadcast_to(params_ref[0:1, :], (128, 128)).T
    bias_t = jnp.broadcast_to(params_ref[1:2, :], (128, 128)).T
    gain_t_ref[...] = gain_t
    scaled = scale_in(x_ref[...], params_ref).astype(BF16)
    gate_sig = sigmoid(dot(scaled, weight_ref[:, 512:640], NN)).reshape(cot_ref.shape)
    open_ref[...] = cot_ref[...].astype(F32) * (1.0 - gate_sig)
    for row in range(ROWS):
        x = x_ref[row * 128 : (row + 1) * 128, :]
        normed, inverse = norm(x.astype(F32).T, 0)
        normed_ref[row] = normed
        inverse_ref[row : row + 1, :] = inverse
        scaled = (normed * gain_t + bias_t).astype(BF16)
        projected = dot(weight_t_ref[...], scaled, NN)
        keep = mask_ref[row : row + 1].astype(F32)
        for side in range(2):
            base = 256 * side
            gate = sigmoid(projected[base : base + 128])
            value = projected[base + 128 : base + 256]
            factor_ref[row, base : base + 128, :] = keep * value * gate * (1.0 - gate)
            factor_ref[row, base + 128 : base + 256, :] = keep * gate


def out_kernel(me_ref, own_ref, near_ref, far_ref, open_ref, weight_ref, out_ref, grad_ref, full_ref):
    places = [(own_ref, 0), (near_ref, SIDE), (far_ref, 0), (far_ref, PIECE)]
    for (ref, at), offset in zip(places, LEFT_OFFSETS):
        piece = ref[at : at + PIECE, :].astype(F32).reshape(ROWS, 4, ROWS, 128)
        for n, start in enumerate(columns_of(me_ref[0] ^ offset, RIGHT_OFFSETS)):
            full_ref[:, pl.ds(start, ROWS), :] = piece[:, n]
    for row in range(ROWS):
        out = full_ref[row]
        out_ref[row] = out.astype(BF16)
        grad_gate = (open_ref[row] * out).astype(BF16)
        grad_ref[row] = dot(weight_ref[:, 512:640], grad_gate, NT)


def right_terms(rows_ref, factor_ref, row, half):
    parts = []
    nothing = jnp.zeros((16, 128), BF16)
    for place in (256, 384):
        for q in range(4):
            grad = rows_ref[pl.ds(q * ROWS + row, 16, stride=4 * ROWS), :]
            at = place + q * 32 + half * 16
            term = (grad * factor_ref[row, at : at + 16, :]).astype(BF16)
            parts += [nothing, term] if half else [term, nothing]
    return jnp.concatenate(parts, axis=0)


def partial_kernel(*refs):
    left_refs, (own_ref, near_ref, got_ref) = refs[0:3], refs[3:6]
    factor_ref, gate_ref, weight_ref, sum_ref, left_rows, right_rows = refs[6:]
    left = [r[:SIDE, :].astype(F32) for r in left_refs]
    left_rows[...] = left[0] + left[1] + left[2]
    right = own_ref[...].astype(F32) + near_ref[: SIDE // 2, :].astype(F32)
    right_rows[...] = right + got_ref[...].astype(F32)
    for row in range(ROWS):
        grad = load_side(left_rows, row)
        parts = [(grad * factor_ref[row, a : a + 128, :]).astype(BF16) for a in (0, 128)]
        parts.append(right_terms(right_rows, factor_ref, row, 0))
        grad_projected = jnp.concatenate(parts, axis=0)
        sum_ref[row] = dot(weight_ref[:, :512], grad_projected, NN) + gate_ref[row]


def pair_kernel(
    own_ref,
    near_ref,
    got_ref,
    factor_ref,
    sum_ref,
    normed_ref,
    inverse_ref,
    gain_t_ref,
    weight_ref,
    out_ref,
    right_rows,
):
    right = own_ref[...].astype(F32) + near_ref[SIDE // 2 :, :].astype(F32)
    right_rows[...] = right + got_ref[...].astype(F32)
    for row in range(ROWS):
        terms = right_terms(right_rows, factor_ref, row, 1)
        grad_scaled = dot(weight_ref[:, 256:512], terms, NN) + sum_ref[row]
        normed = normed_ref[row]
        grad_hat = grad_scaled * gain_t_ref[...]
        first = jnp.mean(grad_hat, axis=0, keepdims=True)
        second = jnp.mean(grad_hat * normed, axis=0, keepdims=True)
        grad = inverse_ref[row : row + 1, :] * (grad_hat - first - normed * second)
        out_ref[row] = grad.T.astype(BF16)


def swap(values, offset):
    return lax.ppermute(values, "row", [(s, s ^ offset) for s in range(16)])


def blocks_device(
    pair_rep,
    pair_mask,
    cotangent,
    in_gain,
    in_bias,
    proj_weight,
    gate_weight,
    mid_gain,
    mid_bias,
    out_weight,
):
    me = lax.axis_index("row").astype(jnp.int32).reshape(1)
    half = SIDE // 2
    cube = (ROWS, 128, 128)
    side, piece = ((SIDE, 128), BF16), ((PIECE, 128), BF16)
    halves, core = ((half, 128), BF16), ((SIDE + PIECE, 128), BF16)
    sig = ((PIECE, 128), F32)
    rows_scratch = pltpu.VMEM((2, SIDE, 128), F32)
    cube_scratch = pltpu.VMEM(cube, F32)

    def after(message, *others):
        return call(pass_kernel, [(message.shape, BF16)], vmem=[message, *others])[0]

    flat = pair_rep.reshape(SIDE, 128)
    weights = jnp.zeros((), BF16)
    for at, weight in ((0, proj_weight), (512, gate_weight), (640, out_weight)):
        weights = weights + jnp.pad(weight, ((0, 0), (at, 768 - at - weight.shape[1])))
    params = jnp.stack([in_gain, in_bias, mid_gain, mid_bias])

    first, second = call(halves_kernel, [halves] * 2, vmem=[flat])
    z_first, z_second = swap(first, Z_HIGH), swap(second, Z_HIGH)
    whole = after(flat, second)
    far = swap(whole, Z_LOW)
    x_near = swap(whole, CHIP_X)
    near = swap(whole, CORE)
    left_0, right_0, sig_0, weight_t, block_weight, mid = call(
        own_kernel,
        [side, side, sig, ((512, 128), BF16), ((512, 512), BF16), ((ROWS, 512), F32)],
        smem=[me],
        vmem=[whole, weights, params],
        scratch=[rows_scratch, cube_scratch],
        weight=WAIT,
    )

    def peer(*messages):
        return call(
            peer_kernel,
            [side, side, sig],
            smem=[me],
            vmem=[*messages, weight_t, weights, params],
            scratch=[rows_scratch, cube_scratch],
            weight=WAIT,
        )

    left_1, right_1, sig_1 = peer(near, x_near)
    own_piece, core_piece, far_piece = call(
        pack_kernel,
        [((HEAD, 128), BF16), ((HEAD, 128), BF16), ((2 * HEAD, 128), BF16)],
        smem=[me],
        vmem=[cotangent, pair_mask, x_near],
        scratch=[cube_scratch],
    )
    far_got = swap(far_piece, Z_LOW)
    both = swap(far, CORE)
    x_second = swap(z_second, CHIP_X)
    x_first = swap(after(z_first, x_second, left_0), CHIP_X)
    (joined,) = call(join_kernel, [((2 * HEAD, 128), BF16)], vmem=[core_piece, far_got])
    core_pieces = swap(joined, CORE)
    left_2, right_2, sig_2 = peer(far, z_first, z_second)
    left_3, sig_3 = call(
        left_kernel,
        [side, sig],
        smem=[me],
        vmem=[both, weight_t, weights, params],
        scratch=[pltpu.VMEM((SIDE, 128), F32), cube_scratch],
        weight=WAIT,
    )

    def right_half(first, last, *operands):
        return call(
            right_kernel(first, last),
            [((SIDE, 128), BF16 if last else F32)],
            vmem=operands,
            scratch=[pltpu.VMEM((SIDE, 128), F32)],
            weight=WAIT // 4,
        )[0]

    right_part = right_half(ROWS // 2, False, x_second, weight_t, params, left_3)
    right_3 = right_half(0, True, x_first, weight_t, params, right_part)

    lefts, rights = [left_0, left_1, left_2, left_3], [right_0, right_1, right_2, right_3]
    out_0, out_1, out_2, out_3, pairs = call(
        block_kernel,
        [piece] * 4 + [((SIDE, 128), F32)],
        smem=[me],
        vmem=lefts
        + rights
        + [sig_0, sig_1, sig_2, sig_3]
        + [own_piece, core_pieces, far_got, block_weight, mid],
    )
    right_a = call(grad_right_kernel(0), [halves] * 4, vmem=[pairs, *lefts])
    x_got = [swap(right_a[3], CHIP_X)]
    grad_left_0, near_back, grad_left_2, both_back = call(
        grad_left_kernel,
        [side, core, side, core],
        vmem=[pairs, *rights, out_1, out_3, right_a[3]],
    )
    both_got = swap(both_back, CORE)
    right_b = call(grad_right_kernel(1), [halves] * 4, vmem=[pairs, *lefts], weight=WAIT)
    left_sum, out_far = call(
        add_left_kernel,
        [side, ((2 * PIECE, 128), BF16)],
        vmem=[grad_left_2, out_2, both_got],
    )
    x_got.append(swap(after(right_b[3], left_sum), CHIP_X))
    left_got = swap(left_sum, Z_LOW)
    out_far = swap(out_far, Z_LOW)
    (total,) = call(add_kernel, [halves], vmem=[right_a[2], x_got[0], left_sum])
    z_got = [swap(total, Z_HIGH)]
    (total,) = call(add_kernel, [halves], vmem=[right_b[2], x_got[1], left_sum])
    z_got.append(swap(total, Z_HIGH))
    (right_back,) = call(near_kernel, [side], vmem=[right_a[1], right_b[1], total])
    right_near = swap(right_back, CHIP_X)
    near_got = swap(after(near_back, total), CORE)

    factors, normed, inverse, open_part, gain_t = call(
        factor_kernel,
        [((ROWS, 512, 128), F32), (cube, F32), ((ROWS, 128), F32), (cube, F32), ((128, 128), F32)],
        vmem=[whole, cotangent, pair_mask, weights, params, weight_t],
        weight=WAIT,
    )
    output, gate_part = call(
        out_kernel,
        [(cube, BF16), (cube, F32)],
        smem=[me],
        vmem=[out_0, near_got, out_far, open_part, weights],
        scratch=[cube_scratch],
    )
    half_scratch = pltpu.VMEM((half, 128), F32)
    (partial,) = call(
        partial_kernel,
        [(cube, F32)],
        vmem=[grad_left_0, near_got, left_got, right_a[0], right_near, z_got[0]]
        + [factors, gate_part, weights],
        scratch=[pltpu.VMEM((SIDE, 128), F32), half_scratch],
        weight=WAIT // 4,
    )
    (grad_pair,) = call(
        pair_kernel,
        [(cube, BF16)],
        vmem=[right_b[0], right_near, z_got[1]]
        + [factors, partial, normed, inverse, gain_t, weights],
        scratch=[half_scratch],
    )
    return (output, grad_pair)


def norm_stats(values, reduce_axis):
    center = values - jnp.mean(values, axis=reduce_axis, keepdims=True)
    inverse = lax.rsqrt(jnp.mean(center * center, axis=reduce_axis, keepdims=True) + EPSILON)
    return (center * inverse, inverse)


def norm_back(grad_hat, normed, inverse, reduce_axis):
    first = jnp.mean(grad_hat, axis=reduce_axis, keepdims=True)
    second = jnp.mean(grad_hat * normed, axis=reduce_axis, keepdims=True)
    return inverse * (grad_hat - first - normed * second)


def forward_products(left_chan, right_chan):
    return jnp.einsum("hik,hjk->hij", left_chan, right_chan, preferred_element_type=jnp.float32)


def backward_products(grad_full, left_chan, right_chan):
    grad_left = jnp.einsum(
        "hij,hjk->hik", grad_full, right_chan, preferred_element_type=jnp.float32
    )
    grad_right = jnp.einsum(
        "hij,hik->hjk", grad_full, left_chan, preferred_element_type=jnp.float32
    )
    return jnp.stack([grad_left, grad_right]).astype(jnp.bfloat16)


def channels_device(
    pair_rep,
    pair_mask,
    cotangent,
    in_gain,
    in_bias,
    proj_weight,
    gate_weight,
    mid_gain,
    mid_bias,
    out_weight,
):
    width = pair_rep.shape[2]
    hidden = out_weight.shape[0]
    weights_four = proj_weight.reshape(width, 2, 2, hidden)
    mask_float = pair_mask.astype(jnp.float32)
    normed_in, inverse_in = norm_stats(pair_rep.astype(jnp.float32), 2)
    scaled_in = (normed_in * in_gain + in_bias).astype(jnp.bfloat16)
    gate_pre = jnp.einsum(
        "ijc,csh->shij", scaled_in, weights_four[:, :, 0], preferred_element_type=jnp.float32
    )
    value_pre = jnp.einsum(
        "ijc,csh->shij", scaled_in, weights_four[:, :, 1], preferred_element_type=jnp.float32
    )
    sigmoid_gate = jax.nn.sigmoid(gate_pre)
    both_sides = (sigmoid_gate * value_pre * mask_float).astype(jnp.bfloat16)
    gate_sig = jax.nn.sigmoid(
        jnp.einsum("ijc,cd->ijd", scaled_in, gate_weight, preferred_element_type=jnp.float32)
    )
    sides_chan = lax.all_to_all(both_sides, "row", split_axis=1, concat_axis=2, tiled=True)
    partial_sum = forward_products(sides_chan[0], sides_chan[1])
    product = lax.psum_scatter(partial_sum, "col", scatter_dimension=2, tiled=True).astype(
        jnp.bfloat16
    )
    mixed_pair = lax.all_to_all(product, "row", split_axis=1, concat_axis=0, tiled=True)
    normed_mid, inverse_mid = norm_stats(mixed_pair.astype(jnp.float32), 0)
    scaled_mid = (normed_mid * mid_gain[:, None, None] + mid_bias[:, None, None]).astype(
        jnp.bfloat16
    )
    update = jnp.einsum("hij,hc->ijc", scaled_mid, out_weight, preferred_element_type=jnp.float32)
    output = (gate_sig * update).astype(jnp.bfloat16)
    grad_out = cotangent.astype(jnp.float32)
    grad_update = (grad_out * gate_sig).astype(jnp.bfloat16)
    grad_gate = (grad_out * update * gate_sig * (1.0 - gate_sig)).astype(jnp.bfloat16)
    grad_scaled_mid = jnp.einsum(
        "ijc,hc->hij", grad_update, out_weight, preferred_element_type=jnp.float32
    )
    grad_mixed = norm_back(
        grad_scaled_mid * mid_gain[:, None, None], normed_mid, inverse_mid, 0
    ).astype(jnp.bfloat16)
    grad_chan = lax.all_to_all(grad_mixed, "row", split_axis=0, concat_axis=1, tiled=True)
    grad_full = lax.all_gather(grad_chan, "col", axis=2, tiled=True)
    grad_local = backward_products(grad_full, sides_chan[0], sides_chan[1])
    grad_sides = lax.all_to_all(grad_local, "row", split_axis=2, concat_axis=1, tiled=True)
    side_float = grad_sides.astype(jnp.float32) * mask_float
    grad_value = (side_float * sigmoid_gate).astype(jnp.bfloat16)
    grad_gate_pre = (side_float * value_pre * sigmoid_gate * (1.0 - sigmoid_gate)).astype(
        jnp.bfloat16
    )
    grad_scaled = jnp.einsum(
        "shij,csh->ijc", grad_gate_pre, weights_four[:, :, 0], preferred_element_type=jnp.float32
    )
    grad_scaled = grad_scaled + jnp.einsum(
        "shij,csh->ijc", grad_value, weights_four[:, :, 1], preferred_element_type=jnp.float32
    )
    grad_scaled = grad_scaled + jnp.einsum(
        "ijd,cd->ijc", grad_gate, gate_weight, preferred_element_type=jnp.float32
    )
    grad_pair = norm_back(grad_scaled * in_gain, normed_in, inverse_in, 2).astype(jnp.bfloat16)
    return (output, grad_pair)


def solution(mesh):
    blocks = mesh.shape["row"] == 16 and mesh.shape["col"] == 1
    placed = (
        P(("grp", "row"), "col", None),
        P(("grp", "row"), "col"),
        P(("grp", "row"), "col", None),
        P(),
        P(),
        P(),
        P(),
        P(),
        P(),
        P(),
    )
    return jax.shard_map(
        blocks_device if blocks else channels_device,
        mesh=mesh,
        in_specs=placed,
        out_specs=(P(("grp", "row"), "col", None), P(("grp", "row"), "col", None)),
        check_vma=False,
    )
```

```python
import jax
import jax.numpy as jnp
from jax import lax
from jax.experimental import pallas as pl
from jax.experimental.pallas import tpu as pltpu
from jax.sharding import PartitionSpec as P

EPSILON = 1e-05
CORE, CHIP_X, Z_LOW, Z_HIGH = 1, 2, 4, 8
LEFT_OFFSETS = (0, CORE, Z_LOW, Z_LOW | CORE)
RIGHT_OFFSETS = (0, CHIP_X, Z_HIGH, Z_HIGH | CHIP_X)
ROWS = 8
SIDE = 1024
PIECE = 256
HEAD = PIECE + 16
VMEM_BYTES = 48 * 2**20
WAIT = 5 * 10**9

NT = (((1,), (1,)), ((), ()))
NN = (((1,), (0,)), ((), ()))
TN = (((0,), (0,)), ((), ()))
F32, BF16 = jnp.float32, jnp.bfloat16


def dot(a, b, dims):
    return lax.dot_general(a, b, dims, preferred_element_type=F32)


def norm(values, axis):
    center = values - jnp.mean(values, axis=axis, keepdims=True)
    inverse = lax.rsqrt(jnp.mean(center * center, axis=axis, keepdims=True) + EPSILON)
    return center * inverse, inverse


def sigmoid(x):
    return 0.5 * jnp.tanh(0.5 * x) + 0.5


def call(kernel, outs, smem=(), vmem=(), scratch=(), weight=2**26):
    vmem_spec = pl.BlockSpec(memory_space=pltpu.VMEM)
    specs = [pl.BlockSpec(memory_space=pltpu.SMEM)] * len(smem)
    specs += [vmem_spec] * len(vmem)
    return pl.pallas_call(
        kernel,
        out_shape=[jax.ShapeDtypeStruct(s, d) for s, d in outs],
        in_specs=specs,
        out_specs=[vmem_spec] * len(outs),
        scratch_shapes=list(scratch),
        compiler_params=pltpu.CompilerParams(vmem_limit_bytes=VMEM_BYTES),
        cost_estimate=pl.CostEstimate(flops=weight, bytes_accessed=2**18, transcendentals=0),
    )(*smem, *vmem)


def side_rows(quarter, row):
    return pl.ds(quarter * ROWS + row, 32, stride=4 * ROWS)


def store_side(rows_ref, row, result):
    for q in range(4):
        rows_ref[side_rows(q, row), :] = result[q * 32 : (q + 1) * 32]


def load_side(rows_ref, row):
    return jnp.concatenate([rows_ref[side_rows(q, row), :] for q in range(4)], axis=0)


def columns_of(me, offsets):
    return [pl.multiple_of((me ^ o) * ROWS, ROWS) for o in offsets]


def pick_columns(full_ref, starts):
    columns = [full_ref[:, pl.ds(s, ROWS), :] for s in starts]
    return jnp.concatenate(columns, axis=1).reshape(PIECE, 128)


def pack_kernel(me_ref, cot_ref, mask_ref, after_ref, own_ref, core_ref, far_ref, full_ref):
    me = me_ref[0]
    full_ref[...] = cot_ref[...].astype(F32)
    mask = jnp.concatenate([mask_ref[...].astype(F32), jnp.zeros((ROWS, 128), F32)], axis=0)
    places = [(own_ref, 0), (core_ref, 0), (far_ref, 0), (far_ref, HEAD)]
    for (ref, place), offset in zip(places, LEFT_OFFSETS):
        piece = pick_columns(full_ref, columns_of(me ^ offset, RIGHT_OFFSETS))
        ref[place : place + PIECE, :] = piece.astype(BF16)
        ref[place + PIECE : place + HEAD, :] = mask.astype(BF16)


def split_sum(values, ones):
    high = values.astype(BF16)
    low = (values - high.astype(F32)).astype(BF16)
    return dot(high, ones, NN) + dot(low, ones, NN)


def scale_in(x, params_ref):
    return norm(x.astype(F32), 1)[0] * params_ref[0:1, :] + params_ref[1:2, :]


def project(weight_t, scaled, row):
    return dot(weight_t, scaled[row * 128 : (row + 1) * 128], NT)


def make_side(projected):
    return sigmoid(projected[:128]) * projected[128:]


def block_gate(me_ref, scaled_ref, weight_ref):
    picked = pick_columns(scaled_ref, columns_of(me_ref[0], RIGHT_OFFSETS))
    return sigmoid(dot(picked.astype(BF16), weight_ref[:, 512:640], NN))


def own_kernel(
    me_ref,
    x_ref,
    weight_ref,
    params_ref,
    left_ref,
    right_ref,
    sig_ref,
    weight_t_ref,
    block_ref,
    mid_ref,
    rows_ref,
    scaled_ref,
):
    weight_t_ref[...] = weight_ref[:, :512].astype(F32).T.astype(BF16)
    scaled = scale_in(x_ref[...], params_ref)
    scaled_ref[...] = scaled.reshape(scaled_ref.shape)
    scaled = scaled.astype(BF16)
    for row in range(ROWS):
        projected = project(weight_t_ref[...], scaled, row)
        store_side(rows_ref.at[0], row, make_side(projected[:256]))
        store_side(rows_ref.at[1], row, make_side(projected[256:]))
    left_ref[...] = rows_ref[0].astype(BF16)
    right_ref[...] = rows_ref[1].astype(BF16)
    sig_ref[...] = block_gate(me_ref, scaled_ref, weight_ref)

    repeat = lax.broadcasted_iota(jnp.int32, (512, 128), 0)
    lane = lax.broadcasted_iota(jnp.int32, (512, 128), 1)
    spread = jnp.where((repeat >> 2) == lane, 1.0, 0.0).astype(BF16)
    tall = dot(spread, weight_ref[:, 640:], NN)
    for m in range(4):
        block_ref[:, m * 128 : (m + 1) * 128] = jnp.where((repeat & 3) == m, tall, 0.0).astype(BF16)
    rows = lax.broadcasted_iota(jnp.int32, (ROWS, 128), 0)
    both = jnp.where(rows == 0, params_ref[2:3, :], params_ref[3:4, :])
    wide = jnp.zeros((ROWS, 512), F32)
    for _ in range(3):
        term = both.astype(BF16)
        wide = wide + dot(term, spread, NT)
        both = both - term.astype(F32)
    mid_ref[...] = wide


def peer_kernel(me_ref, left_in, *refs):
    right_in, rest = refs[:-8], refs[-8:]
    weight_t_ref, weight_ref, params_ref, left_ref, right_ref, sig_ref, rows_ref, scaled_ref = rest
    scaled = scale_in(left_in[...], params_ref)
    scaled_ref[...] = scaled.reshape(scaled_ref.shape)
    scaled = scaled.astype(BF16)
    for row in range(ROWS):
        projected = project(weight_t_ref[:256, :], scaled, row)
        store_side(rows_ref.at[0], row, make_side(projected))
    scaled = [scale_in(r[...], params_ref).astype(BF16) for r in right_in]
    for row in range(ROWS):
        part, place = divmod(row, ROWS // len(right_in))
        projected = project(weight_t_ref[256:, :], scaled[part], place)
        store_side(rows_ref.at[1], row, make_side(projected))
    left_ref[...] = rows_ref[0].astype(BF16)
    right_ref[...] = rows_ref[1].astype(BF16)
    sig_ref[...] = block_gate(me_ref, scaled_ref, weight_ref)


GROUPS = SIDE // 32


def quarters():
    lane = lax.broadcasted_iota(jnp.int32, (ROWS, 128), 1)
    return [((lane >> 3) & 3) == q for q in range(4)]


def slab(side_refs, g):
    return jnp.concatenate([r[g * 32 : (g + 1) * 32, :] for r in side_refs], axis=0)


def block_kernel(*refs):
    me_ref, left_refs, right_refs, sig_refs = refs[0], refs[1:5], refs[5:9], refs[9:13]
    own_ref, core_in, far_in, block_ref, mid_ref = refs[13:18]
    pieces = [(own_ref, 0), (core_in, 0), (far_in, 0), (core_in, HEAD)]
    own_out, near_out, far_out, pairs_ref = refs[18:22]
    outs = [(own_out, 0), (near_out, 0), (far_out, 0), (far_out, PIECE)]
    me = me_ref[0]
    of_quarter = quarters()

    masks = [ref[at + PIECE : at + HEAD, :].astype(F32) for ref, at in pieces]
    valid = jnp.max(jnp.concatenate(masks, axis=0), axis=0, keepdims=True)
    src = lax.broadcasted_iota(jnp.int32, (128, 128), 0)
    dst = lax.broadcasted_iota(jnp.int32, (128, 128), 1)
    pick = jnp.zeros((128, 128), F32)
    for n, offset in enumerate(RIGHT_OFFSETS):
        wanted = (me ^ offset) * ROWS + (dst & 7)
        pick = jnp.where((src == wanted) & ((dst >> 5) == n), 1.0, pick)
    spread = jnp.broadcast_to(valid, (ROWS, 128)).astype(BF16)
    column_valid = dot(spread, pick.astype(BF16), NN)
    pair_valid = [jnp.max(k[:ROWS], axis=1, keepdims=True) * column_valid for k in masks]
    valid = jnp.broadcast_to(valid, (128, 128)).astype(BF16)

    for g in range(GROUPS):
        full = dot(slab(left_refs, g) * valid, slab(right_refs, g), NT).reshape(4, 4, ROWS, 128)
        for m in range(4):
            kept = full[m, 3]
            for q in range(3):
                kept = jnp.where(of_quarter[q], full[m, q], kept)
            pairs_ref[g * 32 + m * ROWS : g * 32 + (m + 1) * ROWS, :] = kept * pair_valid[m]

    turned = []
    for row in range(ROWS):
        turn = pairs_ref[pl.ds(row, 128, stride=ROWS), :].T.reshape(4, 4, ROWS, 128)
        turned.append(jnp.concatenate([turn[:, q].reshape(32, 128) for q in range(4)], axis=1))
    mixed = jnp.concatenate(turned, axis=0).astype(BF16).astype(F32)

    ones = jnp.where((src & 3) == (dst & 3), 1.0, 0.0).astype(BF16)

    def channel_mean(values):
        total = values[:, :128] + values[:, 128:256] + values[:, 256:384] + values[:, 384:]
        mean = split_sum(total, ones) * (1.0 / 128.0)
        return jnp.concatenate([mean] * 4, axis=1)

    mid_gain, mid_bias = mid_ref[0:1, :], mid_ref[1:2, :]
    center = mixed - channel_mean(mixed)
    inverse = lax.rsqrt(channel_mean(center * center) + EPSILON)
    normed = center * inverse
    scaled = (normed * mid_gain + mid_bias).astype(BF16)
    update = dot(scaled, block_ref[...], NN)
    grad_update = []
    for m in range(4):
        sig = sig_refs[m][...]
        out = sig * update[:, m * 128 : (m + 1) * 128]
        ref, at = outs[m]
        ref[at : at + PIECE, :] = out.astype(BF16)
        ref, at = pieces[m]
        cot = ref[at : at + PIECE, :].astype(F32)
        grad_update.append((cot * sig).astype(BF16))
    grad_hat = dot(jnp.concatenate(grad_update, axis=1), block_ref[...], NT) * mid_gain
    first = channel_mean(grad_hat)
    second = channel_mean(grad_hat * normed)
    grad_mixed = inverse * (grad_hat - first - normed * second)

    mask = jnp.concatenate(pair_valid, axis=0)
    for row in range(ROWS):
        part = grad_mixed[row * 32 : (row + 1) * 32]
        parts = [part[:, q * 128 : (q + 1) * 128].reshape(4, 1, ROWS, 128) for q in range(4)]
        turn = jnp.concatenate(parts, axis=1).reshape(128, 128)
        pairs_ref[pl.ds(row, 128, stride=ROWS), :] = turn.T
    for g in range(GROUPS):
        pairs_ref[g * 32 : (g + 1) * 32, :] = pairs_ref[g * 32 : (g + 1) * 32, :] * mask


def spread_group(pairs_ref, g, of_quarter):
    rows = []
    for m in range(4):
        part = pairs_ref[g * 32 + m * ROWS : g * 32 + (m + 1) * ROWS, :]
        rows += [jnp.where(of_quarter[q], part, 0.0) for q in range(4)]
    return jnp.concatenate(rows, axis=0).astype(BF16)


def grad_right_kernel(half):
    def kernel(pairs_ref, *refs):
        left_refs, out_refs = refs[:4], refs[4:]
        of_quarter = quarters()
        for g in range(GROUPS // 2):
            spread = spread_group(pairs_ref, half * GROUPS // 2 + g, of_quarter)
            grad = dot(spread, slab(left_refs, half * GROUPS // 2 + g), TN).astype(BF16)
            for n in range(4):
                out_refs[n][g * 32 : (g + 1) * 32, :] = grad[n * 32 : (n + 1) * 32]

    return kernel


def grad_left_kernel(pairs_ref, *refs):
    right_refs, lefts = refs[:4], refs[5:]
    of_quarter = quarters()
    for g in range(GROUPS):
        spread = spread_group(pairs_ref, g, of_quarter)
        grad = dot(spread, slab(right_refs, g), NN).astype(BF16)
        for m, ref in enumerate(lefts):
            ref[g * 32 : (g + 1) * 32, :] = grad[m * 32 : (m + 1) * 32]


def halves_kernel(x_ref, first_ref, second_ref):
    first_ref[...] = x_ref[: SIDE // 2, :]
    second_ref[...] = x_ref[SIDE // 2 :, :]


def pass_kernel(message_ref, *refs):
    refs[-1][...] = message_ref[...]


def join_kernel(mine_ref, got_ref, both_ref):
    both_ref[:HEAD, :] = mine_ref[...]
    both_ref[HEAD:, :] = got_ref[HEAD:, :]


def add_kernel(mine_ref, got_ref, *refs):
    sum_ref = refs[-1]
    sum_ref[...] = (mine_ref[...].astype(F32) + got_ref[...].astype(F32)).astype(BF16)


def near_kernel(first_ref, second_ref, after_ref, both_ref):
    both_ref[: SIDE // 2, :] = first_ref[...]
    both_ref[SIDE // 2 :, :] = second_ref[...]


def back_kernel(left_ref, own_ref, far_ref, after_ref, both_ref):
    both_ref[:SIDE, :] = left_ref[...]
    both_ref[SIDE : SIDE + PIECE, :] = own_ref[...]
    both_ref[SIDE + PIECE :, :] = far_ref[PIECE:, :]


def factor_kernel(
    x_ref,
    cot_ref,
    mask_ref,
    weight_ref,
    params_ref,
    weight_t_ref,
    factor_ref,
    normed_ref,
    inverse_ref,
    open_ref,
    gain_t_ref,
):
    gain_t = jnp.broadcast_to(params_ref[0:1, :], (128, 128)).T
    bias_t = jnp.broadcast_to(params_ref[1:2, :], (128, 128)).T
    gain_t_ref[...] = gain_t
    scaled = scale_in(x_ref[...], params_ref).astype(BF16)
    gate_sig = sigmoid(dot(scaled, weight_ref[:, 512:640], NN)).reshape(cot_ref.shape)
    open_ref[...] = cot_ref[...].astype(F32) * (1.0 - gate_sig)
    for row in range(ROWS):
        x = x_ref[row * 128 : (row + 1) * 128, :]
        normed, inverse = norm(x.astype(F32).T, 0)
        normed_ref[row] = normed
        inverse_ref[row : row + 1, :] = inverse
        scaled = (normed * gain_t + bias_t).astype(BF16)
        projected = dot(weight_t_ref[...], scaled, NN)
        keep = mask_ref[row : row + 1].astype(F32)
        for side in range(2):
            base = 256 * side
            gate = sigmoid(projected[base : base + 128])
            value = projected[base + 128 : base + 256]
            factor_ref[row, base : base + 128, :] = keep * value * gate * (1.0 - gate)
            factor_ref[row, base + 128 : base + 256, :] = keep * gate


def out_kernel(me_ref, own_ref, near_ref, far_ref, open_ref, weight_ref, out_ref, grad_ref, full_ref):
    places = [(own_ref, 0), (near_ref, SIDE), (far_ref, 0), (near_ref, SIDE + PIECE)]
    for (ref, at), offset in zip(places, LEFT_OFFSETS):
        piece = ref[at : at + PIECE, :].astype(F32).reshape(ROWS, 4, ROWS, 128)
        for n, start in enumerate(columns_of(me_ref[0] ^ offset, RIGHT_OFFSETS)):
            full_ref[:, pl.ds(start, ROWS), :] = piece[:, n]
    for row in range(ROWS):
        out = full_ref[row]
        out_ref[row] = out.astype(BF16)
        grad_gate = (open_ref[row] * out).astype(BF16)
        grad_ref[row] = dot(weight_ref[:, 512:640], grad_gate, NT)


def right_terms(rows_ref, factor_ref, row, half):
    parts = []
    nothing = jnp.zeros((16, 128), BF16)
    for place in (256, 384):
        for q in range(4):
            grad = rows_ref[pl.ds(q * ROWS + row, 16, stride=4 * ROWS), :]
            at = place + q * 32 + half * 16
            term = (grad * factor_ref[row, at : at + 16, :]).astype(BF16)
            parts += [nothing, term] if half else [term, nothing]
    return jnp.concatenate(parts, axis=0)


def partial_kernel(*refs):
    left_refs, (own_ref, near_ref, got_ref) = refs[0:3], refs[3:6]
    factor_ref, gate_ref, weight_ref, sum_ref, left_rows, right_rows = refs[6:]
    left = [r[:SIDE, :].astype(F32) for r in left_refs]
    left_rows[...] = left[0] + left[1] + left[2]
    right = own_ref[...].astype(F32) + near_ref[: SIDE // 2, :].astype(F32)
    right_rows[...] = right + got_ref[...].astype(F32)
    for row in range(ROWS):
        grad = load_side(left_rows, row)
        parts = [(grad * factor_ref[row, a : a + 128, :]).astype(BF16) for a in (0, 128)]
        parts.append(right_terms(right_rows, factor_ref, row, 0))
        grad_projected = jnp.concatenate(parts, axis=0)
        sum_ref[row] = dot(weight_ref[:, :512], grad_projected, NN) + gate_ref[row]


def pair_kernel(
    own_ref,
    near_ref,
    got_ref,
    factor_ref,
    sum_ref,
    normed_ref,
    inverse_ref,
    gain_t_ref,
    weight_ref,
    out_ref,
    right_rows,
):
    right = own_ref[...].astype(F32) + near_ref[SIDE // 2 :, :].astype(F32)
    right_rows[...] = right + got_ref[...].astype(F32)
    for row in range(ROWS):
        terms = right_terms(right_rows, factor_ref, row, 1)
        grad_scaled = dot(weight_ref[:, 256:512], terms, NN) + sum_ref[row]
        normed = normed_ref[row]
        grad_hat = grad_scaled * gain_t_ref[...]
        first = jnp.mean(grad_hat, axis=0, keepdims=True)
        second = jnp.mean(grad_hat * normed, axis=0, keepdims=True)
        grad = inverse_ref[row : row + 1, :] * (grad_hat - first - normed * second)
        out_ref[row] = grad.T.astype(BF16)


def swap(values, offset):
    return lax.ppermute(values, "row", [(s, s ^ offset) for s in range(16)])


def blocks_device(
    pair_rep,
    pair_mask,
    cotangent,
    in_gain,
    in_bias,
    proj_weight,
    gate_weight,
    mid_gain,
    mid_bias,
    out_weight,
):
    me = lax.axis_index("row").astype(jnp.int32).reshape(1)
    half = SIDE // 2
    cube = (ROWS, 128, 128)
    side, piece = ((SIDE, 128), BF16), ((PIECE, 128), BF16)
    halves, core = ((half, 128), BF16), ((SIDE + 2 * PIECE, 128), BF16)
    sig = ((PIECE, 128), F32)
    rows_scratch = pltpu.VMEM((2, SIDE, 128), F32)
    cube_scratch = pltpu.VMEM(cube, F32)

    def after(message, *others):
        return call(pass_kernel, [(message.shape, BF16)], vmem=[message, *others])[0]

    flat = pair_rep.reshape(SIDE, 128)
    weights = jnp.zeros((), BF16)
    for at, weight in ((0, proj_weight), (512, gate_weight), (640, out_weight)):
        weights = weights + jnp.pad(weight, ((0, 0), (at, 768 - at - weight.shape[1])))
    params = jnp.stack([in_gain, in_bias, mid_gain, mid_bias])

    first, second = call(halves_kernel, [halves] * 2, vmem=[flat])
    z_first, z_second = swap(first, Z_HIGH), swap(second, Z_HIGH)
    whole = after(flat, second)
    far = swap(whole, Z_LOW)
    x_near = swap(whole, CHIP_X)
    near = swap(whole, CORE)
    left_0, right_0, sig_0, weight_t, block_weight, mid = call(
        own_kernel,
        [side, side, sig, ((512, 128), BF16), ((512, 512), BF16), ((ROWS, 512), F32)],
        smem=[me],
        vmem=[whole, weights, params],
        scratch=[rows_scratch, cube_scratch],
        weight=WAIT,
    )

    def peer(*messages):
        return call(
            peer_kernel,
            [side, side, sig],
            smem=[me],
            vmem=[*messages, weight_t, weights, params],
            scratch=[rows_scratch, cube_scratch],
            weight=WAIT,
        )

    left_1, right_1, sig_1 = peer(near, x_near)
    own_piece, core_piece, far_piece = call(
        pack_kernel,
        [((HEAD, 128), BF16), ((HEAD, 128), BF16), ((2 * HEAD, 128), BF16)],
        smem=[me],
        vmem=[cotangent, pair_mask, x_near],
        scratch=[cube_scratch],
    )
    far_got = swap(far_piece, Z_LOW)
    both = swap(far, CORE)
    x_second = swap(z_second, CHIP_X)
    x_first = swap(after(z_first, x_second, left_0), CHIP_X)
    (joined,) = call(join_kernel, [((2 * HEAD, 128), BF16)], vmem=[core_piece, far_got])
    core_pieces = swap(joined, CORE)
    left_2, right_2, sig_2 = peer(far, z_first, z_second)
    left_3, right_3, sig_3 = peer(both, x_first, x_second)

    lefts, rights = [left_0, left_1, left_2, left_3], [right_0, right_1, right_2, right_3]
    out_0, out_1, out_far, pairs = call(
        block_kernel,
        [piece, piece, ((2 * PIECE, 128), BF16), ((SIDE, 128), F32)],
        smem=[me],
        vmem=lefts
        + rights
        + [sig_0, sig_1, sig_2, sig_3]
        + [own_piece, core_pieces, far_got, block_weight, mid],
    )
    out_far = swap(out_far, Z_LOW)
    right_a = call(grad_right_kernel(0), [halves] * 4, vmem=[pairs, *lefts])
    x_got = [swap(right_a[3], CHIP_X)]
    left_parts = call(grad_left_kernel, [side] * 4, vmem=[pairs, *rights, right_a[3]])
    both_got = swap(left_parts[3], CORE)
    right_b = call(grad_right_kernel(1), [halves] * 4, vmem=[pairs, *lefts], weight=WAIT)
    (left_sum,) = call(add_kernel, [side], vmem=[left_parts[2], both_got])
    x_got.append(swap(after(right_b[3], left_sum), CHIP_X))
    left_got = swap(left_sum, Z_LOW)
    z_got = []
    for mine, got in zip((right_a[2], right_b[2]), x_got):
        (total,) = call(add_kernel, [halves], vmem=[mine, got, left_sum])
        z_got.append(swap(total, Z_HIGH))
    (near_back,) = call(back_kernel, [core], vmem=[left_parts[1], out_1, out_far, left_sum])
    near_got = swap(near_back, CORE)
    (right_back,) = call(near_kernel, [side], vmem=[right_a[1], right_b[1], total])
    right_near = swap(right_back, CHIP_X)

    factors, normed, inverse, open_part, gain_t = call(
        factor_kernel,
        [((ROWS, 512, 128), F32), (cube, F32), ((ROWS, 128), F32), (cube, F32), ((128, 128), F32)],
        vmem=[whole, cotangent, pair_mask, weights, params, weight_t],
        weight=WAIT,
    )
    output, gate_part = call(
        out_kernel,
        [(cube, BF16), (cube, F32)],
        smem=[me],
        vmem=[out_0, near_got, out_far, open_part, weights],
        scratch=[cube_scratch],
    )
    half_scratch = pltpu.VMEM((half, 128), F32)
    (partial,) = call(
        partial_kernel,
        [(cube, F32)],
        vmem=[left_parts[0], near_got, left_got, right_a[0], right_near, z_got[0]]
        + [factors, gate_part, weights],
        scratch=[pltpu.VMEM((SIDE, 128), F32), half_scratch],
        weight=WAIT // 4,
    )
    (grad_pair,) = call(
        pair_kernel,
        [(cube, BF16)],
        vmem=[right_b[0], right_near, z_got[1]]
        + [factors, partial, normed, inverse, gain_t, weights],
        scratch=[half_scratch],
    )
    return (output, grad_pair)


def norm_stats(values, reduce_axis):
    center = values - jnp.mean(values, axis=reduce_axis, keepdims=True)
    inverse = lax.rsqrt(jnp.mean(center * center, axis=reduce_axis, keepdims=True) + EPSILON)
    return (center * inverse, inverse)


def norm_back(grad_hat, normed, inverse, reduce_axis):
    first = jnp.mean(grad_hat, axis=reduce_axis, keepdims=True)
    second = jnp.mean(grad_hat * normed, axis=reduce_axis, keepdims=True)
    return inverse * (grad_hat - first - normed * second)


def forward_products(left_chan, right_chan):
    return jnp.einsum("hik,hjk->hij", left_chan, right_chan, preferred_element_type=jnp.float32)


def backward_products(grad_full, left_chan, right_chan):
    grad_left = jnp.einsum(
        "hij,hjk->hik", grad_full, right_chan, preferred_element_type=jnp.float32
    )
    grad_right = jnp.einsum(
        "hij,hik->hjk", grad_full, left_chan, preferred_element_type=jnp.float32
    )
    return jnp.stack([grad_left, grad_right]).astype(jnp.bfloat16)


def channels_device(
    pair_rep,
    pair_mask,
    cotangent,
    in_gain,
    in_bias,
    proj_weight,
    gate_weight,
    mid_gain,
    mid_bias,
    out_weight,
):
    width = pair_rep.shape[2]
    hidden = out_weight.shape[0]
    weights_four = proj_weight.reshape(width, 2, 2, hidden)
    mask_float = pair_mask.astype(jnp.float32)
    normed_in, inverse_in = norm_stats(pair_rep.astype(jnp.float32), 2)
    scaled_in = (normed_in * in_gain + in_bias).astype(jnp.bfloat16)
    gate_pre = jnp.einsum(
        "ijc,csh->shij", scaled_in, weights_four[:, :, 0], preferred_element_type=jnp.float32
    )
    value_pre = jnp.einsum(
        "ijc,csh->shij", scaled_in, weights_four[:, :, 1], preferred_element_type=jnp.float32
    )
    sigmoid_gate = jax.nn.sigmoid(gate_pre)
    both_sides = (sigmoid_gate * value_pre * mask_float).astype(jnp.bfloat16)
    gate_sig = jax.nn.sigmoid(
        jnp.einsum("ijc,cd->ijd", scaled_in, gate_weight, preferred_element_type=jnp.float32)
    )
    sides_chan = lax.all_to_all(both_sides, "row", split_axis=1, concat_axis=2, tiled=True)
    partial_sum = forward_products(sides_chan[0], sides_chan[1])
    product = lax.psum_scatter(partial_sum, "col", scatter_dimension=2, tiled=True).astype(
        jnp.bfloat16
    )
    mixed_pair = lax.all_to_all(product, "row", split_axis=1, concat_axis=0, tiled=True)
    normed_mid, inverse_mid = norm_stats(mixed_pair.astype(jnp.float32), 0)
    scaled_mid = (normed_mid * mid_gain[:, None, None] + mid_bias[:, None, None]).astype(
        jnp.bfloat16
    )
    update = jnp.einsum("hij,hc->ijc", scaled_mid, out_weight, preferred_element_type=jnp.float32)
    output = (gate_sig * update).astype(jnp.bfloat16)
    grad_out = cotangent.astype(jnp.float32)
    grad_update = (grad_out * gate_sig).astype(jnp.bfloat16)
    grad_gate = (grad_out * update * gate_sig * (1.0 - gate_sig)).astype(jnp.bfloat16)
    grad_scaled_mid = jnp.einsum(
        "ijc,hc->hij", grad_update, out_weight, preferred_element_type=jnp.float32
    )
    grad_mixed = norm_back(
        grad_scaled_mid * mid_gain[:, None, None], normed_mid, inverse_mid, 0
    ).astype(jnp.bfloat16)
    grad_chan = lax.all_to_all(grad_mixed, "row", split_axis=0, concat_axis=1, tiled=True)
    grad_full = lax.all_gather(grad_chan, "col", axis=2, tiled=True)
    grad_local = backward_products(grad_full, sides_chan[0], sides_chan[1])
    grad_sides = lax.all_to_all(grad_local, "row", split_axis=2, concat_axis=1, tiled=True)
    side_float = grad_sides.astype(jnp.float32) * mask_float
    grad_value = (side_float * sigmoid_gate).astype(jnp.bfloat16)
    grad_gate_pre = (side_float * value_pre * sigmoid_gate * (1.0 - sigmoid_gate)).astype(
        jnp.bfloat16
    )
    grad_scaled = jnp.einsum(
        "shij,csh->ijc", grad_gate_pre, weights_four[:, :, 0], preferred_element_type=jnp.float32
    )
    grad_scaled = grad_scaled + jnp.einsum(
        "shij,csh->ijc", grad_value, weights_four[:, :, 1], preferred_element_type=jnp.float32
    )
    grad_scaled = grad_scaled + jnp.einsum(
        "ijd,cd->ijc", grad_gate, gate_weight, preferred_element_type=jnp.float32
    )
    grad_pair = norm_back(grad_scaled * in_gain, normed_in, inverse_in, 2).astype(jnp.bfloat16)
    return (output, grad_pair)


def solution(mesh):
    blocks = mesh.shape["row"] == 16 and mesh.shape["col"] == 1
    placed = (
        P(("grp", "row"), "col", None),
        P(("grp", "row"), "col"),
        P(("grp", "row"), "col", None),
        P(),
        P(),
        P(),
        P(),
        P(),
        P(),
        P(),
    )
    return jax.shard_map(
        blocks_device if blocks else channels_device,
        mesh=mesh,
        in_specs=placed,
        out_specs=(P(("grp", "row"), "col", None), P(("grp", "row"), "col", None)),
        check_vma=False,
    )
```

```python
import jax
import jax.numpy as jnp
from jax import lax
from jax.experimental import pallas as pl
from jax.experimental.pallas import tpu as pltpu
from jax.sharding import PartitionSpec as P

EPSILON = 1e-05
CORE, CHIP_X, Z_LOW, Z_HIGH = 1, 2, 4, 8
LEFT_OFFSETS = (0, CORE, Z_LOW, Z_LOW | CORE)
RIGHT_OFFSETS = (0, CHIP_X, Z_HIGH, Z_HIGH | CHIP_X)
ROWS = 8
SIDE = 1024
PIECE = 256
HEAD = PIECE + 16
VMEM_BYTES = 48 * 2**20
WAIT = 5 * 10**9

NT = (((1,), (1,)), ((), ()))
NN = (((1,), (0,)), ((), ()))
TN = (((0,), (0,)), ((), ()))
F32, BF16 = jnp.float32, jnp.bfloat16


def dot(a, b, dims):
    return lax.dot_general(a, b, dims, preferred_element_type=F32)


def norm(values, axis):
    center = values - jnp.mean(values, axis=axis, keepdims=True)
    inverse = lax.rsqrt(jnp.mean(center * center, axis=axis, keepdims=True) + EPSILON)
    return center * inverse, inverse


def sigmoid(x):
    return 0.5 * jnp.tanh(0.5 * x) + 0.5


def call(kernel, outs, smem=(), vmem=(), scratch=(), weight=2**26):
    vmem_spec = pl.BlockSpec(memory_space=pltpu.VMEM)
    specs = [pl.BlockSpec(memory_space=pltpu.SMEM)] * len(smem)
    specs += [vmem_spec] * len(vmem)
    return pl.pallas_call(
        kernel,
        out_shape=[jax.ShapeDtypeStruct(s, d) for s, d in outs],
        in_specs=specs,
        out_specs=[vmem_spec] * len(outs),
        scratch_shapes=list(scratch),
        compiler_params=pltpu.CompilerParams(vmem_limit_bytes=VMEM_BYTES),
        cost_estimate=pl.CostEstimate(flops=weight, bytes_accessed=2**18, transcendentals=0),
    )(*smem, *vmem)


def side_rows(quarter, row):
    return pl.ds(quarter * ROWS + row, 32, stride=4 * ROWS)


def store_side(rows_ref, row, result):
    for q in range(4):
        rows_ref[side_rows(q, row), :] = result[q * 32 : (q + 1) * 32]


def load_side(rows_ref, row):
    return jnp.concatenate([rows_ref[side_rows(q, row), :] for q in range(4)], axis=0)


def columns_of(me, offsets):
    return [pl.multiple_of((me ^ o) * ROWS, ROWS) for o in offsets]


def pick_columns(full_ref, starts):
    columns = [full_ref[:, pl.ds(s, ROWS), :] for s in starts]
    return jnp.concatenate(columns, axis=1).reshape(PIECE, 128)


def pack_kernel(me_ref, cot_ref, mask_ref, after_ref, own_ref, core_ref, far_ref, full_ref):
    me = me_ref[0]
    full_ref[...] = cot_ref[...].astype(F32)
    mask = jnp.concatenate([mask_ref[...].astype(F32), jnp.zeros((ROWS, 128), F32)], axis=0)
    places = [(own_ref, 0), (core_ref, 0), (far_ref, 0), (far_ref, HEAD)]
    for (ref, place), offset in zip(places, LEFT_OFFSETS):
        piece = pick_columns(full_ref, columns_of(me ^ offset, RIGHT_OFFSETS))
        ref[place : place + PIECE, :] = piece.astype(BF16)
        ref[place + PIECE : place + HEAD, :] = mask.astype(BF16)


def split_sum(values, ones):
    high = values.astype(BF16)
    low = (values - high.astype(F32)).astype(BF16)
    return dot(high, ones, NN) + dot(low, ones, NN)


def scale_in(x, params_ref):
    return norm(x.astype(F32), 1)[0] * params_ref[0:1, :] + params_ref[1:2, :]


def project(weight_t, scaled, row):
    return dot(weight_t, scaled[row * 128 : (row + 1) * 128], NT)


def make_side(projected):
    return sigmoid(projected[:128]) * projected[128:]


def block_gate(me_ref, scaled_ref, weight_ref):
    picked = pick_columns(scaled_ref, columns_of(me_ref[0], RIGHT_OFFSETS))
    return sigmoid(dot(picked.astype(BF16), weight_ref[:, 512:640], NN))


def own_kernel(
    me_ref,
    x_ref,
    weight_ref,
    params_ref,
    left_ref,
    right_ref,
    sig_ref,
    weight_t_ref,
    block_ref,
    mid_ref,
    rows_ref,
    scaled_ref,
):
    weight_t_ref[...] = weight_ref[:, :512].astype(F32).T.astype(BF16)
    scaled = scale_in(x_ref[...], params_ref)
    scaled_ref[...] = scaled.reshape(scaled_ref.shape)
    scaled = scaled.astype(BF16)
    for row in range(ROWS):
        projected = project(weight_t_ref[...], scaled, row)
        store_side(rows_ref.at[0], row, make_side(projected[:256]))
        store_side(rows_ref.at[1], row, make_side(projected[256:]))
    left_ref[...] = rows_ref[0].astype(BF16)
    right_ref[...] = rows_ref[1].astype(BF16)
    sig_ref[...] = block_gate(me_ref, scaled_ref, weight_ref)

    repeat = lax.broadcasted_iota(jnp.int32, (512, 128), 0)
    lane = lax.broadcasted_iota(jnp.int32, (512, 128), 1)
    spread = jnp.where((repeat >> 2) == lane, 1.0, 0.0).astype(BF16)
    tall = dot(spread, weight_ref[:, 640:], NN)
    for m in range(4):
        block_ref[:, m * 128 : (m + 1) * 128] = jnp.where((repeat & 3) == m, tall, 0.0).astype(BF16)
    rows = lax.broadcasted_iota(jnp.int32, (ROWS, 128), 0)
    both = jnp.where(rows == 0, params_ref[2:3, :], params_ref[3:4, :])
    wide = jnp.zeros((ROWS, 512), F32)
    for _ in range(3):
        term = both.astype(BF16)
        wide = wide + dot(term, spread, NT)
        both = both - term.astype(F32)
    mid_ref[...] = wide


def peer_kernel(me_ref, left_in, *refs):
    right_in, rest = refs[:-8], refs[-8:]
    weight_t_ref, weight_ref, params_ref, left_ref, right_ref, sig_ref, rows_ref, scaled_ref = rest
    scaled = scale_in(left_in[...], params_ref)
    scaled_ref[...] = scaled.reshape(scaled_ref.shape)
    scaled = scaled.astype(BF16)
    for row in range(ROWS):
        projected = project(weight_t_ref[:256, :], scaled, row)
        store_side(rows_ref.at[0], row, make_side(projected))
    scaled = [scale_in(r[...], params_ref).astype(BF16) for r in right_in]
    for row in range(ROWS):
        part, place = divmod(row, ROWS // len(right_in))
        projected = project(weight_t_ref[256:, :], scaled[part], place)
        store_side(rows_ref.at[1], row, make_side(projected))
    left_ref[...] = rows_ref[0].astype(BF16)
    right_ref[...] = rows_ref[1].astype(BF16)
    sig_ref[...] = block_gate(me_ref, scaled_ref, weight_ref)


GROUPS = SIDE // 32


def quarters():
    lane = lax.broadcasted_iota(jnp.int32, (ROWS, 128), 1)
    return [((lane >> 3) & 3) == q for q in range(4)]


def slab(side_refs, g):
    return jnp.concatenate([r[g * 32 : (g + 1) * 32, :] for r in side_refs], axis=0)


def block_kernel(*refs):
    me_ref, left_refs, right_refs, sig_refs = refs[0], refs[1:5], refs[5:9], refs[9:13]
    own_ref, core_in, far_in, block_ref, mid_ref = refs[13:18]
    pieces = [(own_ref, 0), (core_in, 0), (far_in, 0), (core_in, HEAD)]
    own_out, near_out, far_out, pairs_ref = refs[18:22]
    outs = [(own_out, 0), (near_out, 0), (far_out, 0), (far_out, PIECE)]
    me = me_ref[0]
    of_quarter = quarters()

    masks = [ref[at + PIECE : at + HEAD, :].astype(F32) for ref, at in pieces]
    valid = jnp.max(jnp.concatenate(masks, axis=0), axis=0, keepdims=True)
    src = lax.broadcasted_iota(jnp.int32, (128, 128), 0)
    dst = lax.broadcasted_iota(jnp.int32, (128, 128), 1)
    pick = jnp.zeros((128, 128), F32)
    for n, offset in enumerate(RIGHT_OFFSETS):
        wanted = (me ^ offset) * ROWS + (dst & 7)
        pick = jnp.where((src == wanted) & ((dst >> 5) == n), 1.0, pick)
    spread = jnp.broadcast_to(valid, (ROWS, 128)).astype(BF16)
    column_valid = dot(spread, pick.astype(BF16), NN)
    pair_valid = [jnp.max(k[:ROWS], axis=1, keepdims=True) * column_valid for k in masks]
    valid = jnp.broadcast_to(valid, (128, 128)).astype(BF16)

    for g in range(GROUPS):
        full = dot(slab(left_refs, g) * valid, slab(right_refs, g), NT).reshape(4, 4, ROWS, 128)
        for m in range(4):
            kept = full[m, 3]
            for q in range(3):
                kept = jnp.where(of_quarter[q], full[m, q], kept)
            pairs_ref[g * 32 + m * ROWS : g * 32 + (m + 1) * ROWS, :] = kept * pair_valid[m]

    turned = []
    for row in range(ROWS):
        turn = pairs_ref[pl.ds(row, 128, stride=ROWS), :].T.reshape(4, 4, ROWS, 128)
        turned.append(jnp.concatenate([turn[:, q].reshape(32, 128) for q in range(4)], axis=1))
    mixed = jnp.concatenate(turned, axis=0).astype(BF16).astype(F32)

    ones = jnp.where((src & 3) == (dst & 3), 1.0, 0.0).astype(BF16)

    def channel_mean(values):
        total = values[:, :128] + values[:, 128:256] + values[:, 256:384] + values[:, 384:]
        mean = split_sum(total, ones) * (1.0 / 128.0)
        return jnp.concatenate([mean] * 4, axis=1)

    mid_gain, mid_bias = mid_ref[0:1, :], mid_ref[1:2, :]
    center = mixed - channel_mean(mixed)
    inverse = lax.rsqrt(channel_mean(center * center) + EPSILON)
    normed = center * inverse
    scaled = (normed * mid_gain + mid_bias).astype(BF16)
    update = dot(scaled, block_ref[...], NN)
    grad_update = []
    for m in range(4):
        sig = sig_refs[m][...]
        out = sig * update[:, m * 128 : (m + 1) * 128]
        ref, at = outs[m]
        ref[at : at + PIECE, :] = out.astype(BF16)
        ref, at = pieces[m]
        cot = ref[at : at + PIECE, :].astype(F32)
        grad_update.append((cot * sig).astype(BF16))
    grad_hat = dot(jnp.concatenate(grad_update, axis=1), block_ref[...], NT) * mid_gain
    first = channel_mean(grad_hat)
    second = channel_mean(grad_hat * normed)
    grad_mixed = inverse * (grad_hat - first - normed * second)

    mask = jnp.concatenate(pair_valid, axis=0)
    for row in range(ROWS):
        part = grad_mixed[row * 32 : (row + 1) * 32]
        parts = [part[:, q * 128 : (q + 1) * 128].reshape(4, 1, ROWS, 128) for q in range(4)]
        turn = jnp.concatenate(parts, axis=1).reshape(128, 128)
        pairs_ref[pl.ds(row, 128, stride=ROWS), :] = turn.T
    for g in range(GROUPS):
        pairs_ref[g * 32 : (g + 1) * 32, :] = pairs_ref[g * 32 : (g + 1) * 32, :] * mask


def spread_group(pairs_ref, g, of_quarter):
    rows = []
    for m in range(4):
        part = pairs_ref[g * 32 + m * ROWS : g * 32 + (m + 1) * ROWS, :]
        rows += [jnp.where(of_quarter[q], part, 0.0) for q in range(4)]
    return jnp.concatenate(rows, axis=0).astype(BF16)


def grad_right_kernel(half):
    def kernel(pairs_ref, *refs):
        left_refs, out_refs = refs[:4], refs[4:]
        of_quarter = quarters()
        for g in range(GROUPS // 2):
            spread = spread_group(pairs_ref, half * GROUPS // 2 + g, of_quarter)
            grad = dot(spread, slab(left_refs, half * GROUPS // 2 + g), TN).astype(BF16)
            for n in range(4):
                out_refs[n][g * 32 : (g + 1) * 32, :] = grad[n * 32 : (n + 1) * 32]

    return kernel


def grad_left_kernel(pairs_ref, *refs):
    right_refs, lefts = refs[:4], refs[5:]
    of_quarter = quarters()
    for g in range(GROUPS):
        spread = spread_group(pairs_ref, g, of_quarter)
        grad = dot(spread, slab(right_refs, g), NN).astype(BF16)
        for m, ref in enumerate(lefts):
            ref[g * 32 : (g + 1) * 32, :] = grad[m * 32 : (m + 1) * 32]


def halves_kernel(x_ref, first_ref, second_ref):
    first_ref[...] = x_ref[: SIDE // 2, :]
    second_ref[...] = x_ref[SIDE // 2 :, :]


def pass_kernel(message_ref, *refs):
    refs[-1][...] = message_ref[...]


def join_kernel(mine_ref, got_ref, both_ref):
    both_ref[:HEAD, :] = mine_ref[...]
    both_ref[HEAD:, :] = got_ref[HEAD:, :]


def add_kernel(mine_ref, got_ref, *refs):
    sum_ref = refs[-1]
    sum_ref[...] = (mine_ref[...].astype(F32) + got_ref[...].astype(F32)).astype(BF16)


def near_kernel(first_ref, second_ref, after_ref, both_ref):
    both_ref[: SIDE // 2, :] = first_ref[...]
    both_ref[SIDE // 2 :, :] = second_ref[...]


def back_kernel(left_ref, own_ref, far_ref, after_ref, both_ref):
    both_ref[:SIDE, :] = left_ref[...]
    both_ref[SIDE : SIDE + PIECE, :] = own_ref[...]
    both_ref[SIDE + PIECE :, :] = far_ref[PIECE:, :]


def factor_kernel(
    x_ref,
    cot_ref,
    mask_ref,
    weight_ref,
    params_ref,
    weight_t_ref,
    factor_ref,
    normed_ref,
    inverse_ref,
    open_ref,
    gain_t_ref,
):
    gain_t = jnp.broadcast_to(params_ref[0:1, :], (128, 128)).T
    bias_t = jnp.broadcast_to(params_ref[1:2, :], (128, 128)).T
    gain_t_ref[...] = gain_t
    scaled = scale_in(x_ref[...], params_ref).astype(BF16)
    gate_sig = sigmoid(dot(scaled, weight_ref[:, 512:640], NN)).reshape(cot_ref.shape)
    open_ref[...] = cot_ref[...].astype(F32) * (1.0 - gate_sig)
    for row in range(ROWS):
        x = x_ref[row * 128 : (row + 1) * 128, :]
        normed, inverse = norm(x.astype(F32).T, 0)
        normed_ref[row] = normed
        inverse_ref[row : row + 1, :] = inverse
        scaled = (normed * gain_t + bias_t).astype(BF16)
        projected = dot(weight_t_ref[...], scaled, NN)
        keep = mask_ref[row : row + 1].astype(F32)
        for side in range(2):
            base = 256 * side
            gate = sigmoid(projected[base : base + 128])
            value = projected[base + 128 : base + 256]
            factor_ref[row, base : base + 128, :] = keep * value * gate * (1.0 - gate)
            factor_ref[row, base + 128 : base + 256, :] = keep * gate


def out_kernel(me_ref, own_ref, near_ref, far_ref, open_ref, weight_ref, out_ref, grad_ref, full_ref):
    places = [(own_ref, 0), (near_ref, SIDE), (far_ref, 0), (near_ref, SIDE + PIECE)]
    for (ref, at), offset in zip(places, LEFT_OFFSETS):
        piece = ref[at : at + PIECE, :].astype(F32).reshape(ROWS, 4, ROWS, 128)
        for n, start in enumerate(columns_of(me_ref[0] ^ offset, RIGHT_OFFSETS)):
            full_ref[:, pl.ds(start, ROWS), :] = piece[:, n]
    for row in range(ROWS):
        out = full_ref[row]
        out_ref[row] = out.astype(BF16)
        grad_gate = (open_ref[row] * out).astype(BF16)
        grad_ref[row] = dot(weight_ref[:, 512:640], grad_gate, NT)


def right_terms(rows_ref, factor_ref, row, half):
    parts = []
    nothing = jnp.zeros((16, 128), BF16)
    for place in (256, 384):
        for q in range(4):
            grad = rows_ref[pl.ds(q * ROWS + row, 16, stride=4 * ROWS), :]
            at = place + q * 32 + half * 16
            term = (grad * factor_ref[row, at : at + 16, :]).astype(BF16)
            parts += [nothing, term] if half else [term, nothing]
    return jnp.concatenate(parts, axis=0)


def partial_kernel(*refs):
    left_refs, (own_ref, near_ref, got_ref) = refs[0:3], refs[3:6]
    factor_ref, gate_ref, weight_ref, sum_ref, left_rows, right_rows = refs[6:]
    left = [r[:SIDE, :].astype(F32) for r in left_refs]
    left_rows[...] = left[0] + left[1] + left[2]
    right = own_ref[...].astype(F32) + near_ref[: SIDE // 2, :].astype(F32)
    right_rows[...] = right + got_ref[...].astype(F32)
    for row in range(ROWS):
        grad = load_side(left_rows, row)
        parts = [(grad * factor_ref[row, a : a + 128, :]).astype(BF16) for a in (0, 128)]
        parts.append(right_terms(right_rows, factor_ref, row, 0))
        grad_projected = jnp.concatenate(parts, axis=0)
        sum_ref[row] = dot(weight_ref[:, :512], grad_projected, NN) + gate_ref[row]


def pair_kernel(
    own_ref,
    near_ref,
    got_ref,
    factor_ref,
    sum_ref,
    normed_ref,
    inverse_ref,
    gain_t_ref,
    weight_ref,
    out_ref,
    right_rows,
):
    right = own_ref[...].astype(F32) + near_ref[SIDE // 2 :, :].astype(F32)
    right_rows[...] = right + got_ref[...].astype(F32)
    for row in range(ROWS):
        terms = right_terms(right_rows, factor_ref, row, 1)
        grad_scaled = dot(weight_ref[:, 256:512], terms, NN) + sum_ref[row]
        normed = normed_ref[row]
        grad_hat = grad_scaled * gain_t_ref[...]
        first = jnp.mean(grad_hat, axis=0, keepdims=True)
        second = jnp.mean(grad_hat * normed, axis=0, keepdims=True)
        grad = inverse_ref[row : row + 1, :] * (grad_hat - first - normed * second)
        out_ref[row] = grad.T.astype(BF16)


def swap(values, offset):
    return lax.ppermute(values, "row", [(s, s ^ offset) for s in range(16)])


def blocks_device(
    pair_rep,
    pair_mask,
    cotangent,
    in_gain,
    in_bias,
    proj_weight,
    gate_weight,
    mid_gain,
    mid_bias,
    out_weight,
):
    me = lax.axis_index("row").astype(jnp.int32).reshape(1)
    half = SIDE // 2
    cube = (ROWS, 128, 128)
    side, piece = ((SIDE, 128), BF16), ((PIECE, 128), BF16)
    halves, core = ((half, 128), BF16), ((SIDE + 2 * PIECE, 128), BF16)
    sig = ((PIECE, 128), F32)
    rows_scratch = pltpu.VMEM((2, SIDE, 128), F32)
    cube_scratch = pltpu.VMEM(cube, F32)

    def after(message, *others):
        return call(pass_kernel, [(message.shape, BF16)], vmem=[message, *others])[0]

    flat = pair_rep.reshape(SIDE, 128)
    weights = jnp.zeros((), BF16)
    for at, weight in ((0, proj_weight), (512, gate_weight), (640, out_weight)):
        weights = weights + jnp.pad(weight, ((0, 0), (at, 768 - at - weight.shape[1])))
    params = jnp.stack([in_gain, in_bias, mid_gain, mid_bias])

    first, second = call(halves_kernel, [halves] * 2, vmem=[flat])
    z_first, z_second = swap(first, Z_HIGH), swap(second, Z_HIGH)
    whole = after(flat, second)
    far = swap(whole, Z_LOW)
    x_near = swap(whole, CHIP_X)
    near = swap(whole, CORE)
    left_0, right_0, sig_0, weight_t, block_weight, mid = call(
        own_kernel,
        [side, side, sig, ((512, 128), BF16), ((512, 512), BF16), ((ROWS, 512), F32)],
        smem=[me],
        vmem=[whole, weights, params],
        scratch=[rows_scratch, cube_scratch],
        weight=WAIT,
    )

    def peer(*messages):
        return call(
            peer_kernel,
            [side, side, sig],
            smem=[me],
            vmem=[*messages, weight_t, weights, params],
            scratch=[rows_scratch, cube_scratch],
            weight=WAIT,
        )

    left_1, right_1, sig_1 = peer(near, x_near)
    own_piece, core_piece, far_piece = call(
        pack_kernel,
        [((HEAD, 128), BF16), ((HEAD, 128), BF16), ((2 * HEAD, 128), BF16)],
        smem=[me],
        vmem=[cotangent, pair_mask, x_near],
        scratch=[cube_scratch],
    )
    far_got = swap(far_piece, Z_LOW)
    both = swap(far, CORE)
    x_second = swap(z_second, CHIP_X)
    x_first = swap(after(z_first, x_second, left_0), CHIP_X)
    (joined,) = call(join_kernel, [((2 * HEAD, 128), BF16)], vmem=[core_piece, far_got])
    core_pieces = swap(joined, CORE)
    left_2, right_2, sig_2 = peer(far, z_first, z_second)
    left_3, right_3, sig_3 = peer(both, x_first, x_second)

    lefts, rights = [left_0, left_1, left_2, left_3], [right_0, right_1, right_2, right_3]
    out_0, out_1, out_far, pairs = call(
        block_kernel,
        [piece, piece, ((2 * PIECE, 128), BF16), ((SIDE, 128), F32)],
        smem=[me],
        vmem=lefts
        + rights
        + [sig_0, sig_1, sig_2, sig_3]
        + [own_piece, core_pieces, far_got, block_weight, mid],
    )
    out_far = swap(out_far, Z_LOW)
    right_a = call(grad_right_kernel(0), [halves] * 4, vmem=[pairs, *lefts])
    x_got = [swap(right_a[3], CHIP_X)]
    left_parts = call(grad_left_kernel, [side] * 4, vmem=[pairs, *rights, right_a[3]])
    both_got = swap(left_parts[3], CORE)
    right_b = call(grad_right_kernel(1), [halves] * 4, vmem=[pairs, *lefts], weight=WAIT)
    (left_sum,) = call(add_kernel, [side], vmem=[left_parts[2], both_got])
    x_got.append(swap(after(right_b[3], left_sum), CHIP_X))
    left_got = swap(left_sum, Z_LOW)
    (right_back,) = call(near_kernel, [side], vmem=[right_a[1], right_b[1], x_got[1]])
    z_got = []
    for mine, got, late in zip((right_a[2], right_b[2]), x_got, (left_sum, right_back)):
        (total,) = call(add_kernel, [halves], vmem=[mine, got, late])
        z_got.append(swap(total, Z_HIGH))
    (near_back,) = call(back_kernel, [core], vmem=[left_parts[1], out_1, out_far, left_sum])
    near_got = swap(near_back, CORE)
    right_near = swap(right_back, CHIP_X)

    factors, normed, inverse, open_part, gain_t = call(
        factor_kernel,
        [((ROWS, 512, 128), F32), (cube, F32), ((ROWS, 128), F32), (cube, F32), ((128, 128), F32)],
        vmem=[whole, cotangent, pair_mask, weights, params, weight_t],
        weight=WAIT,
    )
    output, gate_part = call(
        out_kernel,
        [(cube, BF16), (cube, F32)],
        smem=[me],
        vmem=[out_0, near_got, out_far, open_part, weights],
        scratch=[cube_scratch],
    )
    half_scratch = pltpu.VMEM((half, 128), F32)
    (partial,) = call(
        partial_kernel,
        [(cube, F32)],
        vmem=[left_parts[0], near_got, left_got, right_a[0], right_near, z_got[0]]
        + [factors, gate_part, weights],
        scratch=[pltpu.VMEM((SIDE, 128), F32), half_scratch],
        weight=WAIT // 4,
    )
    (grad_pair,) = call(
        pair_kernel,
        [(cube, BF16)],
        vmem=[right_b[0], right_near, z_got[1]]
        + [factors, partial, normed, inverse, gain_t, weights],
        scratch=[half_scratch],
    )
    return (output, grad_pair)


def norm_stats(values, reduce_axis):
    center = values - jnp.mean(values, axis=reduce_axis, keepdims=True)
    inverse = lax.rsqrt(jnp.mean(center * center, axis=reduce_axis, keepdims=True) + EPSILON)
    return (center * inverse, inverse)


def norm_back(grad_hat, normed, inverse, reduce_axis):
    first = jnp.mean(grad_hat, axis=reduce_axis, keepdims=True)
    second = jnp.mean(grad_hat * normed, axis=reduce_axis, keepdims=True)
    return inverse * (grad_hat - first - normed * second)


def forward_products(left_chan, right_chan):
    return jnp.einsum("hik,hjk->hij", left_chan, right_chan, preferred_element_type=jnp.float32)


def backward_products(grad_full, left_chan, right_chan):
    grad_left = jnp.einsum(
        "hij,hjk->hik", grad_full, right_chan, preferred_element_type=jnp.float32
    )
    grad_right = jnp.einsum(
        "hij,hik->hjk", grad_full, left_chan, preferred_element_type=jnp.float32
    )
    return jnp.stack([grad_left, grad_right]).astype(jnp.bfloat16)


def channels_device(
    pair_rep,
    pair_mask,
    cotangent,
    in_gain,
    in_bias,
    proj_weight,
    gate_weight,
    mid_gain,
    mid_bias,
    out_weight,
):
    width = pair_rep.shape[2]
    hidden = out_weight.shape[0]
    weights_four = proj_weight.reshape(width, 2, 2, hidden)
    mask_float = pair_mask.astype(jnp.float32)
    normed_in, inverse_in = norm_stats(pair_rep.astype(jnp.float32), 2)
    scaled_in = (normed_in * in_gain + in_bias).astype(jnp.bfloat16)
    gate_pre = jnp.einsum(
        "ijc,csh->shij", scaled_in, weights_four[:, :, 0], preferred_element_type=jnp.float32
    )
    value_pre = jnp.einsum(
        "ijc,csh->shij", scaled_in, weights_four[:, :, 1], preferred_element_type=jnp.float32
    )
    sigmoid_gate = jax.nn.sigmoid(gate_pre)
    both_sides = (sigmoid_gate * value_pre * mask_float).astype(jnp.bfloat16)
    gate_sig = jax.nn.sigmoid(
        jnp.einsum("ijc,cd->ijd", scaled_in, gate_weight, preferred_element_type=jnp.float32)
    )
    sides_chan = lax.all_to_all(both_sides, "row", split_axis=1, concat_axis=2, tiled=True)
    partial_sum = forward_products(sides_chan[0], sides_chan[1])
    product = lax.psum_scatter(partial_sum, "col", scatter_dimension=2, tiled=True).astype(
        jnp.bfloat16
    )
    mixed_pair = lax.all_to_all(product, "row", split_axis=1, concat_axis=0, tiled=True)
    normed_mid, inverse_mid = norm_stats(mixed_pair.astype(jnp.float32), 0)
    scaled_mid = (normed_mid * mid_gain[:, None, None] + mid_bias[:, None, None]).astype(
        jnp.bfloat16
    )
    update = jnp.einsum("hij,hc->ijc", scaled_mid, out_weight, preferred_element_type=jnp.float32)
    output = (gate_sig * update).astype(jnp.bfloat16)
    grad_out = cotangent.astype(jnp.float32)
    grad_update = (grad_out * gate_sig).astype(jnp.bfloat16)
    grad_gate = (grad_out * update * gate_sig * (1.0 - gate_sig)).astype(jnp.bfloat16)
    grad_scaled_mid = jnp.einsum(
        "ijc,hc->hij", grad_update, out_weight, preferred_element_type=jnp.float32
    )
    grad_mixed = norm_back(
        grad_scaled_mid * mid_gain[:, None, None], normed_mid, inverse_mid, 0
    ).astype(jnp.bfloat16)
    grad_chan = lax.all_to_all(grad_mixed, "row", split_axis=0, concat_axis=1, tiled=True)
    grad_full = lax.all_gather(grad_chan, "col", axis=2, tiled=True)
    grad_local = backward_products(grad_full, sides_chan[0], sides_chan[1])
    grad_sides = lax.all_to_all(grad_local, "row", split_axis=2, concat_axis=1, tiled=True)
    side_float = grad_sides.astype(jnp.float32) * mask_float
    grad_value = (side_float * sigmoid_gate).astype(jnp.bfloat16)
    grad_gate_pre = (side_float * value_pre * sigmoid_gate * (1.0 - sigmoid_gate)).astype(
        jnp.bfloat16
    )
    grad_scaled = jnp.einsum(
        "shij,csh->ijc", grad_gate_pre, weights_four[:, :, 0], preferred_element_type=jnp.float32
    )
    grad_scaled = grad_scaled + jnp.einsum(
        "shij,csh->ijc", grad_value, weights_four[:, :, 1], preferred_element_type=jnp.float32
    )
    grad_scaled = grad_scaled + jnp.einsum(
        "ijd,cd->ijc", grad_gate, gate_weight, preferred_element_type=jnp.float32
    )
    grad_pair = norm_back(grad_scaled * in_gain, normed_in, inverse_in, 2).astype(jnp.bfloat16)
    return (output, grad_pair)


def solution(mesh):
    blocks = mesh.shape["row"] == 16 and mesh.shape["col"] == 1
    placed = (
        P(("grp", "row"), "col", None),
        P(("grp", "row"), "col"),
        P(("grp", "row"), "col", None),
        P(),
        P(),
        P(),
        P(),
        P(),
        P(),
        P(),
    )
    return jax.shard_map(
        blocks_device if blocks else channels_device,
        mesh=mesh,
        in_specs=placed,
        out_specs=(P(("grp", "row"), "col", None), P(("grp", "row"), "col", None)),
        check_vma=False,
    )
```
